32 devices in a mesh: dp: 8 (over z, y), fsdp: 4 (over x, core).
Axes of the slice: x: 2, y: 2, z: 4, core: 2. Of those that a mesh axis runs over, the one named last changes fastest.
Arguments:
- images: bfloat16 [128, 197, 768], P(('dp', 'fsdp')), may hold values from -6 to 6
- first_gain: bfloat16 [768], P('fsdp'), may hold values from 0.099609375 to 1.8984375
- first_shift: bfloat16 [768], P('fsdp'), may hold values from -3 to 3
- joint_weight: bfloat16 [768, 2304], P('fsdp'), may hold values from -0.21875 to 0.21875
- out_weight: bfloat16 [768, 768], P('fsdp'), may hold values from -1.75 to 1.75
- second_gain: bfloat16 [768], P('fsdp'), may hold values from 0.099609375 to 1.8984375
- second_shift: bfloat16 [768], P('fsdp'), may hold values from -3 to 3
- up_weight: bfloat16 [768, 3072], P('fsdp'), may hold values from -0.21875 to 0.21875
- down_weight: bfloat16 [3072, 768], P('fsdp'), may hold values from -0.109375 to 0.109375
- keep_flags: int32 [128, 197], P(('dp', 'fsdp')), may hold values from 0 to 1, as said below
- cotangent: bfloat16 [128, 197, 768], P(('dp', 'fsdp')), may hold values from -6 to 6
Outputs:
- output: bfloat16 [128, 197, 768], P(('dp', 'fsdp'))
- grad_images: float32 [128, 197, 768], P(('dp', 'fsdp'))
- grad_first_gain: float32 [768], P('fsdp')
- grad_first_shift: float32 [768], P('fsdp')
- grad_joint: float32 [768, 2304], P('fsdp')
- grad_out: float32 [768, 768], P('fsdp')
- grad_second_gain: float32 [768], P('fsdp')
- grad_second_shift: float32 [768], P('fsdp')
- grad_up: float32 [768, 3072], P('fsdp')
- grad_down: float32 [3072, 768], P('fsdp')
The draws below stay inside these ranges and needn't reach their ends.
Inputs may be any that keep to these rules, and one draw needn't show every extreme that they name: `keep_flags`: position 0 (the class token) of every image is 1; the share of tissue patches differs from image to image.
All inputs are finite; a program needn't handle non-finite values.
Results may differ from the reference program's by a relative error of at most 0.015.
Values may be sent and summed in bfloat16 or wider, within the bound.
No kernel may reach another device: no remote copies, remote signals or barrier semaphores. Data moves between devices by JAX's collectives and lax.ppermute only.
A program may use at most 192 MiB of HBM per device.

```python
import math
import jax
import jax.numpy as jnp
from jax import lax

D = 768
H = 12
FF = 3072
SEQ = 197
IMAGES = 128


def draw_keep_flags(key, part):
    key = jax.random.fold_in(key, 7)
    level_key, roll_key = jax.random.split(key)
    level = jax.random.randint(level_key, (IMAGES, 1), 200, 1001)
    roll = jax.random.randint(roll_key, (IMAGES, SEQ), 0, 1000)
    flags = (roll < level).astype(jnp.int32)
    return flags.at[:, 0].set(1)


def shard_levels(key, shape, cuts, low, top_value):
    factor_of, own = 1.0, jax.random.fold_in(key, 6)
    for position, shards_of in cuts:
        heights = jnp.exp(jax.random.uniform(jax.random.fold_in(own, position), (shards_of,), jnp.float32, low / len(cuts), top_value / len(cuts)))
        factor_of = factor_of * jnp.repeat(heights, shape[position] // shards_of).reshape([-1 if axis == position else 1 for axis in range(len(shape))])
    return factor_of


def normal_values(own_key, shape, deviation, reach, cuts=(), dtype=jnp.bfloat16):
    array = jax.random.normal(own_key, shape, jnp.float32) * deviation
    if len(cuts) > 0:
        array = shard_levels(own_key, shape, cuts, -0.22, 0.18) * array
    return jnp.clip(array, min=-reach, max=reach).astype(dtype)


def setup_inputs(seed: int = 0) -> dict:
    streams_of = jax.random.split(jax.random.key(seed), 12)
    return {
        "images": normal_values(streams_of[0], (IMAGES, SEQ, D), 1.0, 6.0, ((0, 32),)),
        "first_gain": jnp.clip(1.0 + 0.18 * jax.random.normal(streams_of[1], (D,), jnp.float32), 0.099609375, 1.8984375).astype(jnp.bfloat16),
        "first_shift": normal_values(streams_of[2], (D,), 0.3, 3.0, ((0, 4),)),
        "joint_weight": normal_values(streams_of[3], (D, 3 * D), D ** -0.5, 0.21875, ((0, 4),)),
        "out_weight": normal_values(streams_of[4], (D, D), (max(D // 64, 1)) ** -0.5, 1.75, ((0, 4),)),
        "second_gain": jnp.clip(1.0 + 0.18 * jax.random.normal(streams_of[5], (D,), jnp.float32), 0.099609375, 1.8984375).astype(jnp.bfloat16),
        "second_shift": normal_values(streams_of[6], (D,), 0.3, 3.0, ((0, 4),)),
        "up_weight": normal_values(streams_of[7], (D, FF), D ** -0.5, 0.21875, ((0, 4),)),
        "down_weight": normal_values(streams_of[8], (FF, D), FF ** -0.5, 0.109375, ((0, 4),)),
        "keep_flags": draw_keep_flags(jax.random.fold_in(streams_of[11], 71), 0),
        "cotangent": normal_values(streams_of[10], (IMAGES, SEQ, D), 1.0, 6.0, ((0, 32),)),
    }


@jax.custom_vjp
def low(v):
    return lax.optimization_barrier(v.astype(jnp.bfloat16)).astype(jnp.float32)

@jax.custom_vjp
def low_back(v):
    return v

def low_keep(v):
    return (low(v), None)

def low_pass(kept, grad):
    return (grad,)

def back_keep(v):
    return (v, None)

def back_low(kept, grad):
    return (low(grad),)
low.defvjp(low_keep, low_pass)
low_back.defvjp(back_keep, back_low)
norm_eps = 1e-06
masked_score = -1e+30

def layer_norm(value, gain, shift):
    center = value - lax.optimization_barrier(jnp.mean(value, axis=-1, keepdims=True))
    spread = lax.optimization_barrier(jnp.mean(center * center, axis=-1, keepdims=True))
    return center * lax.rsqrt(spread + norm_eps) * gain + shift

def block(value, first_gain, first_shift, joint_weight, out_weight, second_gain, second_shift, up_weight, down_weight, keep_flags):
    highest = lax.Precision.HIGHEST
    count, length, width = value.shape
    heads = H
    size = width // heads
    normed = low(layer_norm(value, first_gain, first_shift))
    joint = low(low_back(jnp.einsum('bsd,de->bse', normed, joint_weight, precision=highest)))
    query = joint[..., :width].reshape(count, length, heads, size)
    keys = joint[..., width:2 * width].reshape(count, length, heads, size)
    values = joint[..., 2 * width:].reshape(count, length, heads, size)
    scores = low_back(jnp.einsum('bqhd,bkhd->bhqk', query, keys, precision=highest) * size ** (-0.5))
    scores = jnp.where(keep_flags[:, None, None, :] > 0, scores, masked_score)
    probs = low(jax.nn.softmax(scores, axis=-1))
    context = jnp.einsum('bhqk,bkhd->bqhd', probs, values, precision=highest).reshape(count, length, width)
    context = low(low_back(context))
    branch = low_back(jnp.einsum('bsd,de->bse', context, out_weight, precision=highest))
    middle = value + branch
    normed_two = low(layer_norm(middle, second_gain, second_shift))
    upper = low_back(jnp.einsum('bsd,df->bsf', normed_two, up_weight, precision=highest))
    active = low(jax.nn.gelu(upper, approximate=False))
    second = low_back(jnp.einsum('bsf,fd->bsd', active, down_weight, precision=highest))
    return middle + second

def reference(images, first_gain, first_shift, joint_weight, out_weight, second_gain, second_shift, up_weight, down_weight, keep_flags, cotangent):
    params = tuple((p.astype(jnp.float32) for p in (first_gain, first_shift, joint_weight, out_weight, second_gain, second_shift, up_weight, down_weight)))
    group = math.gcd(IMAGES, 16)
    steps = IMAGES // group
    inputs = images.astype(jnp.float32).reshape(steps, group, SEQ, D)
    flags = keep_flags.reshape(steps, group, SEQ)
    pulls = cotangent.astype(jnp.float32).reshape(steps, group, SEQ, D)

    def step(carry, items):
        value, flag, pull_in = items

        def forward(v, *ps):
            return block(v, *ps, flag)
        result, puller = jax.vjp(forward, value, *params)
        grads = puller(pull_in)
        carry = tuple((c + g for c, g in zip(carry, grads[1:])))
        return (carry, (result.astype(jnp.bfloat16), grads[0]))
    start = tuple((jnp.zeros(p.shape, jnp.float32) for p in params))
    totals, (outputs, grad_input) = lax.scan(step, start, (inputs, flags, pulls))
    output = outputs.reshape(IMAGES, SEQ, D)
    grad_images = grad_input.reshape(IMAGES, SEQ, D)
    return (output, grad_images, totals[0], totals[1], totals[2], totals[3], totals[4], totals[5], totals[6], totals[7])
```

```python
import jax
import jax.numpy as jnp
from jax import lax
from jax.experimental import pallas as pl
from jax.experimental.pallas import tpu as pltpu
from jax.sharding import PartitionSpec as P

HEADS = 12
EPS = 1e-06
MASKED = -1e30
F32 = jnp.float32
BF16 = jnp.bfloat16
VM = pltpu.VMEM
ANY = pl.ANY
LIMIT = 56 * 1024 * 1024


def vmem():
    return pl.BlockSpec(memory_space=VM)


def anywhere():
    return pl.BlockSpec(memory_space=ANY)


def up_to(value, step):
    return (value + step - 1) // step * step


def dot(a, b):
    return jnp.dot(a, b, preferred_element_type=F32)


def dot_bt(a, b):
    return lax.dot_general(a, b, (((1,), (1,)), ((), ())), preferred_element_type=F32)


def dot_at(a, b):
    return lax.dot_general(a, b, (((0,), (0,)), ((), ())), preferred_element_type=F32)


def place():
    me = lax.axis_index("fsdp")
    dp = lax.axis_index("dp")
    return me, dp & 1, (dp >> 1) & 1


def cost(flops, moved):
    return pl.CostEstimate(flops=flops, bytes_accessed=moved, transcendentals=0)


def start_pieces(pieces, dest, sems, base, me, y):
    rows = pieces[0].shape[0]
    half = rows // 2
    starts = (
        me * rows,
        (me ^ 1) * rows,
        (me ^ 2) * rows + y * half,
        (me ^ 2) * rows + (1 - y) * half,
        (me ^ 3) * rows + y * half,
        (me ^ 3) * rows + (1 - y) * half,
    )
    copies = []
    for index, (piece, start) in enumerate(zip(pieces, starts)):
        where = pl.ds(pl.multiple_of(start, half), piece.shape[0])
        copy = pltpu.make_async_copy(piece, dest.at[where], sems.at[base + index])
        copy.start()
        copies.append(copy)
    return copies


def standardize(value):
    mean = jnp.mean(value, axis=-1, keepdims=True)
    center = value - mean
    spread = jnp.mean(center * center, axis=-1, keepdims=True)
    factor = lax.rsqrt(spread + EPS)
    return center * factor, factor


def norm_back(upstream, normal, factor):
    first = jnp.mean(upstream, axis=-1, keepdims=True)
    second = jnp.mean(upstream * normal, axis=-1, keepdims=True)
    return factor * (upstream - first - normal * second)


def owner_rows(turned, dest, me, y, z):
    width = turned.shape[0]
    piece = width // 16
    for block in range(16):
        owner, yb, zb = block // 4, (block // 2) % 2, block % 2
        rel = owner ^ me
        at = (rel & 1) * 8 + (rel >> 1) * 4 + (yb ^ y) * 2 + (zb ^ z)
        where = pl.ds(pl.multiple_of(at * piece, piece), piece)
        dest[where, :] = turned[block * piece : (block + 1) * piece, :]


def quarter_rows(turned, dest, y, z):
    piece = turned.shape[0] // 4
    for block in range(4):
        yb, zb = block // 2, block % 2
        at = (yb ^ y) * 2 + (zb ^ z)
        where = pl.ds(pl.multiple_of(at * piece, piece), piece)
        dest[where, :] = turned[block * piece : (block + 1) * piece, :]


def turn_kernel(g_ref, out_ref):
    me, y, z = place()
    quarter_rows(g_ref[...].T, out_ref, y, z)


def qkv_kernel(x_ref, vec_ref, *refs):
    pieces, (hn_ref, joint_ref, w_s, sems) = refs[:6], refs[6:]
    me, y, z = place()
    copies = start_pieces(pieces, w_s, sems, 0, me, y)
    tokens = x_ref.shape[0]
    gain, shift = vec_ref[0:1, :], vec_ref[1:2, :]

    @pl.loop(0, tokens // 208)
    def _(i):
        rows = pl.ds(pl.multiple_of(i * 208, 16), 208)
        normal, factor = standardize(x_ref[rows, :].astype(F32))
        hn_ref[rows, :] = (normal * gain + shift).astype(BF16)

    extra = joint_ref.shape[0] - tokens
    joint_ref[tokens:, :] = jnp.zeros((extra, joint_ref.shape[1]), BF16)
    for copy in copies:
        copy.wait()
    width = x_ref.shape[1]
    steps = joint_ref.shape[1] // 256

    @pl.loop(0, steps)
    def _(n):
        cols = pl.ds(pl.multiple_of(n * 256, 256), 256)
        scale = jnp.where(n < width // 256, 0.125, 1.0).astype(F32)
        value = dot(hn_ref[...], w_s[:, cols])
        joint_ref[0:tokens, cols] = (value.astype(BF16) * scale.astype(BF16))


def head_masks(width, size):
    lane = lax.broadcasted_iota(jnp.int32, (1, width), 1) // size
    return [(lane == h) for h in range(width // size)]


def attn_kernel(joint_ref, mask_ref, p_ref, ctx_ref):
    tokens, seq, window = ctx_ref.shape[0] * 4, ctx_ref.shape[0], mask_ref.shape[2]
    width = ctx_ref.shape[1]
    base = pl.multiple_of(pl.program_id(0) * seq, 16)
    rows, keys = pl.ds(base, seq), pl.ds(base, window)
    live = mask_ref[0]
    masks = head_masks(256, width // HEADS)
    for quad in range(width // 256):
        at = quad * 256
        q = joint_ref[rows, at : at + 256]
        k = joint_ref[keys, width + at : width + at + 256]
        v = joint_ref[keys, 2 * width + at : 2 * width + at + 256]
        total = None
        for h in range(4):
            s = dot_bt(q * masks[h].astype(BF16), k)
            s = jnp.where(live > 0.5, s, MASKED)
            top = jnp.max(s, axis=-1, keepdims=True)
            e = jnp.exp(s - top)
            p = (e * (1.0 / jnp.sum(e, axis=-1, keepdims=True))).astype(BF16)
            p_ref[0, quad * 4 + h] = p
            c = dot(p, v)
            total = jnp.where(masks[h], c, 0.0 if total is None else total)
        ctx_ref[:, at : at + 256] = total.astype(BF16)


def branch_kernel(ctx_ref, x_ref, vec_ref, *refs):
    pieces, (x1_ref, hn_ref, turned_ref, w_s, sems) = refs[:6], refs[6:]
    me, y, z = place()
    for copy in start_pieces(pieces, w_s, sems, 0, me, y):
        copy.wait()
    gain, shift = vec_ref[2:3, :], vec_ref[3:4, :]

    @pl.loop(0, ctx_ref.shape[0] // 208)
    def _(i):
        rows = pl.ds(pl.multiple_of(i * 208, 16), 208)
        middle = x_ref[rows, :].astype(F32) + dot(ctx_ref[rows, :], w_s[...])
        x1_ref[rows, :] = middle
        normal, factor = standardize(middle)
        hn_ref[rows, :] = (normal * gain + shift).astype(BF16)

    owner_rows(hn_ref[...].T, turned_ref, me, y, z)


def gelu_both(u):
    t = 1.0 / (1.0 + 0.23164190 * jnp.abs(u))
    poly = 0.5 * 1.061405429 * t + 0.5 * -1.453152027
    poly = poly * t + 0.5 * 1.421413741
    poly = poly * t + 0.5 * -0.284496736
    poly = poly * t + 0.5 * 0.254829592
    e = jnp.exp(-0.5 * (u * u))
    tail = poly * t * e
    phi = jnp.where(u >= 0.0, 1.0 - tail, tail)
    return u * phi, phi + u * (e * 0.3989422804014327)


def mlp_kernel(first, hn_ref, g_ref, gt_ref, ht_ref, *refs):
    ups, refs = refs[:6], refs[6:]
    downs, refs = refs[:6], refs[6:]
    if not first:
        (out_in, dh_in), refs = refs[:2], refs[2:]
    keep_ref, send_ref, out_ref, dh_ref, wu_s, wd_s, sems = refs
    me, y, z = place()
    copies = start_pieces(ups, wu_s, sems, 0, me, y)
    rows = downs[0].shape[0]
    half = rows // 2
    for index, (piece, start) in enumerate(
        zip(
            downs,
            (0, 2 * rows, rows + y * half, rows + (1 - y) * half, 3 * rows + y * half, 3 * rows + (1 - y) * half),
        )
    ):
        where = pl.ds(pl.multiple_of(start, half), piece.shape[0])
        copy = pltpu.make_async_copy(piece, wd_s.at[where], sems.at[6 + index])
        copy.start()
        copies.append(copy)
    for copy in copies:
        copy.wait()
    width = hn_ref.shape[1]
    quarter = width // 4
    eighth = width // 16
    for c in range(2):
        acts, pulls, cols = [], [], []
        for x in range(2):
            owner = me ^ (c + 2 * x)
            col = pl.ds(pl.multiple_of(owner * rows, rows), rows)
            act, slope = gelu_both(dot(hn_ref[...], wu_s[:, col]))
            act = act.astype(BF16)
            at = (2 * c + x) * rows
            pull = (dot_bt(g_ref[...], wd_s[at : at + rows, :]) * slope).astype(BF16)
            acts.append(act)
            pulls.append(pull)
            cols.append(col)
            gd = dot(gt_ref[...], act).astype(BF16)
            dest = send_ref if c else keep_ref
            for part in range(4):
                dest[x, part, 0:quarter, :] = gd[part * quarter : (part + 1) * quarter, :]
            gu = dot(ht_ref[...], pull).astype(BF16)
            where = pl.ds(pl.multiple_of(quarter + owner * eighth, eighth), eighth)
            for block in range(16):
                dest = send_ref if block // 8 else keep_ref
                dest[(block // 4) % 2, block % 4, where, :] = gu[block * eighth : (block + 1) * eighth, :]
        act, pull = jnp.concatenate(acts, axis=1), jnp.concatenate(pulls, axis=1)
        plus = dot(act, wd_s[2 * c * rows : 2 * (c + 1) * rows, :])
        wu = jnp.concatenate([wu_s[:, col] for col in cols], axis=1)
        back = dot_bt(pull, wu)
        if c == 0 and first:
            out_ref[...] = plus
            dh_ref[...] = back
        elif c == 0:
            out_ref[...] = out_in[...] + plus
            dh_ref[...] = dh_in[...] + back
        else:
            out_ref[...] += plus
            dh_ref[...] += back


def middle_kernel(x1_ref, out_in, dh_in, g_ref, vec_ref, ctx_ref, hn_ref, *refs):
    pieces, refs = refs[:6], refs[6:]
    result_ref, dx_ref, dctx_ref, keep_ref, send_ref, dvec_ref, ht_ref, w_s, dy_s, ct_s, sems = refs
    me, y, z = place()
    copies = start_pieces(pieces, w_s, sems, 0, me, y)
    gain = vec_ref[2:3, :]
    tokens, width = ctx_ref.shape
    dvec_ref[...] = jnp.zeros_like(dvec_ref)

    @pl.loop(0, tokens // 208)
    def _(i):
        rows = pl.ds(pl.multiple_of(i * 208, 16), 208)
        middle = x1_ref[rows, :]
        result_ref[rows, :] = (middle + out_in[rows, :]).astype(BF16)
        normal, factor = standardize(middle)
        pull = dh_in[rows, :]
        dvec_ref[0:1, :] += jnp.sum(pull * normal, axis=0, keepdims=True)
        dvec_ref[1:2, :] += jnp.sum(pull, axis=0, keepdims=True)
        dx = g_ref[rows, :].astype(F32) + norm_back(pull * gain, normal, factor)
        dx_ref[rows, :] = dx
        dy_s[rows, :] = dx.astype(BF16)

    owner_rows(ctx_ref[...].T, ct_s, me, y, z)
    owner_rows(hn_ref[...].T, ht_ref, me, y, z)
    for copy in copies:
        copy.wait()
    dctx_ref[...] = dot_bt(dy_s[...], w_s[...]).astype(BF16)
    eighth = width // 16
    for part in range(2):
        go = dot(ct_s[...], dy_s[:, part * 384 : part * 384 + 384]).astype(BF16)
        for block in range(16):
            dest = send_ref if block // 8 else keep_ref
            dest[(block // 4) % 2, block % 4, :, part * 384 : part * 384 + 384] = go[
                block * eighth : (block + 1) * eighth, :
            ]


def back_kernel(first, joint_q, joint_k, joint_v, p_ref, dctx_ref, ht_ref, *refs):
    pieces, refs = refs[:6], refs[6:]
    if not first:
        dh_in, refs = refs[0], refs[1:]
    keep_ref, send_ref, dh_ref, w_s, dj_s, sems = refs
    me, y, z = place()
    quad = p_ref.shape[1] // 4
    copies = start_pieces(pieces, w_s, sems, 0, me, y)
    images, heads, seq, window = p_ref.shape
    masks = head_masks(256, 64)

    @pl.loop(0, images)
    def _(b):
        base = pl.multiple_of(b * seq, 16)
        rows, keys = pl.ds(base, seq), pl.ds(base, window)
        q, k, v = joint_q[rows, :], joint_k[keys, :], joint_v[keys, :]
        d = dctx_ref[rows, :]
        dq, dk, dv = None, None, None
        for h in range(4):
            mask = masks[h].astype(BF16)
            dm = d * mask
            p = p_ref[b, h]
            dp = dot_bt(dm, v)
            pf = p.astype(F32)
            prod = pf * dp
            ds = (prod - pf * jnp.sum(prod, axis=-1, keepdims=True)).astype(BF16)
            q_part = dot(ds, k)
            dq = jnp.where(masks[h], q_part, 0.0 if dq is None else dq)
            k_part, v_part = dot_at(ds, q * mask), dot_at(p, dm)
            dk = k_part if dk is None else dk + k_part
            dv = v_part if dv is None else dv + v_part
        dj_s[rows, 0:256] = (dq * 0.125).astype(BF16)
        dj_s[rows, 256:512] = dk[0:seq, :].astype(BF16)
        dj_s[rows, 512:768] = dv[0:seq, :].astype(BF16)

    width = ht_ref.shape[0]
    eighth = width // 16
    for part in range(3):
        gj = dot(ht_ref[...], dj_s[:, part * 256 : part * 256 + 256]).astype(BF16)
        for block in range(16):
            dest = send_ref if block // 8 else keep_ref
            dest[(block // 4) % 2, block % 4, :, part * 256 : part * 256 + 256] = gj[
                block * eighth : (block + 1) * eighth, :
            ]
    for copy in copies:
        copy.wait()
    plus = dot_bt(dj_s[...], w_s[...])
    dh_ref[...] = plus if first else dh_in[...] + plus


def last_kernel(dh_ref, x_ref, dx_ref, vec_ref, out_ref, dvec_ref):
    gain = vec_ref[0:1, :]
    dvec_ref[...] = jnp.zeros_like(dvec_ref)

    @pl.loop(0, x_ref.shape[0] // 208)
    def _(i):
        rows = pl.ds(pl.multiple_of(i * 208, 16), 208)
        normal, factor = standardize(x_ref[rows, :].astype(F32))
        pull = dh_ref[rows, :]
        dvec_ref[0:1, :] += jnp.sum(pull * normal, axis=0, keepdims=True)
        dvec_ref[1:2, :] += jnp.sum(pull, axis=0, keepdims=True)
        out_ref[rows, :] = dx_ref[rows, :] + norm_back(pull * gain, normal, factor)


def mlp_end_kernel(*refs):
    parts, (up_ref, down_ref, turn_s) = refs[:12], refs[12:]
    me, y, z = place()
    rows = parts[0].shape[0]
    half = rows // 2
    eighth = half // 4
    lanes = parts[0].shape[1]
    for chunk in range(3):
        for rel in range(4):
            piece = parts[chunk * 4 + rel]
            at = ((rel // 2) ^ y) * 2 + ((rel % 2) ^ z)
            where = pl.ds(pl.multiple_of(at * half, half), half)
            turn_s[where, :] = piece[0:half, :].astype(F32)
            where = pl.ds(pl.multiple_of(at * eighth, eighth), eighth)
            for owner in range(4):
                col = (owner * 3 + chunk) * lanes
                up_ref[where, col : col + lanes] = piece[half + owner * eighth : half + (owner + 1) * eighth, :].astype(F32)
        down_ref[chunk * lanes : (chunk + 1) * lanes, :] = turn_s[...].T


def rows_end_kernel(*refs):
    out_ref = refs[-1]
    me, y, z = place()
    piece = refs[0].shape[0]
    chunks = (len(refs) - 1) // 4
    width = refs[0].shape[1]
    for chunk in range(chunks):
        for rel in range(4):
            value = refs[chunk * 4 + rel][...].astype(F32)
            at = ((rel // 2) ^ y) * 2 + ((rel % 2) ^ z)
            where = pl.ds(pl.multiple_of(at * piece, piece), piece)
            if chunks == 1:
                out_ref[where, :] = value
            else:
                third = width // 3
                for kind in range(3):
                    col = kind * width + chunk * third
                    out_ref[where, col : col + third] = value[:, kind * third : (kind + 1) * third]


def on_device(
    images,
    first_gain,
    first_shift,
    joint_weight,
    out_weight,
    second_gain,
    second_shift,
    up_weight,
    down_weight,
    keep_flags,
    cotangent,
):
    count, length, width = images.shape
    n_dp = lax.axis_size("dp")
    n_fs = lax.axis_size("fsdp")
    me = lax.axis_index("fsdp")
    dp = lax.axis_index("dp")
    y = dp & 1
    seq = up_to(length, 16)
    window = up_to(seq, 256)
    tokens = count * seq
    ff = up_weight.shape[1]
    params = pltpu.CompilerParams(vmem_limit_bytes=LIMIT)

    def swap(axis, bit):
        n = n_dp if axis == "dp" else n_fs
        return lambda v: lax.ppermute(v, axis, [(i, i ^ bit) for i in range(n)])

    core, over_x, over_y, over_z = swap("fsdp", 1), swap("fsdp", 2), swap("dp", 1), swap("dp", 2)

    def call(body, outs, args, scratch=(), flops=0, spaces=None, **more):
        moved = sum(a.size * a.dtype.itemsize for a in args) + sum(o.size * o.dtype.itemsize for o in outs)
        return pl.pallas_call(
            body,
            out_shape=outs,
            in_specs=spaces or [vmem()] * len(args),
            out_specs=[vmem()] * len(outs),
            scratch_shapes=list(scratch),
            compiler_params=params,
            cost_estimate=cost(flops, moved),
            **more,
        )(*args)

    def shape(*dims, dtype=BF16):
        return jax.ShapeDtypeStruct(dims, dtype)

    def gather(own, after=None):
        half = own.shape[0] // 2
        mine = lax.dynamic_slice_in_dim(own, y * half, half, 0)
        if after is not None:
            mine, after = lax.optimization_barrier((mine, after))
        near = core(own)
        xh = over_x(mine)
        yh = over_y(xh)
        return (own, near, xh, yh, core(xh), core(yh)), xh

    fourth = ff // n_fs
    third = fourth // 3
    vec = jnp.stack([first_gain, first_shift, second_gain, second_shift]).astype(BF16)
    other = over_x(vec)
    both = jnp.stack([vec, core(vec), other, core(other)])
    vecs = jnp.concatenate([lax.dynamic_index_in_dim(both, me ^ i, 0, False) for i in range(n_fs)], axis=1)
    vecs = jnp.pad(vecs.astype(F32), ((0, 4), (0, 0)))

    w_joint, last = gather(joint_weight)
    w_out, last = gather(out_weight, last)
    w_ups, w_downs = [], []
    for chunk in range(3):
        cut = up_weight.reshape(-1, n_fs, 3, third)[:, :, chunk, :].reshape(-1, n_fs * third)
        pieces, last = gather(cut, last)
        w_ups.append(pieces)
        pieces, last = gather(down_weight[chunk * third : (chunk + 1) * third], last)
        w_downs.append(pieces)

    pads = ((0, 0), (0, seq - length), (0, 0))
    x = jnp.pad(images, pads).reshape(tokens, width)
    g = jnp.pad(cotangent, pads).reshape(tokens, width)
    live = jnp.pad(keep_flags, ((0, 0), (0, window - length))).astype(F32).reshape(count, 1, window)

    (gt,) = call(turn_kernel, [shape(width, tokens)], [g])

    piece_spaces = [anywhere()] * 6
    long = tokens + window - seq
    hn1, joint = call(
        qkv_kernel,
        [shape(tokens, width), shape(long, 3 * width)],
        [x, vecs, *w_joint],
        [pltpu.VMEM((width, 3 * width), BF16), pltpu.SemaphoreType.DMA((6,))],
        flops=2 * tokens * width * 3 * width,
        spaces=[vmem()] * 2 + piece_spaces,
    )
    probs, ctx = pl.pallas_call(
        attn_kernel,
        grid=(count,),
        out_shape=[shape(count, HEADS, seq, window), shape(tokens, width)],
        in_specs=[
            pl.BlockSpec((long, 3 * width), lambda i: (0, 0)),
            pl.BlockSpec((1, 1, window), lambda i: (i, 0, 0)),
        ],
        out_specs=[
            pl.BlockSpec((1, HEADS, seq, window), lambda i: (i, 0, 0, 0)),
            pl.BlockSpec((seq, width), lambda i: (i, 0)),
        ],
        compiler_params=params,
        cost_estimate=cost(8 * count * HEADS * seq * window * 256, 10 * 2**20),
    )(joint, live)
    x1, hn2, h2t = call(
        branch_kernel,
        [shape(tokens, width, dtype=F32), shape(tokens, width), shape(width, tokens)],
        [ctx, x, vecs, *w_out],
        [pltpu.VMEM((width, width), BF16), pltpu.SemaphoreType.DMA((6,))],
        flops=2 * tokens * width * width,
        spaces=[vmem()] * 3 + piece_spaces,
    )

    def plus(*terms):
        total = terms[0].astype(F32)
        for term in terms[1:]:
            total = total + term.astype(F32)
        return total.astype(BF16)

    def reduce(keep, send):
        rc = core(send)
        rx = over_x(plus(keep[1], rc[1]))
        ry = over_y(plus(keep[0, 2:4], rc[0, 2:4], rx[2:4]))
        rz = over_z(plus(keep[0, 1], rc[0, 1], rx[1], ry[1]))
        total = plus(keep[0, 0], rc[0, 0], rx[0], ry[0], rz)
        bit = 4
        while bit < n_dp:
            total = lax.optimization_barrier(total)
            total = plus(total, swap("dp", bit)(total))
            bit *= 2
        total = lax.optimization_barrier(total)
        side = over_z(total)
        return total, side, over_y(total), over_y(side)

    out_sum, dh = None, None
    mlp_parts = []
    for chunk in range(3):
        first = chunk == 0
        carried = [] if first else [out_sum, dh]
        keep, send, out_sum, dh = call(
            lambda *refs, first=first: mlp_kernel(first, *refs),
            [shape(2, 4, width // 2, third)] * 2 + [shape(tokens, width, dtype=F32)] * 2,
            [hn2, g, gt, h2t, *w_ups[chunk], *w_downs[chunk], *carried],
            [
                pltpu.VMEM((width, n_fs * third), BF16),
                pltpu.VMEM((n_fs * third, width), BF16),
                pltpu.SemaphoreType.DMA((12,)),
            ],
            flops=12 * tokens * width * n_fs * third,
            spaces=[vmem()] * 4 + piece_spaces * 2 + [vmem()] * len(carried),
        )
        mlp_parts += reduce(keep, send)

    eighth = width // 16
    result, dx1, dctx, keep, send, dvec2, h1t = call(
        middle_kernel,
        [
            shape(tokens, width),
            shape(tokens, width, dtype=F32),
            shape(tokens, width),
            shape(2, 4, eighth, width),
            shape(2, 4, eighth, width),
            shape(8, width, dtype=F32),
            shape(width, tokens),
        ],
        [x1, out_sum, dh, g, vecs, ctx, hn1, *w_out],
        [
            pltpu.VMEM((width, width), BF16),
            pltpu.VMEM((tokens, width), BF16),
            pltpu.VMEM((width, tokens), BF16),
            pltpu.SemaphoreType.DMA((6,)),
        ],
        flops=4 * tokens * width * width,
        spaces=[vmem()] * 7 + piece_spaces,
    )
    out_parts = reduce(keep, send)

    joint_parts = []
    dh1 = None
    for quad in range(width // 256):
        first = quad == 0
        carried = [] if first else [dh1]

        def column(kind, quad=quad):
            return pl.BlockSpec((long, 256), lambda i, c=kind * (width // 256) + quad: (0, c))

        keep, send, dh1 = pl.pallas_call(
            lambda *refs, first=first: back_kernel(first, *refs),
            grid=(1,),
            out_shape=[shape(2, 4, eighth, width)] * 2 + [shape(tokens, width, dtype=F32)],
            in_specs=[
                column(0),
                column(1),
                column(2),
                pl.BlockSpec((count, 4, seq, window), lambda i, quad=quad: (0, quad, 0, 0)),
                pl.BlockSpec((tokens, 256), lambda i, quad=quad: (0, quad)),
                pl.BlockSpec((width, tokens), lambda i: (0, 0)),
                *piece_spaces,
                *[vmem()] * len(carried),
            ],
            out_specs=[vmem()] * 3,
            scratch_shapes=[
                pltpu.VMEM((width, width), BF16),
                pltpu.VMEM((tokens, width), BF16),
                pltpu.SemaphoreType.DMA((6,)),
            ],
            compiler_params=params,
            cost_estimate=cost(4 * tokens * width * width + 10 * count * 4 * seq * window * 256, 12 * 2**20),
        )(joint, joint, joint, probs, dctx, h1t, *[cut_joint(p, quad, width) for p in w_joint], *carried)
        joint_parts += reduce(keep, send)

    grad_x, dvec1 = call(
        last_kernel,
        [shape(tokens, width, dtype=F32), shape(8, width, dtype=F32)],
        [dh1, x, dx1, vecs],
    )
    small = jnp.concatenate([dvec1[0:2], dvec2[0:2]], axis=0)
    for hop in (core, over_x):
        small = small + hop(small)
        small = lax.optimization_barrier(small)
    bit = 1
    while bit < n_dp:
        small = lax.optimization_barrier(small + swap("dp", bit)(small))
        bit *= 2
    mine = lax.dynamic_slice_in_dim(small, me * (width // n_fs), width // n_fs, 1)

    grad_up, grad_down = call(
        mlp_end_kernel,
        [shape(width // n_fs, ff, dtype=F32), shape(fourth, width, dtype=F32)],
        mlp_parts,
        [pltpu.VMEM((width, third), F32)],
    )
    (grad_out,) = call(rows_end_kernel, [shape(width // n_fs, width, dtype=F32)], out_parts)
    (grad_joint,) = call(rows_end_kernel, [shape(width // n_fs, 3 * width, dtype=F32)], joint_parts)
    output = result.reshape(count, seq, width)[:, :length]
    grad_images = grad_x.reshape(count, seq, width)[:, :length]
    return (
        output,
        grad_images,
        mine[0],
        mine[1],
        grad_joint,
        grad_out,
        mine[2],
        mine[3],
        grad_up,
        grad_down,
    )


def cut_joint(piece, quad, width):
    return jnp.concatenate(
        [piece[:, kind * width + quad * 256 : kind * width + quad * 256 + 256] for kind in range(3)], axis=1
    )


def solution(mesh):
    rows = P("fsdp", None)
    tokens = P(("dp", "fsdp"), None, None)
    one = P("fsdp")
    return jax.shard_map(
        on_device,
        mesh=mesh,
        in_specs=(tokens, one, one, rows, rows, one, one, rows, rows, P(("dp", "fsdp"), None), tokens),
        out_specs=(tokens, tokens, one, one, rows, rows, one, one, rows, rows),
        check_vma=False,
    )
```

```python
import jax
import jax.numpy as jnp
from jax import lax
from jax.experimental import pallas as pl
from jax.experimental.pallas import tpu as pltpu
from jax.sharding import PartitionSpec as P

HEADS = 12
EPS = 1e-06
MASKED = -1e30
F32 = jnp.float32
BF16 = jnp.bfloat16
VM = pltpu.VMEM
ANY = pl.ANY
LIMIT = 12 * 1024 * 1024
FLOPS = 10**9


def vmem():
    return pl.BlockSpec(memory_space=VM)


def anywhere():
    return pl.BlockSpec(memory_space=ANY)


def in_hbm():
    return pl.BlockSpec(memory_space=pltpu.HBM)


def up_to(value, step):
    return (value + step - 1) // step * step


def dot(a, b):
    return jnp.dot(a, b, preferred_element_type=F32)


def dot_bt(a, b):
    return lax.dot_general(a, b, (((1,), (1,)), ((), ())), preferred_element_type=F32)


def dot_at(a, b):
    return lax.dot_general(a, b, (((0,), (0,)), ((), ())), preferred_element_type=F32)


def place():
    me = lax.axis_index("fsdp")
    dp = lax.axis_index("dp")
    return me, dp & 1, (dp >> 1) & 1


def start(table, sems, base=0):
    copies = []
    for index, (source, first, count, dest, at, col) in enumerate(table):
        src = source if count == source.shape[0] else source.at[pl.ds(pl.multiple_of(first, 16), count)]
        where = pl.ds(pl.multiple_of(at, 16), count)
        into = dest.at[where] if col is None else dest.at[where, col : col + source.shape[1]]
        copy = pltpu.make_async_copy(src, into, sems.at[base + index])
        copy.start()
        copies.append(copy)
    return copies


def cost(flops, moved):
    return pl.CostEstimate(flops=flops, bytes_accessed=moved, transcendentals=0)


def shard_rows(pieces, dest, me, y):
    rows = pieces[0].shape[0]
    half = rows // 2
    starts = (
        me * rows,
        (me ^ 1) * rows,
        (me ^ 2) * rows + y * half,
        (me ^ 2) * rows + (1 - y) * half,
        (me ^ 3) * rows + y * half,
        (me ^ 3) * rows + (1 - y) * half,
    )
    return [(piece, 0, piece.shape[0], dest, at, None) for piece, at in zip(pieces, starts)]


def packed_rows(pieces, dests, me, y, width):
    rows = width // 4
    n_halves = 2 if len(pieces) == 6 else 1
    owners = ((0, (0, 1)), (1, (0, 1)), (2, (y,)), (2, (1 - y,)), (3, (y,)), (3, (1 - y,)))
    if n_halves == 1:
        owners = tuple((rel, (0,)) for rel in range(4))
    tables = ([], [], [])
    for piece, (rel, halves) in zip(pieces, owners):
        size = piece.shape[0] // len(halves)
        for index, half in enumerate(halves):
            first = index * size
            for table, dest, blocks, count, at in (
                (tables[0], dests[0], 4, rows // n_halves, (me ^ rel) * rows),
                (tables[1], dests[1], 3, 256 // n_halves, (0, 2, 1, 3)[rel] * 256),
                (tables[2], dests[2], 3, rows // n_halves, (me ^ rel) * rows),
            ):
                for block in range(blocks):
                    table.append((piece, first, count, dest, at + half * count, block * 256))
                    first = first + count
    return tables


def pack_kernel(up_ref, down_ref, out_ref, whole_ref, half_ref, rest1_ref, rest2_ref, sems):
    me, y, z = place()
    rows, third = up_ref.shape[0], down_ref.shape[0] // 3
    copies = []

    def put(source, first, count, col, dest, at):
        copy = pltpu.make_async_copy(
            source.at[pl.ds(pl.multiple_of(first, 16), count), col : col + third],
            dest.at[pl.ds(at, count)],
            sems.at[len(copies)],
        )
        copy.start()
        copies.append(copy)

    for dest, halves in ((half_ref, (y,)), (whole_ref, (0, 1))):
        at = 0
        for half in halves:
            for source, first, count, cols in (
                (up_ref, 0, rows // 2, [owner * 3 * third for owner in range(4)]),
                (down_ref, 0, third // 2, [block * third for block in range(3)]),
                (out_ref, 0, rows // 2, [block * third for block in range(3)]),
            ):
                for col in cols:
                    put(source, first + half * count, count, col, dest, at)
                    at += count
    for chunk, rest_ref in ((1, rest1_ref), (2, rest2_ref)):
        at = 0
        for owner in range(4):
            put(up_ref, 0, rows, (owner * 3 + chunk) * third, rest_ref, at)
            at += rows
        for block in range(3):
            put(down_ref, chunk * third, third, block * third, rest_ref, at)
            at += third
    for copy in copies:
        copy.wait()


def standardize(value):
    mean = jnp.mean(value, axis=-1, keepdims=True)
    center = value - mean
    spread = jnp.mean(center * center, axis=-1, keepdims=True)
    factor = lax.rsqrt(spread + EPS)
    return center * factor, factor


def norm_back(upstream, normal, factor):
    first = jnp.mean(upstream, axis=-1, keepdims=True)
    second = jnp.mean(upstream * normal, axis=-1, keepdims=True)
    return factor * (upstream - first - normal * second)


def owner_rows(turned, dest, me, y, z):
    piece = turned.shape[0] // 16
    for block in range(16):
        owner, yb, zb = block // 4, (block // 2) % 2, block % 2
        rel = owner ^ me
        at = (rel & 1) * 8 + (rel >> 1) * 4 + (yb ^ y) * 2 + (zb ^ z)
        where = pl.ds(pl.multiple_of(at * piece, piece), piece)
        dest[where, :] = turned[block * piece : (block + 1) * piece, :]


def quarter_rows(turned, dest, y, z):
    piece = turned.shape[0] // 4
    for block in range(4):
        yb, zb = block // 2, block % 2
        at = (yb ^ y) * 2 + (zb ^ z)
        where = pl.ds(pl.multiple_of(at * piece, piece), piece)
        dest[where, :] = turned[block * piece : (block + 1) * piece, :]


def row_loop(tokens, step):
    return pl.loop(0, tokens // step)


def first_norm_kernel(x_ref, vec_ref, hn_ref):
    gain, shift = vec_ref[0:1, :], vec_ref[1:2, :]

    @row_loop(x_ref.shape[0], 208)
    def _(i):
        rows = pl.ds(pl.multiple_of(i * 208, 16), 208)
        normal, factor = standardize(x_ref[rows, :].astype(F32))
        hn_ref[rows, :] = (normal * gain + shift).astype(BF16)


def turn_kernel(hn_ref, g_ref, h1t_ref, gt_ref):
    me, y, z = place()
    owner_rows(hn_ref[...].T, h1t_ref, me, y, z)
    quarter_rows(g_ref[...].T, gt_ref, y, z)


def head_masks():
    lane = lax.broadcasted_iota(jnp.int32, (1, 256), 1) // 64
    return [lane == h for h in range(4)]


def stack(value, masks):
    return jnp.concatenate([value * mask.astype(BF16) for mask in masks], axis=0)


def pick(value, masks):
    seq = value.shape[0] // 4
    total = jnp.where(masks[0], value[0:seq], 0.0)
    for h in range(1, 4):
        total = jnp.where(masks[h], value[h * seq : (h + 1) * seq], total)
    return total


def front_kernel(deps, hn_ref, mask_ref, *refs):
    pieces, (joint_ref, p_ref, ctx_ref, w_s, joint_s, sems, out_sem) = refs[:6], refs[6 + deps :]
    me, y, z = place()
    step = pl.program_id(0)
    tokens, width = hn_ref.shape
    seq, window = ctx_ref.shape[0], mask_ref.shape[2]

    @pl.when(step == 0)
    def _():
        copies = start(shard_rows(pieces, w_s, me, y), sems)
        joint_s[tokens:, :] = jnp.zeros((joint_s.shape[0] - tokens, 3 * width), BF16)
        for copy in copies:
            copy.wait()

        @pl.loop(0, 3 * width // 256)
        def _(n):
            cols = pl.ds(pl.multiple_of(n * 256, 256), 256)
            scale = jnp.where(n < width // 256, 0.125, 1.0).astype(BF16)
            value = dot(hn_ref[...], w_s[:, cols])
            joint_s[0:tokens, cols] = value.astype(BF16) * scale

        pltpu.make_async_copy(joint_s, joint_ref, out_sem).start()

    @pl.when(step > 0)
    def _():
        image = step - 1
        base = pl.multiple_of(image * seq, 16)
        rows, keys = pl.ds(base, seq), pl.ds(base, window)
        live = mask_ref[image]
        masks = head_masks()
        for quad in range(width // 256):
            at = quad * 256
            q = joint_s[rows, at : at + 256]
            k = joint_s[keys, width + at : width + at + 256]
            v = joint_s[keys, 2 * width + at : 2 * width + at + 256]
            s = dot_bt(stack(q, masks), k)
            s = jnp.where(live > 0.5, s, MASKED)
            e = jnp.exp(s - jnp.max(s, axis=-1, keepdims=True))
            p = (e * (1.0 / jnp.sum(e, axis=-1, keepdims=True))).astype(BF16)
            p_ref[0, quad] = p
            ctx_ref[:, at : at + 256] = pick(dot(p, v), masks).astype(BF16)

    @pl.when(step == pl.num_programs(0) - 1)
    def _():
        pltpu.make_async_copy(joint_s, joint_ref, out_sem).wait()


def gelu_both(u):
    phi = 0.5 + 0.5 * lax.erf(u * 0.7071067811865476)
    bell = jnp.exp(-0.5 * (u * u)) * 0.3989422804014327
    return u * phi, phi + u * bell


def mlp_kernel(chunk, deps, g_ref, *refs):
    me, y, z = place()
    first = chunk == 0
    if first:
        (ctx_ref, x_ref, vec_ref), refs = refs[:3], refs[3:]
        pieces, refs = refs[:6], refs[6 + deps :]
        act_ref, pull_ref, out_ref, dh_ref, hn_ref, ht_ref, x1_ref, wu_s, wd_s, wo_s, sems = refs
        width = ctx_ref.shape[1]
        ups, downs, outs = packed_rows(pieces, (wu_s, wd_s, wo_s), me, y, width)
        early = start(outs, sems)
        late = start(ups + downs, sems, len(outs))
    else:
        (hn_ref, out_in, dh_in), refs = refs[:3], refs[3:]
        pieces, refs = refs[:4], refs[4 + deps :]
        act_ref, pull_ref, out_ref, dh_ref, wu_s, wd_s, sems = refs
        width = hn_ref.shape[1]
        ups, downs, _ = packed_rows(pieces, (wu_s, wd_s, None), me, y, width)
        early, late = [], start(ups + downs, sems)
    rows = wd_s.shape[0] // 4
    for copy in early:
        copy.wait()
    if first:
        gain, shift = vec_ref[2:3, :], vec_ref[3:4, :]

        @row_loop(ctx_ref.shape[0], 208)
        def _(i):
            part = pl.ds(pl.multiple_of(i * 208, 16), 208)
            middle = x_ref[part, :].astype(F32) + dot(ctx_ref[part, :], wo_s[...])
            x1_ref[part, :] = middle
            normal, factor = standardize(middle)
            hn_ref[part, :] = (normal * gain + shift).astype(BF16)

        owner_rows(hn_ref[...].T, ht_ref, me, y, z)
    for copy in late:
        copy.wait()
    for c in range(2):
        cols = []
        both = slice(2 * c * rows, 2 * (c + 1) * rows)
        for x in range(2):
            owner = me ^ (c + 2 * x)
            col = pl.ds(pl.multiple_of(owner * rows, rows), rows)
            act, slope = gelu_both(dot(hn_ref[...], wu_s[:, col]))
            at = (2 * c + x) * rows
            act_ref[:, at : at + rows] = act.astype(BF16)
            pull_ref[:, at : at + rows] = (dot_bt(g_ref[...], wd_s[at : at + rows, :]) * slope).astype(BF16)
            cols.append(col)
        plus = dot(act_ref[:, both], wd_s[both, :])
        wu = jnp.concatenate([wu_s[:, col] for col in cols], axis=1)
        back = dot_bt(pull_ref[:, both], wu)
        if c == 0 and first:
            out_ref[...] = plus
            dh_ref[...] = back
        elif c == 0:
            out_ref[...] = out_in[...] + plus
            dh_ref[...] = dh_in[...] + back
        else:
            out_ref[...] += plus
            dh_ref[...] += back


def mlp_grad_kernel(deps, act_ref, pull_ref, gt_ref, ht_ref, *refs):
    k0, k1, s0, s1 = refs[deps:]
    me, y, z = place()
    keep, send = (k0, k1), (s0, s1)
    width = gt_ref.shape[0]
    rows = act_ref.shape[1] // 4
    quarter = width // 4
    eighth = width // 16
    for c in range(2):
        for x in range(2):
            owner = me ^ (c + 2 * x)
            cols = slice((2 * c + x) * rows, (2 * c + x + 1) * rows)
            gd = dot(gt_ref[...], act_ref[:, cols]).astype(BF16)
            dest = (send if c else keep)[x]
            for part in range(4):
                dest[part, 0:quarter, :] = gd[part * quarter : (part + 1) * quarter, :]
            gu = dot(ht_ref[...], pull_ref[:, cols]).astype(BF16)
            where = pl.ds(pl.multiple_of(quarter + owner * eighth, eighth), eighth)
            for block in range(16):
                dest = (send if block // 8 else keep)[(block // 4) % 2]
                dest[block % 4, where, :] = gu[block * eighth : (block + 1) * eighth, :]


def middle_kernel(deps, x1_ref, out_in, dh_in, g_ref, vec_ref, ctx_ref, *refs):
    pieces, refs = refs[:6], refs[6 + deps :]
    result_ref, dx_ref, dctx_ref, k0, k1, s0, s1, dvec_ref, w_s, dy_s, ct_s, sems = refs
    me, y, z = place()
    tokens, width = ctx_ref.shape
    copies = start(packed_rows(pieces, (None, None, w_s), me, y, width)[2], sems)
    gain = vec_ref[2:3, :]
    dvec_ref[...] = jnp.zeros_like(dvec_ref)

    @row_loop(tokens, 208)
    def _(i):
        rows = pl.ds(pl.multiple_of(i * 208, 16), 208)
        middle = x1_ref[rows, :]
        result_ref[rows, :] = (middle + out_in[rows, :]).astype(BF16)
        normal, factor = standardize(middle)
        pull = dh_in[rows, :]
        dvec_ref[0:1, :] += jnp.sum(pull * normal, axis=0, keepdims=True)
        dvec_ref[1:2, :] += jnp.sum(pull, axis=0, keepdims=True)
        dx = g_ref[rows, :].astype(F32) + norm_back(pull * gain, normal, factor)
        dx_ref[rows, :] = dx
        dy_s[rows, :] = dx.astype(BF16)

    owner_rows(ctx_ref[...].T, ct_s, me, y, z)
    for copy in copies:
        copy.wait()
    dctx_ref[...] = dot_bt(dy_s[...], w_s[...]).astype(BF16)
    store_blocks(dot(ct_s[...], dy_s[...]).astype(BF16), (k0, k1), (s0, s1))


def store_blocks(value, keep, send, at=0):
    piece = value.shape[0] // 16
    for block in range(16):
        dest = (send if block // 8 else keep)[(block // 4) % 2]
        dest[block % 4, at : at + piece, :] = value[block * piece : (block + 1) * piece, :]


def back_kernel(quads, prior, deps, ht_ref, *refs):
    parts, refs = refs[: 5 * quads], refs[5 * quads :]
    if prior:
        before, refs = refs[:4], refs[4:]
    refs = refs[deps:]
    ends, djs = refs[:4], refs[4:]
    masks = head_masks()
    piece = ht_ref.shape[0] // 16
    if prior:
        for old, new in zip(before, ends):
            new[:, 0:piece, :] = old[...]
    for quad in range(quads):
        joint_q, joint_k, joint_v, p_ref, dctx_ref = parts[5 * quad : 5 * quad + 5]
        dj_ref = djs[quad]
        images, _, stacked, window = p_ref.shape
        seq = stacked // 4

        @pl.loop(0, images)
        def _(b):
            base = pl.multiple_of(b * seq, 16)
            rows, keys = pl.ds(base, seq), pl.ds(base, window)
            q, k, v = joint_q[rows, :], joint_k[keys, :], joint_v[keys, :]
            p = p_ref[b, 0]
            dm, qm = stack(dctx_ref[rows, :], masks), stack(q, masks)
            pf = p.astype(F32)
            prod = pf * dot_bt(dm, v)
            ds = (prod - pf * jnp.sum(prod, axis=-1, keepdims=True)).astype(BF16)
            dj_ref[rows, 0:256] = (pick(dot(ds, k), masks) * 0.125).astype(BF16)
            dj_ref[rows, 256:512] = dot_at(ds, qm)[0:seq, :].astype(BF16)
            dj_ref[rows, 512:768] = dot_at(p, dm)[0:seq, :].astype(BF16)

        grad = dot(ht_ref[...], dj_ref[...]).astype(BF16)
        store_blocks(grad, ends[:2], ends[2:], piece * (quad + prior))


def last_kernel(deps, dj0, dj1, dj2, x_ref, dx_ref, vec_ref, *refs):
    pieces, (out_ref, dvec_ref, w_s, dh_s, sems) = refs[:6], refs[6 + deps :]
    me, y, z = place()
    copies = start(shard_rows(pieces, w_s, me, y), sems)
    gain = vec_ref[0:1, :]
    dvec_ref[...] = jnp.zeros_like(dvec_ref)
    tokens, width = x_ref.shape
    for copy in copies:
        copy.wait()
    pull = jnp.concatenate(
        [dj[:, kind * 256 : kind * 256 + 256] for kind in range(3) for dj in (dj0, dj1, dj2)], axis=1
    )
    dh_s[...] = dot_bt(pull, w_s[...])

    @row_loop(tokens, 208)
    def _(i):
        rows = pl.ds(pl.multiple_of(i * 208, 16), 208)
        normal, factor = standardize(x_ref[rows, :].astype(F32))
        pull = dh_s[rows, :]
        dvec_ref[0:1, :] += jnp.sum(pull * normal, axis=0, keepdims=True)
        dvec_ref[1:2, :] += jnp.sum(pull, axis=0, keepdims=True)
        out_ref[rows, :] = dx_ref[rows, :] + norm_back(pull * gain, normal, factor)


def mlp_end_kernel(*refs):
    parts, (up_ref, down_ref, turn_s) = refs[:12], refs[12:]
    me, y, z = place()
    rows = parts[0].shape[0]
    half = rows // 2
    eighth = half // 4
    lanes = parts[0].shape[1]
    for chunk in range(3):
        for rel in range(4):
            piece = parts[chunk * 4 + rel]
            at = ((rel // 2) ^ y) * 2 + ((rel % 2) ^ z)
            where = pl.ds(pl.multiple_of(at * half, half), half)
            turn_s[where, :] = piece[0:half, :].astype(F32)
            where = pl.ds(pl.multiple_of(at * eighth, eighth), eighth)
            for owner in range(4):
                col = (owner * 3 + chunk) * lanes
                up_ref[where, col : col + lanes] = piece[half + owner * eighth : half + (owner + 1) * eighth, :].astype(F32)
        down_ref[chunk * lanes : (chunk + 1) * lanes, :] = turn_s[...].T


def rows_end_kernel(*refs):
    parts, (joint_ref, out_ref) = refs[:8], refs[8:]
    me, y, z = place()
    piece = parts[0].shape[0] // 2
    width = parts[0].shape[1]
    third = width // 3
    for chunk in range(2):
        for rel in range(4):
            value = parts[chunk * 4 + rel][...].astype(F32)
            at = ((rel // 2) ^ y) * 2 + ((rel % 2) ^ z)
            where = pl.ds(pl.multiple_of(at * piece, piece), piece)
            for half in range(2):
                quad = chunk * 2 + half - 1
                block = value[half * piece : (half + 1) * piece, :]
                if quad < 0:
                    out_ref[where, :] = block
                    continue
                for kind in range(3):
                    col = kind * width + quad * third
                    joint_ref[where, col : col + third] = block[:, kind * third : (kind + 1) * third]


def on_device(
    images,
    first_gain,
    first_shift,
    joint_weight,
    out_weight,
    second_gain,
    second_shift,
    up_weight,
    down_weight,
    keep_flags,
    cotangent,
):
    count, length, width = images.shape
    n_dp = lax.axis_size("dp")
    n_fs = lax.axis_size("fsdp")
    me = lax.axis_index("fsdp")
    y = lax.axis_index("dp") & 1
    seq = up_to(length, 16)
    window = up_to(seq, 256)
    tokens = count * seq
    long = tokens + window - seq
    ff = up_weight.shape[1]
    fourth = ff // n_fs
    third = fourth // 3
    eighth = width // 16

    def swap(axis, bit):
        n = n_dp if axis == "dp" else n_fs
        return lambda v: lax.ppermute(v, axis, [(i, i ^ bit) for i in range(n)])

    core, over_x, over_y, over_z = swap("fsdp", 1), swap("fsdp", 2), swap("dp", 1), swap("dp", 2)

    def call(body, outs, dense, pieces=(), deps=(), scratch=(), outside=False):
        args = [*dense, *pieces, *deps]
        return pl.pallas_call(
            body,
            out_shape=outs,
            in_specs=[vmem()] * len(dense) + [in_hbm()] * len(pieces) + [anywhere()] * len(deps),
            out_specs=[in_hbm() if outside else vmem()] * len(outs),
            scratch_shapes=list(scratch),
            compiler_params=pltpu.CompilerParams(vmem_limit_bytes=LIMIT),
            cost_estimate=cost(FLOPS, 0),
        )(*args)

    def shape(*dims, dtype=BF16):
        return jax.ShapeDtypeStruct(dims, dtype)

    def dma(n):
        return pltpu.SemaphoreType.DMA((n,))

    def tie(value, *tokens):
        return lax.optimization_barrier((value, *tokens))[0]

    def gather_halves(own, mine):
        near = core(own)
        xh = over_x(mine)
        yh = over_y(xh)
        return [own, near, xh, yh, core(xh), core(yh)]

    half = joint_weight.shape[0] // 2
    w_joint = gather_halves(joint_weight, lax.dynamic_slice_in_dim(joint_weight, y * half, half, 0))

    vec = jnp.concatenate([first_gain, first_shift, second_gain, second_shift])
    other = over_x(vec)
    both = jnp.stack([vec, core(vec), other, core(other)])
    both = both.reshape(n_fs, 4, -1)
    vecs = jnp.concatenate([lax.dynamic_index_in_dim(both, me ^ i, 0, False) for i in range(n_fs)], axis=1)
    vecs = jnp.pad(vecs.astype(F32), ((0, 4), (0, 0)))

    packed = (4 * (width // n_fs) + 3 * third, 3 * (width // n_fs))
    whole, mine, rest1, rest2 = call(
        pack_kernel,
        [shape(sum(packed), third), shape(sum(packed) // 2, third), *[shape(packed[0], third)] * 2],
        [],
        [up_weight, down_weight, out_weight],
        scratch=[dma(44)],
        outside=True,
    )
    near = core(whole)
    xh = over_x(tie(mine, w_joint[2]))
    yh = over_y(xh)
    w_rest = [[rest, core(rest), over_x(tie(rest, w_joint[3], other))] for rest in (rest1, rest2)]

    pads = ((0, 0), (0, seq - length), (0, 0))
    x = jnp.pad(images, pads).reshape(tokens, width)
    g = jnp.pad(cotangent, pads).reshape(tokens, width)
    live = jnp.pad(keep_flags, ((0, 0), (0, window - length))).astype(F32).reshape(count, 1, window)

    (hn1,) = call(first_norm_kernel, [shape(tokens, width)], [x, vecs])
    h1t, gt = call(turn_kernel, [shape(width, tokens), shape(width, tokens)], [hn1, g])

    def front(deps):
        prior = lambda i: jnp.maximum(i - 1, 0)
        return pl.pallas_call(
            lambda *refs: front_kernel(len(deps), *refs),
            grid=(1 + count,),
            out_shape=[shape(long, 3 * width), shape(count, 3, 4 * seq, window), shape(tokens, width)],
            in_specs=[
                pl.BlockSpec((tokens, width), lambda i: (0, 0)),
                pl.BlockSpec((count, 1, window), lambda i: (0, 0, 0)),
                *[in_hbm()] * 6,
                *[anywhere()] * len(deps),
            ],
            out_specs=[
                anywhere(),
                pl.BlockSpec((1, 3, 4 * seq, window), lambda i: (prior(i), 0, 0, 0)),
                pl.BlockSpec((seq, width), lambda i: (prior(i), 0)),
            ],
            scratch_shapes=[
                pltpu.VMEM((width, 3 * width), BF16),
                pltpu.VMEM((long, 3 * width), BF16),
                dma(6),
                pltpu.SemaphoreType.DMA,
            ],
            compiler_params=pltpu.CompilerParams(vmem_limit_bytes=LIMIT),
            cost_estimate=cost(FLOPS, 0),
        )(hn1, live, *w_joint, *deps)

    def plus(*terms):
        total = terms[0].astype(F32)
        for term in terms[1:]:
            total = total + term.astype(F32)
        return total.astype(BF16)

    class Chunk:
        def __init__(self, k0, k1, s0, s1):
            self.keeps, self.parts, self.stage = (k0, k1), [], 0
            self.bits = [1 << bit for bit in range(2, n_dp.bit_length() - 1)]
            self.fly([s0, s1], [core, core])

        def fly(self, arrays, hops):
            self.flying = [hop(array) for array, hop in zip(arrays, hops)]

        def sends(self):
            k0, k1 = self.keeps
            got, self.stage = self.flying, self.stage + 1
            if self.stage == 1:
                self.near = got[0]
                return [plus(k1, got[1])], [over_x]
            if self.stage == 2:
                self.rx = got[0]
                return [plus(k0[2:4], self.near[2:4], self.rx[2:4])], [over_y]
            if self.stage == 3:
                self.ry = got[0]
                return [plus(k0[1], self.near[1], self.rx[1], self.ry[1])], [over_z]
            if self.stage == 4:
                total = plus(k0[0], self.near[0], self.rx[0], self.ry[0], got[0])
            elif self.stage <= 4 + len(self.bits):
                total = plus(self.sent[0], got[0])
            else:
                self.parts = [*(self.parts or [self.sent[0]]), *got]
                return ([got[0]], [over_y]) if len(got) == 2 else ([], [])
            if self.stage < 4 + len(self.bits):
                return [total], [swap("dp", self.bits[self.stage - 4])]
            return [total, total], [over_z, over_y]

        @property
        def done(self):
            return len(self.parts) == 4

    class Small:
        def __init__(self, total):
            self.total, self.parts, self.done = total, [], False
            self.hops = [core, over_x] + [swap("dp", 1 << bit) for bit in range(n_dp.bit_length() - 1)]
            self.flying = None

        def fly(self, arrays, hops):
            self.flying = [hop(array) for array, hop in zip(arrays, hops)]

        def sends(self):
            if self.flying is not None:
                self.total = self.sent[0] + self.flying[0]
            if not self.hops:
                self.done = True
                return [], []
            hop, self.hops = self.hops[0], self.hops[1:]
            return [self.total], [hop]

    def advance(items, *tokens):
        plans = [item.sends() for item in items]
        home = [part for item in items for part in item.parts[1:]]
        flat = lax.optimization_barrier((*[array for arrays, _ in plans for array in arrays], *home, *tokens))
        sent, at = home, 0
        for item, (arrays, hops) in zip(items, plans):
            item.sent = list(flat[at : at + len(arrays)])
            at += len(arrays)
            if arrays:
                item.fly(item.sent, hops)
                sent = [*sent, item.sent[0]]
        return sent

    joint, probs, ctx = front([])
    w_first = [whole, near, xh, yh, core(xh), core(yh)]

    wide = shape(tokens, n_fs * third)
    full = shape(tokens, width, dtype=F32)
    weights = [pltpu.VMEM((width, n_fs * third), BF16), pltpu.VMEM((n_fs * third, width), BF16)]

    def grads(act, pull, deps):
        ends = call(
            lambda *refs: mlp_grad_kernel(len(deps), *refs),
            [shape(4, width // 2, third)] * 4,
            [act, pull, gt, h2t],
            deps=deps,
        )
        return Chunk(*ends)

    def mlp(chunk, out_sum, dh, deps):
        return call(
            lambda *refs: mlp_kernel(chunk, len(deps), *refs),
            [wide, wide, full, full],
            [g, hn2, out_sum, dh],
            w_rest[chunk - 1],
            deps,
            [*weights, dma(28)],
        )

    act, pull, out_sum, dh, hn2, h2t, x1 = call(
        lambda *refs: mlp_kernel(0, 0, *refs),
        [wide, wide, full, full, shape(tokens, width), shape(width, tokens), full],
        [g, ctx, x, vecs],
        w_first,
        scratch=[*weights, pltpu.VMEM((width, width), BF16), dma(80)],
    )
    w_rest[0].append(core(tie(w_rest[0][2], x1)))
    m0 = grads(act, pull, [])
    act, pull, out_sum, dh = mlp(1, out_sum, dh, [])
    w_rest[1].append(core(tie(w_rest[1][2], dh)))
    m1 = grads(act, pull, advance([m0], dh))
    act, pull, out_sum, dh = mlp(2, out_sum, dh, [])
    m2 = grads(act, pull, advance([m1, m0], dh))
    deps = []
    result, dx1, dctx, *ends, dvec2 = call(
        lambda *refs: middle_kernel(len(deps), *refs),
        [
            shape(tokens, width),
            shape(tokens, width, dtype=F32),
            shape(tokens, width),
            *[shape(4, eighth, width)] * 4,
            shape(8, width, dtype=F32),
        ],
        [x1, out_sum, dh, g, vecs, ctx],
        w_first,
        deps,
        [pltpu.VMEM((width, width), BF16), pltpu.VMEM((tokens, width), BF16), pltpu.VMEM((width, tokens), BF16), dma(24)],
    )

    def back(first, quads, prior, deps):
        sets, specs = [], []
        for quad in range(first, first + quads):
            sets += [joint, joint, joint, probs, dctx]
            specs += [pl.BlockSpec((long, 256), lambda i, c=kind * (width // 256) + quad: (0, c)) for kind in range(3)]
            specs += [
                pl.BlockSpec((count, 1, 4 * seq, window), lambda i, quad=quad: (0, quad, 0, 0)),
                pl.BlockSpec((tokens, 256), lambda i, quad=quad: (0, quad)),
            ]
        size = eighth * (quads + (1 if prior else 0))
        return pl.pallas_call(
            lambda *refs: back_kernel(quads, 1 if prior else 0, len(deps), *refs),
            grid=(1,),
            out_shape=[shape(4, size, width)] * 4 + [shape(tokens, width)] * quads,
            in_specs=[vmem(), *specs, *[vmem()] * len(prior), *[anywhere()] * len(deps)],
            out_specs=[vmem()] * (4 + quads),
            compiler_params=pltpu.CompilerParams(vmem_limit_bytes=LIMIT),
            cost_estimate=cost(FLOPS, 0),
        )(h1t, *sets, *prior, *deps)

    *ends, dj0 = back(0, 1, ends, advance([m2, m0], dctx))
    oj = Chunk(*ends)
    *ends, dj1 = back(1, 1, [], advance([m1, m0], dj0))
    *ends, dj2 = back(2, 1, ends, advance([oj, m1, m0], dj1))
    jj = Chunk(*ends)
    deps = advance([jj, m2, m1, m0], dj2)
    grad_x, dvec1 = call(
        lambda *refs: last_kernel(len(deps), *refs),
        [shape(tokens, width, dtype=F32), shape(8, width, dtype=F32)],
        [dj0, dj1, dj2, x, dx1, vecs],
        w_joint,
        deps,
        [pltpu.VMEM((width, 3 * width), BF16), pltpu.VMEM((tokens, width), F32), dma(6)],
    )
    small = Small(jnp.concatenate([dvec1[0:2], dvec2[0:2]], axis=0))
    tail = [[oj, m2, m1, m0, small], [jj, oj, m2, m1, m0, small]]
    tokens = [dvec1]
    items = [jj, oj, m2, m1, m0, small]
    while any(not item.done for item in items):
        group = tail.pop(0) if tail else items
        advance([item for item in group if not item.done], *tokens)
        tokens = []
    mine = lax.dynamic_slice_in_dim(small.total, me * (width // n_fs), width // n_fs, 1)

    grad_up, grad_down = call(
        mlp_end_kernel,
        [shape(width // n_fs, ff, dtype=F32), shape(fourth, width, dtype=F32)],
        [*m0.parts, *m1.parts, *m2.parts],
        scratch=[pltpu.VMEM((width, third), F32)],
    )
    grad_joint, grad_out = call(
        rows_end_kernel,
        [shape(width // n_fs, 3 * width, dtype=F32), shape(width // n_fs, width, dtype=F32)],
        [*oj.parts, *jj.parts],
    )
    output = result.reshape(count, seq, width)[:, :length]
    grad_images = grad_x.reshape(count, seq, width)[:, :length]
    return (
        output,
        grad_images,
        mine[0],
        mine[1],
        grad_joint,
        grad_out,
        mine[2],
        mine[3],
        grad_up,
        grad_down,
    )


def solution(mesh):
    rows = P("fsdp", None)
    tokens = P(("dp", "fsdp"), None, None)
    one = P("fsdp")
    return jax.shard_map(
        on_device,
        mesh=mesh,
        in_specs=(tokens, one, one, rows, rows, one, one, rows, rows, P(("dp", "fsdp"), None), tokens),
        out_specs=(tokens, tokens, one, one, rows, rows, one, one, rows, rows),
        check_vma=False,
    )
```

```python
import jax
import jax.numpy as jnp
from jax import lax
from jax.experimental import pallas as pl
from jax.experimental.pallas import tpu as pltpu
from jax.sharding import PartitionSpec as P

HEADS = 12
EPS = 1e-06
MASKED = -1e30
F32 = jnp.float32
BF16 = jnp.bfloat16
VM = pltpu.VMEM
ANY = pl.ANY
LIMIT = 12 * 1024 * 1024
FLOPS = int(1.15e9 * 0.3)


def vmem():
    return pl.BlockSpec(memory_space=VM)


def anywhere():
    return pl.BlockSpec(memory_space=ANY)


def in_hbm():
    return pl.BlockSpec(memory_space=pltpu.HBM)


def up_to(value, step):
    return (value + step - 1) // step * step


def dot(a, b):
    return jnp.dot(a, b, preferred_element_type=F32)


def dot_bt(a, b):
    return lax.dot_general(a, b, (((1,), (1,)), ((), ())), preferred_element_type=F32)


def dot_at(a, b):
    return lax.dot_general(a, b, (((0,), (0,)), ((), ())), preferred_element_type=F32)


def place():
    me = lax.axis_index("fsdp")
    dp = lax.axis_index("dp")
    return me, dp & 1, (dp >> 1) & 1


def start(table, sems, base=0):
    copies = []
    for index, (source, first, count, dest, at, col) in enumerate(table):
        src = source if count == source.shape[0] else source.at[pl.ds(pl.multiple_of(first, 16), count)]
        where = pl.ds(pl.multiple_of(at, 16), count)
        into = dest.at[where] if col is None else dest.at[where, col : col + source.shape[1]]
        copy = pltpu.make_async_copy(src, into, sems.at[base + index])
        copy.start()
        copies.append(copy)
    return copies


def cost(flops, moved):
    return pl.CostEstimate(flops=flops, bytes_accessed=moved, transcendentals=0)


def shard_rows(pieces, dest, me, y):
    rows = pieces[0].shape[0]
    half = rows // 2
    starts = (
        me * rows,
        (me ^ 1) * rows,
        (me ^ 2) * rows + y * half,
        (me ^ 2) * rows + (1 - y) * half,
        (me ^ 3) * rows + y * half,
        (me ^ 3) * rows + (1 - y) * half,
    )
    return [(piece, 0, piece.shape[0], dest, at, None) for piece, at in zip(pieces, starts)]


def packed_rows(pieces, dests, me, y, width, chunk=0):
    rows = width // 4
    n_halves = 2 if len(pieces) == 6 else 1
    owners = ((0, (0, 1)), (1, (0, 1)), (2, (y,)), (2, (1 - y,)), (3, (y,)), (3, (1 - y,)))
    if n_halves == 1:
        owners = tuple((rel, (0,)) for rel in range(4))
    tables = ([], [], [])
    for piece, (rel, halves) in zip(pieces, owners):
        size = piece.shape[0] // len(halves)
        for index, half in enumerate(halves):
            first = index * size if len(halves) > 1 or piece.shape[0] < 4 * width else chunk * 2 * width
            for table, dest, blocks, count, at in (
                (tables[0], dests[0], 4, rows // n_halves, (me ^ rel) * rows),
                (tables[1], dests[1], 3, 256 // n_halves, (0, 2, 1, 3)[rel] * 256),
                (tables[2], dests[2], 3, rows // n_halves, (me ^ rel) * rows),
            ):
                for block in range(blocks):
                    table.append((piece, first, count, dest, at + half * count, block * 256))
                    first = first + count
    return tables


def pack_kernel(up_ref, down_ref, out_ref, whole_ref, half_ref, rest_ref, sems):
    me, y, z = place()
    rows, third = up_ref.shape[0], down_ref.shape[0] // 3
    copies = []

    def put(source, first, count, col, dest, at):
        copy = pltpu.make_async_copy(
            source.at[pl.ds(pl.multiple_of(first, 16), count), col : col + third],
            dest.at[pl.ds(at, count)],
            sems.at[len(copies)],
        )
        copy.start()
        copies.append(copy)

    for dest, halves in ((half_ref, (y,)), (whole_ref, (0, 1))):
        at = 0
        for half in halves:
            for source, first, count, cols in (
                (up_ref, 0, rows // 2, [owner * 3 * third for owner in range(4)]),
                (down_ref, 0, third // 2, [block * third for block in range(3)]),
                (out_ref, 0, rows // 2, [block * third for block in range(3)]),
            ):
                for col in cols:
                    put(source, first + half * count, count, col, dest, at)
                    at += count
    at = 0
    for chunk in (1, 2):
        for owner in range(4):
            put(up_ref, 0, rows, (owner * 3 + chunk) * third, rest_ref, at)
            at += rows
        for block in range(3):
            put(down_ref, chunk * third, third, block * third, rest_ref, at)
            at += third
    for copy in copies:
        copy.wait()


def standardize(value):
    mean = jnp.mean(value, axis=-1, keepdims=True)
    center = value - mean
    spread = jnp.mean(center * center, axis=-1, keepdims=True)
    factor = lax.rsqrt(spread + EPS)
    return center * factor, factor


def norm_back(upstream, normal, factor):
    first = jnp.mean(upstream, axis=-1, keepdims=True)
    second = jnp.mean(upstream * normal, axis=-1, keepdims=True)
    return factor * (upstream - first - normal * second)


def owner_rows(turned, dest, me, y, z):
    piece = turned.shape[0] // 16
    for block in range(16):
        owner, yb, zb = block // 4, (block // 2) % 2, block % 2
        rel = owner ^ me
        at = (rel & 1) * 8 + (rel >> 1) * 4 + (yb ^ y) * 2 + (zb ^ z)
        where = pl.ds(pl.multiple_of(at * piece, piece), piece)
        dest[where, :] = turned[block * piece : (block + 1) * piece, :]


def quarter_rows(turned, dest, y, z):
    piece = turned.shape[0] // 4
    for block in range(4):
        yb, zb = block // 2, block % 2
        at = (yb ^ y) * 2 + (zb ^ z)
        where = pl.ds(pl.multiple_of(at * piece, piece), piece)
        dest[where, :] = turned[block * piece : (block + 1) * piece, :]


def row_loop(tokens, step):
    return pl.loop(0, tokens // step)


def first_norm_kernel(x_ref, vec_ref, hn_ref):
    gain, shift = vec_ref[0:1, :], vec_ref[1:2, :]

    @row_loop(x_ref.shape[0], 208)
    def _(i):
        rows = pl.ds(pl.multiple_of(i * 208, 16), 208)
        normal, factor = standardize(x_ref[rows, :].astype(F32))
        hn_ref[rows, :] = (normal * gain + shift).astype(BF16)


def turn_kernel(hn_ref, g_ref, h1t_ref, gt_ref):
    me, y, z = place()
    owner_rows(hn_ref[...].T, h1t_ref, me, y, z)
    quarter_rows(g_ref[...].T, gt_ref, y, z)


def head_masks():
    lane = lax.broadcasted_iota(jnp.int32, (1, 256), 1) // 64
    return [lane == h for h in range(4)]


def stack(value, masks):
    return jnp.concatenate([value * mask.astype(BF16) for mask in masks], axis=0)


def pick(value, masks):
    seq = value.shape[0] // 4
    total = jnp.where(masks[0], value[0:seq], 0.0)
    for h in range(1, 4):
        total = jnp.where(masks[h], value[h * seq : (h + 1) * seq], total)
    return total


def front_kernel(deps, hn_ref, mask_ref, *refs):
    pieces, (joint_ref, p_ref, ctx_ref, w_s, joint_s, sems, out_sem) = refs[:6], refs[6 + deps :]
    me, y, z = place()
    step = pl.program_id(0)
    tokens, width = hn_ref.shape
    seq, window = ctx_ref.shape[0], mask_ref.shape[2]

    @pl.when(step == 0)
    def _():
        copies = start(shard_rows(pieces, w_s, me, y), sems)
        joint_s[tokens:, :] = jnp.zeros((joint_s.shape[0] - tokens, 3 * width), BF16)
        for copy in copies:
            copy.wait()

        @pl.loop(0, 3 * width // 256)
        def _(n):
            cols = pl.ds(pl.multiple_of(n * 256, 256), 256)
            scale = jnp.where(n < width // 256, 0.125, 1.0).astype(BF16)
            value = dot(hn_ref[...], w_s[:, cols])
            joint_s[0:tokens, cols] = value.astype(BF16) * scale

        pltpu.make_async_copy(joint_s, joint_ref, out_sem).start()

    @pl.when(step > 0)
    def _():
        image = step - 1
        base = pl.multiple_of(image * seq, 16)
        rows, keys = pl.ds(base, seq), pl.ds(base, window)
        live = mask_ref[image]
        masks = head_masks()
        for quad in range(width // 256):
            at = quad * 256
            q = joint_s[rows, at : at + 256]
            k = joint_s[keys, width + at : width + at + 256]
            v = joint_s[keys, 2 * width + at : 2 * width + at + 256]
            s = dot_bt(stack(q, masks), k)
            s = jnp.where(live > 0.5, s, MASKED)
            e = jnp.exp(s - jnp.max(s, axis=-1, keepdims=True))
            p = (e * (1.0 / jnp.sum(e, axis=-1, keepdims=True))).astype(BF16)
            p_ref[0, quad] = p
            ctx_ref[:, at : at + 256] = pick(dot(p, v), masks).astype(BF16)

    @pl.when(step == pl.num_programs(0) - 1)
    def _():
        pltpu.make_async_copy(joint_s, joint_ref, out_sem).wait()


def gelu_both(u):
    phi = 0.5 + 0.5 * lax.erf(u * 0.7071067811865476)
    bell = jnp.exp(-0.5 * (u * u)) * 0.3989422804014327
    return u * phi, phi + u * bell


def mlp_kernel(chunk, deps, g_ref, *refs):
    me, y, z = place()
    first = chunk == 0
    if first:
        (ctx_ref, x_ref, vec_ref), refs = refs[:3], refs[3:]
        pieces, refs = refs[:6], refs[6 + deps :]
        act_ref, pull_ref, out_ref, dh_ref, hn_ref, ht_ref, x1_ref, wu_s, wd_s, wo_s, sems = refs
        width = ctx_ref.shape[1]
        ups, downs, outs = packed_rows(pieces, (wu_s, wd_s, wo_s), me, y, width)
        early = start(outs, sems)
        late = start(ups + downs, sems, len(outs))
    else:
        (hn_ref, out_in, dh_in), refs = refs[:3], refs[3:]
        pieces, refs = refs[:4], refs[4 + deps :]
        act_ref, pull_ref, out_ref, dh_ref, wu_s, wd_s, sems = refs
        width = hn_ref.shape[1]
        ups, downs, _ = packed_rows(pieces, (wu_s, wd_s, None), me, y, width, chunk - 1)
        early, late = [], start(ups + downs, sems)
    rows = wd_s.shape[0] // 4
    for copy in early:
        copy.wait()
    if first:
        gain, shift = vec_ref[2:3, :], vec_ref[3:4, :]

        @row_loop(ctx_ref.shape[0], 208)
        def _(i):
            part = pl.ds(pl.multiple_of(i * 208, 16), 208)
            middle = x_ref[part, :].astype(F32) + dot(ctx_ref[part, :], wo_s[...])
            x1_ref[part, :] = middle
            normal, factor = standardize(middle)
            hn_ref[part, :] = (normal * gain + shift).astype(BF16)

        owner_rows(hn_ref[...].T, ht_ref, me, y, z)
    for copy in late:
        copy.wait()
    for c in range(2):
        cols = []
        both = slice(2 * c * rows, 2 * (c + 1) * rows)
        for x in range(2):
            owner = me ^ (c + 2 * x)
            col = pl.ds(pl.multiple_of(owner * rows, rows), rows)
            act, slope = gelu_both(dot(hn_ref[...], wu_s[:, col]))
            at = (2 * c + x) * rows
            act_ref[:, at : at + rows] = act.astype(BF16)
            pull_ref[:, at : at + rows] = (dot_bt(g_ref[...], wd_s[at : at + rows, :]) * slope).astype(BF16)
            cols.append(col)
        plus = dot(act_ref[:, both], wd_s[both, :])
        wu = jnp.concatenate([wu_s[:, col] for col in cols], axis=1)
        back = dot_bt(pull_ref[:, both], wu)
        if c == 0 and first:
            out_ref[...] = plus
            dh_ref[...] = back
        elif c == 0:
            out_ref[...] = out_in[...] + plus
            dh_ref[...] = dh_in[...] + back
        else:
            out_ref[...] += plus
            dh_ref[...] += back


def mlp_grad_kernel(deps, act_ref, pull_ref, gt_ref, ht_ref, *refs):
    k0, k1, s0, s1 = refs[deps:]
    me, y, z = place()
    keep, send = (k0, k1), (s0, s1)
    width = gt_ref.shape[0]
    rows = act_ref.shape[1] // 4
    quarter = width // 4
    eighth = width // 16
    for c in range(2):
        for x in range(2):
            owner = me ^ (c + 2 * x)
            cols = slice((2 * c + x) * rows, (2 * c + x + 1) * rows)
            gd = dot(gt_ref[...], act_ref[:, cols]).astype(BF16)
            dest = (send if c else keep)[x]
            for part in range(4):
                dest[part, 0:quarter, :] = gd[part * quarter : (part + 1) * quarter, :]
            gu = dot(ht_ref[...], pull_ref[:, cols]).astype(BF16)
            where = pl.ds(pl.multiple_of(quarter + owner * eighth, eighth), eighth)
            for block in range(16):
                dest = (send if block // 8 else keep)[(block // 4) % 2]
                dest[block % 4, where, :] = gu[block * eighth : (block + 1) * eighth, :]


def middle_kernel(deps, x1_ref, out_in, dh_in, g_ref, vec_ref, ctx_ref, *refs):
    before, refs = refs[:4], refs[4:]
    pieces, refs = refs[:6], refs[6 + deps :]
    result_ref, dx_ref, dctx_ref, k0, k1, s0, s1, dvec_ref, w_s, dy_s, ct_s, sems = refs
    me, y, z = place()
    tokens, width = ctx_ref.shape
    copies = start(packed_rows(pieces, (None, None, w_s), me, y, width)[2], sems)
    gain = vec_ref[2:3, :]
    dvec_ref[...] = jnp.zeros_like(dvec_ref)

    @row_loop(tokens, 208)
    def _(i):
        rows = pl.ds(pl.multiple_of(i * 208, 16), 208)
        middle = x1_ref[rows, :]
        result_ref[rows, :] = (middle + out_in[rows, :]).astype(BF16)
        normal, factor = standardize(middle)
        pull = dh_in[rows, :]
        dvec_ref[0:1, :] += jnp.sum(pull * normal, axis=0, keepdims=True)
        dvec_ref[1:2, :] += jnp.sum(pull, axis=0, keepdims=True)
        dx = g_ref[rows, :].astype(F32) + norm_back(pull * gain, normal, factor)
        dx_ref[rows, :] = dx
        dy_s[rows, :] = dx.astype(BF16)

    owner_rows(ctx_ref[...].T, ct_s, me, y, z)
    for copy in copies:
        copy.wait()
    dctx_ref[...] = dot_bt(dy_s[...], w_s[...]).astype(BF16)
    value = dot(ct_s[...], dy_s[...]).astype(BF16)
    piece = width // 16
    base = before[0].shape[1]
    for old, new in zip(before, (k0, k1, s0, s1)):
        new[:, 0:base, :] = old[...]
    for block in range(16):
        dest = ((s0, s1) if block // 8 else (k0, k1))[(block // 4) % 2]
        for cols in range(width // 256):
            at = base + cols * piece
            dest[block % 4, at : at + piece, :] = value[block * piece : (block + 1) * piece, cols * 256 : cols * 256 + 256]


def store_blocks(value, keep, send, at=0):
    piece = value.shape[0] // 16
    for block in range(16):
        dest = (send if block // 8 else keep)[(block // 4) % 2]
        dest[block % 4, at : at + piece, :] = value[block * piece : (block + 1) * piece, :]


def back_kernel(quads, prior, deps, ht_ref, *refs):
    parts, refs = refs[: 5 * quads], refs[5 * quads :]
    if prior:
        before, refs = refs[:4], refs[4:]
    refs = refs[deps:]
    ends, djs = refs[:4], refs[4:]
    masks = head_masks()
    piece = ht_ref.shape[0] // 16
    if prior:
        for old, new in zip(before, ends):
            new[:, 0 : old.shape[1], :] = old[...]
    for quad in range(quads):
        joint_q, joint_k, joint_v, p_ref, dctx_ref = parts[5 * quad : 5 * quad + 5]
        dj_ref = djs[quad]
        images, _, stacked, window = p_ref.shape
        seq = stacked // 4

        @pl.loop(0, images)
        def _(b):
            base = pl.multiple_of(b * seq, 16)
            rows, keys = pl.ds(base, seq), pl.ds(base, window)
            q, k, v = joint_q[rows, :], joint_k[keys, :], joint_v[keys, :]
            p = p_ref[b, 0]
            dm, qm = stack(dctx_ref[rows, :], masks), stack(q, masks)
            pf = p.astype(F32)
            prod = pf * dot_bt(dm, v)
            ds = (prod - pf * jnp.sum(prod, axis=-1, keepdims=True)).astype(BF16)
            dj_ref[rows, 0:256] = (pick(dot(ds, k), masks) * 0.125).astype(BF16)
            dj_ref[rows, 256:512] = dot_at(ds, qm)[0:seq, :].astype(BF16)
            dj_ref[rows, 512:768] = dot_at(p, dm)[0:seq, :].astype(BF16)

        grad = dot(ht_ref[...], dj_ref[...]).astype(BF16)
        store_blocks(grad, ends[:2], ends[2:], piece * (quad + prior))


def last_kernel(deps, dj0, dj1, dj2, x_ref, dx_ref, vec_ref, *refs):
    pieces, (out_ref, dvec_ref, w_s, dh_s, sems) = refs[:6], refs[6 + deps :]
    me, y, z = place()
    copies = start(shard_rows(pieces, w_s, me, y), sems)
    gain = vec_ref[0:1, :]
    dvec_ref[...] = jnp.zeros_like(dvec_ref)
    tokens, width = x_ref.shape
    for copy in copies:
        copy.wait()
    pull = jnp.concatenate(
        [dj[:, kind * 256 : kind * 256 + 256] for kind in range(3) for dj in (dj0, dj1, dj2)], axis=1
    )
    dh_s[...] = dot_bt(pull, w_s[...])

    @row_loop(tokens, 208)
    def _(i):
        rows = pl.ds(pl.multiple_of(i * 208, 16), 208)
        normal, factor = standardize(x_ref[rows, :].astype(F32))
        pull = dh_s[rows, :]
        dvec_ref[0:1, :] += jnp.sum(pull * normal, axis=0, keepdims=True)
        dvec_ref[1:2, :] += jnp.sum(pull, axis=0, keepdims=True)
        out_ref[rows, :] = dx_ref[rows, :] + norm_back(pull * gain, normal, factor)


def mlp_end_kernel(*refs):
    parts, (up_ref, down_ref, out_ref, turn_s) = refs[:12], refs[12:]
    me, y, z = place()
    rows, lanes = parts[0].shape
    half = rows // 2
    eighth = half // 4
    for chunk in range(3):
        for rel in range(4):
            piece = parts[chunk * 4 + rel]
            at = ((rel // 2) ^ y) * 2 + ((rel % 2) ^ z)
            where = pl.ds(pl.multiple_of(at * half, half), half)
            turn_s[where, :] = piece[0:half, :].astype(F32)
            where = pl.ds(pl.multiple_of(at * eighth, eighth), eighth)
            for owner in range(4):
                col = (owner * 3 + chunk) * lanes
                up_ref[where, col : col + lanes] = piece[half + owner * eighth : half + (owner + 1) * eighth, :].astype(F32)
            if chunk == 2:
                for block in range(3):
                    first = rows + block * eighth
                    col = block * lanes
                    out_ref[where, col : col + lanes] = piece[first : first + eighth, :].astype(F32)
        down_ref[chunk * lanes : (chunk + 1) * lanes, :] = turn_s[...].T


def rows_end_kernel(*refs):
    parts, joint_ref = refs[:4], refs[4]
    me, y, z = place()
    width = parts[0].shape[1]
    third = width // 3
    piece = parts[0].shape[0] // 3
    for rel in range(4):
        at = ((rel // 2) ^ y) * 2 + ((rel % 2) ^ z)
        where = pl.ds(pl.multiple_of(at * piece, piece), piece)
        for quad in range(3):
            block = parts[rel][quad * piece : (quad + 1) * piece, :].astype(F32)
            for kind in range(3):
                col = kind * width + quad * third
                joint_ref[where, col : col + third] = block[:, kind * third : (kind + 1) * third]


def on_device(
    images,
    first_gain,
    first_shift,
    joint_weight,
    out_weight,
    second_gain,
    second_shift,
    up_weight,
    down_weight,
    keep_flags,
    cotangent,
):
    count, length, width = images.shape
    n_dp = lax.axis_size("dp")
    n_fs = lax.axis_size("fsdp")
    me = lax.axis_index("fsdp")
    y = lax.axis_index("dp") & 1
    seq = up_to(length, 16)
    window = up_to(seq, 256)
    tokens = count * seq
    long = tokens + window - seq
    ff = up_weight.shape[1]
    fourth = ff // n_fs
    third = fourth // 3
    eighth = width // 16

    def swap(axis, bit):
        n = n_dp if axis == "dp" else n_fs
        return lambda v: lax.ppermute(v, axis, [(i, i ^ bit) for i in range(n)])

    core, over_x, over_y, over_z = swap("fsdp", 1), swap("fsdp", 2), swap("dp", 1), swap("dp", 2)

    def call(body, outs, dense, pieces=(), deps=(), scratch=(), outside=False, us=1):
        args = [*dense, *pieces, *deps]
        return pl.pallas_call(
            body,
            out_shape=outs,
            in_specs=[vmem()] * len(dense) + [in_hbm()] * len(pieces) + [anywhere()] * len(deps),
            out_specs=[in_hbm() if outside else vmem()] * len(outs),
            scratch_shapes=list(scratch),
            compiler_params=pltpu.CompilerParams(vmem_limit_bytes=LIMIT),
            cost_estimate=cost(us * FLOPS, 0),
        )(*args)

    def shape(*dims, dtype=BF16):
        return jax.ShapeDtypeStruct(dims, dtype)

    def dma(n):
        return pltpu.SemaphoreType.DMA((n,))

    def tie(value, *tokens):
        return lax.optimization_barrier((value, *tokens))[0]

    half = joint_weight.shape[0] // 2
    xh_joint = over_x(lax.dynamic_slice_in_dim(joint_weight, y * half, half, 0))

    vec = jnp.concatenate([first_gain, first_shift, second_gain, second_shift])
    other = over_x(vec)
    both = jnp.stack([vec, core(vec), other, core(other)])
    both = both.reshape(n_fs, 4, -1)
    vecs = jnp.concatenate([lax.dynamic_index_in_dim(both, me ^ i, 0, False) for i in range(n_fs)], axis=1)
    vecs = jnp.pad(vecs.astype(F32), ((0, 4), (0, 0)))

    packed = (4 * (width // n_fs) + 3 * third, 3 * (width // n_fs))
    whole, mine, rest = call(
        pack_kernel,
        [shape(sum(packed), third), shape(sum(packed) // 2, third), shape(2 * packed[0], third)],
        [],
        [up_weight, down_weight, out_weight],
        scratch=[dma(44)],
        outside=True,
    )
    yh_joint = over_y(tie(xh_joint, mine, whole))
    w_joint = [joint_weight, core(joint_weight), xh_joint, yh_joint, core(xh_joint), core(yh_joint)]
    near = core(whole)
    xh = over_x(tie(mine, xh_joint, other))
    yh = over_y(xh)
    w_rest = [rest, core(rest), over_x(tie(rest, w_joint[3], vecs))]

    pads = ((0, 0), (0, seq - length), (0, 0))
    x = jnp.pad(images, pads).reshape(tokens, width)
    g = jnp.pad(cotangent, pads).reshape(tokens, width)
    live = jnp.pad(keep_flags, ((0, 0), (0, window - length))).astype(F32).reshape(count, 1, window)

    (hn1,) = call(first_norm_kernel, [shape(tokens, width)], [x, vecs])
    h1t, gt = call(turn_kernel, [shape(width, tokens), shape(width, tokens)], [hn1, g])

    def front(deps):
        prior = lambda i: jnp.maximum(i - 1, 0)
        return pl.pallas_call(
            lambda *refs: front_kernel(len(deps), *refs),
            grid=(1 + count,),
            out_shape=[pltpu.HBM((long, 3 * width), BF16), pltpu.HBM((count, 3, 4 * seq, window), BF16), shape(tokens, width)],
            in_specs=[
                pl.BlockSpec((tokens, width), lambda i: (0, 0)),
                pl.BlockSpec((count, 1, window), lambda i: (0, 0, 0)),
                *[in_hbm()] * 6,
                *[anywhere()] * len(deps),
            ],
            out_specs=[
                anywhere(),
                pl.BlockSpec((1, 3, 4 * seq, window), lambda i: (prior(i), 0, 0, 0)),
                pl.BlockSpec((seq, width), lambda i: (prior(i), 0)),
            ],
            scratch_shapes=[
                pltpu.VMEM((width, 3 * width), BF16),
                pltpu.VMEM((long, 3 * width), BF16),
                dma(6),
                pltpu.SemaphoreType.DMA,
            ],
            compiler_params=pltpu.CompilerParams(vmem_limit_bytes=LIMIT),
            cost_estimate=cost(14 * FLOPS, 0),
        )(hn1, live, *w_joint, *deps)

    def plus(*terms):
        total = terms[0].astype(F32)
        for term in terms[1:]:
            total = total + term.astype(F32)
        return total.astype(BF16)

    far_bits = [1 << bit for bit in range(2, n_dp.bit_length() - 1)]

    class Chunk:
        def __init__(self, k0, k1, s0, s1):
            self.keeps, self.parts, self.stage = (k0, k1), [], 0
            self.hops = [[over_x], [over_y], [over_z], *[[swap("dp", bit)] for bit in far_bits], [over_z, over_y], [over_y], []]
            self.flying = [core(s0), core(s1)]

        def sends(self):
            k0, k1 = self.keeps
            got, self.stage = self.flying, self.stage + 1
            left = len(self.hops) - self.stage
            if self.stage == 1:
                self.near = got[0]
                return [plus(k1, got[1])]
            if self.stage == 2:
                self.rx = got[0]
                return [plus(k0[2:4], self.near[2:4], self.rx[2:4])]
            if self.stage == 3:
                self.ry = got[0]
                return [plus(k0[1], self.near[1], self.rx[1], self.ry[1])]
            if self.stage == 4:
                total = plus(k0[0], self.near[0], self.rx[0], self.ry[0], got[0])
                return [total] * (2 if left == 2 else 1)
            if left >= 2:
                return [plus(self.sent[0], got[0])] * (2 if left == 2 else 1)
            if left == 1:
                self.parts = [self.sent[0], *got]
                rounds[-1] += got[1:]
                return got[:1]
            self.parts = self.parts + got
            rounds[-1] += got
            return []

        def fly(self):
            self.flying = [hop(array) for array, hop in zip(self.sent, self.hops[self.stage - 1])]

        @property
        def done(self):
            return len(self.parts) == 4

        def hold(self, tokens):
            if self.stage <= 3:
                k0, k1 = self.keeps
                self.keeps = (tie(k0, *tokens), tie(k1, *tokens)) if self.stage == 0 else (tie(k0, *tokens), k1)
            elif self.stage <= 3 + len(far_bits):
                self.sent = [tie(self.sent[0], *tokens), *self.sent[1:]]

    class Small:
        def __init__(self, total):
            self.total, self.flying, self.done = total, None, False
            self.hops = [core, over_z, over_y, over_x, *[swap("dp", bit) for bit in far_bits]]

        def hold(self, tokens):
            pass

        def sends(self):
            if self.flying is not None:
                self.total = self.sent[0] + self.flying[0]
            self.done = not self.hops
            return [] if self.done else [self.total]

        def fly(self):
            self.flying = [self.hops.pop(0)(self.sent[0])]

    rounds = []

    def advance(items, *tokens):
        rounds.append([])
        tokens = [*tokens, *(rounds.pop(0) if len(rounds) > 2 else [])]
        items = [item for item in items if not item.done]
        if tokens:
            for item in items:
                item.hold(tokens)
        plans = [item.sends() for item in items]
        flat = lax.optimization_barrier((*[array for arrays in plans for array in arrays], *tokens))
        sent, at = list(flat[len(flat) - len(tokens) :]), 0
        for item, arrays in zip(items, plans):
            item.sent = list(flat[at : at + len(arrays)])
            at += len(arrays)
            if arrays:
                item.fly()
                sent = [*sent, item.sent[0]]
        return sent

    joint, probs, ctx = front([])
    w_first = [whole, near, xh, yh, core(xh), core(tie(yh, ctx))]

    wide = shape(tokens, n_fs * third)
    full = shape(tokens, width, dtype=F32)
    weights = [pltpu.VMEM((width, n_fs * third), BF16), pltpu.VMEM((n_fs * third, width), BF16)]

    def grads(act, pull, deps):
        ends = call(
            lambda *refs: mlp_grad_kernel(len(deps), *refs),
            [shape(4, width // 2, third)] * 4,
            [act, pull, gt, h2t],
            deps=deps,
            us=4,
        )
        return ends

    def mlp(chunk, out_sum, dh, deps):
        return call(
            lambda *refs: mlp_kernel(chunk, len(deps), *refs),
            [wide, wide, full, full],
            [g, hn2, out_sum, dh],
            [*w_rest, fars[chunk - 1]],
            deps,
            [*weights, dma(28)],
            us=7,
        )

    act, pull, out_sum, dh, hn2, h2t, x1 = call(
        lambda *refs: mlp_kernel(0, 0, *refs),
        [wide, wide, full, full, shape(tokens, width), shape(width, tokens), full],
        [g, ctx, x, vecs],
        w_first,
        scratch=[*weights, pltpu.VMEM((width, width), BF16), dma(80)],
        us=11,
    )
    part = 2 * width
    far = tie(w_rest[2][:part], x1)
    fars = [core(far)]
    m0 = Chunk(*grads(act, pull, [far]))
    act, pull, out_sum, dh = mlp(1, out_sum, dh, [])
    fars.append(core(tie(w_rest[2][part:], dh)))
    m1 = Chunk(*grads(act, pull, advance([m0])))
    act, pull, out_sum, dh = mlp(2, out_sum, dh, advance([m0]))
    ends = grads(act, pull, [*advance([m1]), *advance([m0], dh)])
    deps = advance([m1, m0])
    result, dx1, dctx, *ends, dvec2 = call(
        lambda *refs: middle_kernel(len(deps), *refs),
        [
            shape(tokens, width),
            shape(tokens, width, dtype=F32),
            shape(tokens, width),
            *[shape(4, width // 2 + 3 * eighth, third)] * 4,
            shape(8, width, dtype=F32),
        ],
        [x1, out_sum, dh, g, vecs, ctx, *ends],
        w_first,
        deps,
        [pltpu.VMEM((width, width), BF16), pltpu.VMEM((tokens, width), BF16), pltpu.VMEM((width, tokens), BF16), dma(24)],
        us=5,
    )

    m2 = Chunk(*ends)

    def images_of(array):
        return array.reshape(count, seq, width)[:, :length]

    output = images_of(result)

    def back(first, quads, prior, deps):
        sets, specs = [], []
        for quad in range(first, first + quads):
            sets += [joint, joint, joint, probs, dctx]
            specs += [pl.BlockSpec((long, 256), lambda i, c=kind * (width // 256) + quad: (0, c)) for kind in range(3)]
            specs += [
                pl.BlockSpec((count, 1, 4 * seq, window), lambda i, quad=quad: (0, quad, 0, 0)),
                pl.BlockSpec((tokens, 256), lambda i, quad=quad: (0, quad)),
            ]
        size = eighth * (first + quads)
        return pl.pallas_call(
            lambda *refs: back_kernel(quads, first, len(deps), *refs),
            grid=(1,),
            out_shape=[shape(4, size, width)] * 4 + [shape(tokens, width)] * quads,
            in_specs=[vmem(), *specs, *[vmem()] * len(prior), *[anywhere()] * len(deps)],
            out_specs=[vmem()] * (4 + quads),
            compiler_params=pltpu.CompilerParams(vmem_limit_bytes=LIMIT),
            cost_estimate=cost(5 * quads * FLOPS, 0),
        )(h1t, *sets, *prior, *deps)

    *ends, dj0, dj1 = back(0, 2, [], advance([m2]))
    *ends, dj2 = back(2, 1, ends, advance([m2, m1, m0], dj0))
    jj = Chunk(*ends)
    deps = [*advance([jj]), *advance([m1, m0], dj0)]
    grad_x, dvec1 = call(
        lambda *refs: last_kernel(len(deps), *refs),
        [shape(tokens, width, dtype=F32), shape(8, width, dtype=F32)],
        [dj0, dj1, dj2, x, dx1, vecs],
        w_joint,
        deps,
        [pltpu.VMEM((width, 3 * width), BF16), pltpu.VMEM((tokens, width), F32), dma(6)],
    )
    small = Small(jnp.concatenate([dvec1[0:2], dvec2[0:2]], axis=0))
    grad_images = images_of(grad_x)
    advance([m2, m1, m0], dvec1)
    advance([jj, m2, m1, small])
    advance([jj, m2, m1, m0, small])
    items = [jj, m2, m1, m0, small]
    while any(not item.done for item in items):
        advance(items)
    mine = lax.dynamic_slice_in_dim(small.total, me * (width // n_fs), width // n_fs, 1)

    grad_up, grad_down, grad_out = call(
        mlp_end_kernel,
        [shape(width // n_fs, ff, dtype=F32), shape(fourth, width, dtype=F32), shape(width // n_fs, width, dtype=F32)],
        [*m0.parts, *m1.parts, *m2.parts],
        scratch=[pltpu.VMEM((width, third), F32)],
        us=3,
    )
    (grad_joint,) = call(rows_end_kernel, [shape(width // n_fs, 3 * width, dtype=F32)], jj.parts)
    return (
        output,
        grad_images,
        mine[0],
        mine[1],
        grad_joint,
        grad_out,
        mine[2],
        mine[3],
        grad_up,
        grad_down,
    )


def solution(mesh):
    rows = P("fsdp", None)
    tokens = P(("dp", "fsdp"), None, None)
    one = P("fsdp")
    return jax.shard_map(
        on_device,
        mesh=mesh,
        in_specs=(tokens, one, one, rows, rows, one, one, rows, rows, P(("dp", "fsdp"), None), tokens),
        out_specs=(tokens, tokens, one, one, rows, rows, one, one, rows, rows),
        check_vma=False,
    )
```

```python
import jax
import jax.numpy as jnp
from jax import lax
from jax.experimental import pallas as pl
from jax.experimental.pallas import tpu as pltpu
from jax.sharding import PartitionSpec as P

HEADS = 12
EPS = 1e-06
MASKED = -1e30
F32 = jnp.float32
BF16 = jnp.bfloat16
VM = pltpu.VMEM
ANY = pl.ANY
LIMIT = 12 * 1024 * 1024
FLOPS = int(1.15e9 * 0.3)


def vmem():
    return pl.BlockSpec(memory_space=VM)


def anywhere():
    return pl.BlockSpec(memory_space=ANY)


def in_hbm():
    return pl.BlockSpec(memory_space=pltpu.HBM)


def up_to(value, step):
    return (value + step - 1) // step * step


def dot(a, b):
    return jnp.dot(a, b, preferred_element_type=F32)


def dot_bt(a, b):
    return lax.dot_general(a, b, (((1,), (1,)), ((), ())), preferred_element_type=F32)


def dot_at(a, b):
    return lax.dot_general(a, b, (((0,), (0,)), ((), ())), preferred_element_type=F32)


def place():
    me = lax.axis_index("fsdp")
    dp = lax.axis_index("dp")
    return me, dp & 1, (dp >> 1) & 1


def start(table, sems, base=0):
    copies = []
    for index, (source, first, count, dest, at, col) in enumerate(table):
        src = source if count == source.shape[0] else source.at[pl.ds(pl.multiple_of(first, 16), count)]
        where = pl.ds(pl.multiple_of(at, 16), count)
        into = dest.at[where] if col is None else dest.at[where, col : col + source.shape[1]]
        copy = pltpu.make_async_copy(src, into, sems.at[base + index])
        copy.start()
        copies.append(copy)
    return copies


def cost(flops, moved):
    return pl.CostEstimate(flops=flops, bytes_accessed=moved, transcendentals=0)


def shard_rows(pieces, dest, me, y):
    rows = pieces[0].shape[0]
    half = rows // 2
    starts = (
        me * rows,
        (me ^ 1) * rows,
        (me ^ 2) * rows + y * half,
        (me ^ 2) * rows + (1 - y) * half,
        (me ^ 3) * rows + y * half,
        (me ^ 3) * rows + (1 - y) * half,
    )
    return [(piece, 0, piece.shape[0], dest, at, None) for piece, at in zip(pieces, starts)]


def packed_rows(pieces, dests, me, y, width, chunk=0):
    rows = width // 4
    n_halves = 2 if len(pieces) == 6 else 1
    owners = ((0, (0, 1)), (1, (0, 1)), (2, (y,)), (2, (1 - y,)), (3, (y,)), (3, (1 - y,)))
    if n_halves == 1:
        owners = tuple((rel, (0,)) for rel in range(4))
    tables = ([], [], [])
    for piece, (rel, halves) in zip(pieces, owners):
        size = piece.shape[0] // len(halves)
        for index, half in enumerate(halves):
            first = index * size if len(halves) > 1 or piece.shape[0] < 4 * width else chunk * 2 * width
            for table, dest, blocks, count, at in (
                (tables[0], dests[0], 4, rows // n_halves, (me ^ rel) * rows),
                (tables[1], dests[1], 3, 256 // n_halves, (0, 2, 1, 3)[rel] * 256),
                (tables[2], dests[2], 3, rows // n_halves, (me ^ rel) * rows),
            ):
                for block in range(blocks):
                    table.append((piece, first, count, dest, at + half * count, block * 256))
                    first = first + count
    return tables


def pack_kernel(up_ref, down_ref, out_ref, whole_ref, half_ref, rest_ref, sems):
    me, y, z = place()
    rows, third = up_ref.shape[0], down_ref.shape[0] // 3
    copies = []

    def put(source, first, count, col, dest, at):
        copy = pltpu.make_async_copy(
            source.at[pl.ds(pl.multiple_of(first, 16), count), col : col + third],
            dest.at[pl.ds(at, count)],
            sems.at[len(copies)],
        )
        copy.start()
        copies.append(copy)

    for dest, halves in ((half_ref, (y,)), (whole_ref, (0, 1))):
        at = 0
        for half in halves:
            for source, first, count, cols in (
                (up_ref, 0, rows // 2, [owner * 3 * third for owner in range(4)]),
                (down_ref, 0, third // 2, [block * third for block in range(3)]),
                (out_ref, 0, rows // 2, [block * third for block in range(3)]),
            ):
                for col in cols:
                    put(source, first + half * count, count, col, dest, at)
                    at += count
    at = 0
    for chunk in (1, 2):
        for owner in range(4):
            put(up_ref, 0, rows, (owner * 3 + chunk) * third, rest_ref, at)
            at += rows
        for block in range(3):
            put(down_ref, chunk * third, third, block * third, rest_ref, at)
            at += third
    for copy in copies:
        copy.wait()


def standardize(value):
    mean = jnp.mean(value, axis=-1, keepdims=True)
    center = value - mean
    spread = jnp.mean(center * center, axis=-1, keepdims=True)
    factor = lax.rsqrt(spread + EPS)
    return center * factor, factor


def norm_back(upstream, normal, factor):
    first = jnp.mean(upstream, axis=-1, keepdims=True)
    second = jnp.mean(upstream * normal, axis=-1, keepdims=True)
    return factor * (upstream - first - normal * second)


def owner_rows(turned, dest, me, y, z):
    piece = turned.shape[0] // 16
    for block in range(16):
        owner, yb, zb = block // 4, (block // 2) % 2, block % 2
        rel = owner ^ me
        at = (rel & 1) * 8 + (rel >> 1) * 4 + (yb ^ y) * 2 + (zb ^ z)
        where = pl.ds(pl.multiple_of(at * piece, piece), piece)
        dest[where, :] = turned[block * piece : (block + 1) * piece, :]


def quarter_rows(turned, dest, y, z):
    piece = turned.shape[0] // 4
    for block in range(4):
        yb, zb = block // 2, block % 2
        at = (yb ^ y) * 2 + (zb ^ z)
        where = pl.ds(pl.multiple_of(at * piece, piece), piece)
        dest[where, :] = turned[block * piece : (block + 1) * piece, :]


def row_loop(tokens, step):
    return pl.loop(0, tokens // step)


def first_norm_kernel(x_ref, vec_ref, hn_ref):
    gain, shift = vec_ref[0:1, :], vec_ref[1:2, :]

    @row_loop(x_ref.shape[0], 208)
    def _(i):
        rows = pl.ds(pl.multiple_of(i * 208, 16), 208)
        normal, factor = standardize(x_ref[rows, :].astype(F32))
        hn_ref[rows, :] = (normal * gain + shift).astype(BF16)


def turn_kernel(hn_ref, g_ref, h1t_ref, gt_ref):
    me, y, z = place()
    owner_rows(hn_ref[...].T, h1t_ref, me, y, z)
    quarter_rows(g_ref[...].T, gt_ref, y, z)


def head_masks():
    lane = lax.broadcasted_iota(jnp.int32, (1, 256), 1) // 64
    return [lane == h for h in range(4)]


def stack(value, masks):
    return jnp.concatenate([value * mask.astype(BF16) for mask in masks], axis=0)


def pick(value, masks):
    seq = value.shape[0] // 4
    total = jnp.where(masks[0], value[0:seq], 0.0)
    for h in range(1, 4):
        total = jnp.where(masks[h], value[h * seq : (h + 1) * seq], total)
    return total


def front_kernel(deps, hn_ref, mask_ref, *refs):
    pieces, (joint_ref, p_ref, ctx_ref, w_s, joint_s, sems, out_sem) = refs[:6], refs[6 + deps :]
    me, y, z = place()
    step = pl.program_id(0)
    tokens, width = hn_ref.shape
    seq, window = ctx_ref.shape[0], mask_ref.shape[2]

    @pl.when(step == 0)
    def _():
        copies = start(shard_rows(pieces, w_s, me, y), sems)
        joint_s[tokens:, :] = jnp.zeros((joint_s.shape[0] - tokens, 3 * width), BF16)
        for copy in copies:
            copy.wait()

        @pl.loop(0, 3 * width // 256)
        def _(n):
            cols = pl.ds(pl.multiple_of(n * 256, 256), 256)
            scale = jnp.where(n < width // 256, 0.125, 1.0).astype(BF16)
            value = dot(hn_ref[...], w_s[:, cols])
            joint_s[0:tokens, cols] = value.astype(BF16) * scale

        pltpu.make_async_copy(joint_s, joint_ref, out_sem).start()

    @pl.when(step > 0)
    def _():
        image = step - 1
        base = pl.multiple_of(image * seq, 16)
        rows, keys = pl.ds(base, seq), pl.ds(base, window)
        live = mask_ref[image]
        masks = head_masks()
        for quad in range(width // 256):
            at = quad * 256
            q = joint_s[rows, at : at + 256]
            k = joint_s[keys, width + at : width + at + 256]
            v = joint_s[keys, 2 * width + at : 2 * width + at + 256]
            s = dot_bt(stack(q, masks), k)
            s = jnp.where(live > 0.5, s, MASKED)
            e = jnp.exp(s - jnp.max(s, axis=-1, keepdims=True))
            p = (e * (1.0 / jnp.sum(e, axis=-1, keepdims=True))).astype(BF16)
            p_ref[0, quad] = p
            ctx_ref[:, at : at + 256] = pick(dot(p, v), masks).astype(BF16)

    @pl.when(step == pl.num_programs(0) - 1)
    def _():
        pltpu.make_async_copy(joint_s, joint_ref, out_sem).wait()


def gelu_both(u):
    phi = 0.5 + 0.5 * lax.erf(u * 0.7071067811865476)
    bell = jnp.exp(-0.5 * (u * u)) * 0.3989422804014327
    return u * phi, phi + u * bell


def mlp_kernel(chunk, deps, g_ref, *refs):
    me, y, z = place()
    first = chunk == 0
    if first:
        (ctx_ref, x_ref, vec_ref), refs = refs[:3], refs[3:]
        pieces, refs = refs[:6], refs[6 + deps :]
        act_ref, pull_ref, out_ref, dh_ref, hn_ref, ht_ref, x1_ref, wu_s, wd_s, wo_s, sems = refs
        width = ctx_ref.shape[1]
        ups, downs, outs = packed_rows(pieces, (wu_s, wd_s, wo_s), me, y, width)
        early = start(outs, sems)
        late = start(ups + downs, sems, len(outs))
    else:
        (hn_ref, out_in, dh_in), refs = refs[:3], refs[3:]
        pieces, refs = refs[:4], refs[4 + deps :]
        act_ref, pull_ref, out_ref, dh_ref, wu_s, wd_s, sems = refs
        width = hn_ref.shape[1]
        ups, downs, _ = packed_rows(pieces, (wu_s, wd_s, None), me, y, width, chunk - 1)
        early, late = [], start(ups + downs, sems)
    rows = wd_s.shape[0] // 4
    for copy in early:
        copy.wait()
    if first:
        gain, shift = vec_ref[2:3, :], vec_ref[3:4, :]

        @row_loop(ctx_ref.shape[0], 208)
        def _(i):
            part = pl.ds(pl.multiple_of(i * 208, 16), 208)
            middle = x_ref[part, :].astype(F32) + dot(ctx_ref[part, :], wo_s[...])
            x1_ref[part, :] = middle
            normal, factor = standardize(middle)
            hn_ref[part, :] = (normal * gain + shift).astype(BF16)

        owner_rows(hn_ref[...].T, ht_ref, me, y, z)
    for copy in late:
        copy.wait()
    for c in range(2):
        cols = []
        both = slice(2 * c * rows, 2 * (c + 1) * rows)
        for x in range(2):
            owner = me ^ (c + 2 * x)
            col = pl.ds(pl.multiple_of(owner * rows, rows), rows)
            act, slope = gelu_both(dot(hn_ref[...], wu_s[:, col]))
            at = (2 * c + x) * rows
            act_ref[:, at : at + rows] = act.astype(BF16)
            pull_ref[:, at : at + rows] = (dot_bt(g_ref[...], wd_s[at : at + rows, :]) * slope).astype(BF16)
            cols.append(col)
        plus = dot(act_ref[:, both], wd_s[both, :])
        wu = jnp.concatenate([wu_s[:, col] for col in cols], axis=1)
        back = dot_bt(pull_ref[:, both], wu)
        if c == 0 and first:
            out_ref[...] = plus
            dh_ref[...] = back
        elif c == 0:
            out_ref[...] = out_in[...] + plus
            dh_ref[...] = dh_in[...] + back
        else:
            out_ref[...] += plus
            dh_ref[...] += back


def mlp_grad_kernel(deps, act_ref, pull_ref, gt_ref, ht_ref, *refs):
    k0, k1, s0, s1 = refs[deps:]
    me, y, z = place()
    keep, send = (k0, k1), (s0, s1)
    width = gt_ref.shape[0]
    rows = act_ref.shape[1] // 4
    quarter = width // 4
    eighth = width // 16
    for c in range(2):
        for x in range(2):
            owner = me ^ (c + 2 * x)
            cols = slice((2 * c + x) * rows, (2 * c + x + 1) * rows)
            gd = dot(gt_ref[...], act_ref[:, cols]).astype(BF16)
            dest = (send if c else keep)[x]
            for part in range(4):
                dest[part, 0:quarter, :] = gd[part * quarter : (part + 1) * quarter, :]
            gu = dot(ht_ref[...], pull_ref[:, cols]).astype(BF16)
            where = pl.ds(pl.multiple_of(quarter + owner * eighth, eighth), eighth)
            for block in range(16):
                dest = (send if block // 8 else keep)[(block // 4) % 2]
                dest[block % 4, where, :] = gu[block * eighth : (block + 1) * eighth, :]


def middle_kernel(deps, x1_ref, out_in, dh_in, g_ref, vec_ref, ctx_ref, *refs):
    before, refs = refs[:4], refs[4:]
    pieces, refs = refs[:6], refs[6 + deps :]
    result_ref, dx_ref, dctx_ref, k0, k1, s0, s1, dvec_ref, w_s, dy_s, ct_s, sems = refs
    me, y, z = place()
    tokens, width = ctx_ref.shape
    copies = start(packed_rows(pieces, (None, None, w_s), me, y, width)[2], sems)
    gain = vec_ref[2:3, :]
    dvec_ref[...] = jnp.zeros_like(dvec_ref)

    @row_loop(tokens, 208)
    def _(i):
        rows = pl.ds(pl.multiple_of(i * 208, 16), 208)
        middle = x1_ref[rows, :]
        result_ref[rows, :] = (middle + out_in[rows, :]).astype(BF16)
        normal, factor = standardize(middle)
        pull = dh_in[rows, :]
        dvec_ref[0:1, :] += jnp.sum(pull * normal, axis=0, keepdims=True)
        dvec_ref[1:2, :] += jnp.sum(pull, axis=0, keepdims=True)
        dx = g_ref[rows, :].astype(F32) + norm_back(pull * gain, normal, factor)
        dx_ref[rows, :] = dx
        dy_s[rows, :] = dx.astype(BF16)

    owner_rows(ctx_ref[...].T, ct_s, me, y, z)
    for copy in copies:
        copy.wait()
    dctx_ref[...] = dot_bt(dy_s[...], w_s[...]).astype(BF16)
    value = dot(ct_s[...], dy_s[...]).astype(BF16)
    piece = width // 16
    base = before[0].shape[1]
    for old, new in zip(before, (k0, k1, s0, s1)):
        new[:, 0:base, :] = old[...]
    for block in range(16):
        dest = ((s0, s1) if block // 8 else (k0, k1))[(block // 4) % 2]
        for cols in range(width // 256):
            at = base + cols * piece
            dest[block % 4, at : at + piece, :] = value[block * piece : (block + 1) * piece, cols * 256 : cols * 256 + 256]


def store_blocks(value, keep, send, at=0):
    piece = value.shape[0] // 16
    for block in range(16):
        dest = (send if block // 8 else keep)[(block // 4) % 2]
        dest[block % 4, at : at + piece, :] = value[block * piece : (block + 1) * piece, :]


def back_kernel(quads, prior, deps, ht_ref, *refs):
    parts, refs = refs[: 5 * quads], refs[5 * quads :]
    if prior:
        before, refs = refs[:4], refs[4:]
    refs = refs[deps:]
    ends, djs = refs[:4], refs[4:]
    masks = head_masks()
    piece = ht_ref.shape[0] // 16
    if prior:
        for old, new in zip(before, ends):
            new[:, 0 : old.shape[1], :] = old[...]
    for quad in range(quads):
        joint_q, joint_k, joint_v, p_ref, dctx_ref = parts[5 * quad : 5 * quad + 5]
        dj_ref = djs[quad]
        images, _, stacked, window = p_ref.shape
        seq = stacked // 4

        @pl.loop(0, images)
        def _(b):
            base = pl.multiple_of(b * seq, 16)
            rows, keys = pl.ds(base, seq), pl.ds(base, window)
            q, k, v = joint_q[rows, :], joint_k[keys, :], joint_v[keys, :]
            p = p_ref[b, 0]
            dm, qm = stack(dctx_ref[rows, :], masks), stack(q, masks)
            pf = p.astype(F32)
            prod = pf * dot_bt(dm, v)
            ds = (prod - pf * jnp.sum(prod, axis=-1, keepdims=True)).astype(BF16)
            dj_ref[rows, 0:256] = (pick(dot(ds, k), masks) * 0.125).astype(BF16)
            dj_ref[rows, 256:512] = dot_at(ds, qm)[0:seq, :].astype(BF16)
            dj_ref[rows, 512:768] = dot_at(p, dm)[0:seq, :].astype(BF16)

        grad = dot(ht_ref[...], dj_ref[...]).astype(BF16)
        store_blocks(grad, ends[:2], ends[2:], piece * (quad + prior))


def last_kernel(deps, dj0, dj1, dj2, x_ref, dx_ref, vec_ref, *refs):
    pieces, (out_ref, dvec_ref, w_s, dh_s, sems) = refs[:6], refs[6 + deps :]
    me, y, z = place()
    copies = start(shard_rows(pieces, w_s, me, y), sems)
    gain = vec_ref[0:1, :]
    dvec_ref[...] = jnp.zeros_like(dvec_ref)
    tokens, width = x_ref.shape
    for copy in copies:
        copy.wait()
    pull = jnp.concatenate(
        [dj[:, kind * 256 : kind * 256 + 256] for kind in range(3) for dj in (dj0, dj1, dj2)], axis=1
    )
    dh_s[...] = dot_bt(pull, w_s[...])

    length, count, _ = out_ref.shape
    seq = tokens // count
    for image in range(count):
        rows = slice(image * seq, (image + 1) * seq)
        normal, factor = standardize(x_ref[rows, :].astype(F32))
        pull = dh_s[rows, :]
        dvec_ref[0:1, :] += jnp.sum(pull * normal, axis=0, keepdims=True)
        dvec_ref[1:2, :] += jnp.sum(pull, axis=0, keepdims=True)
        total = dx_ref[rows, :] + norm_back(pull * gain, normal, factor)
        out_ref[:, image, :] = total[0:length, :]


def mlp_end_kernel(*refs):
    parts, (up_ref, down_ref, out_ref, turn_s) = refs[:12], refs[12:]
    me, y, z = place()
    rows, lanes = parts[0].shape
    half = rows // 2
    eighth = half // 4
    for chunk in range(3):
        for rel in range(4):
            piece = parts[chunk * 4 + rel]
            at = ((rel // 2) ^ y) * 2 + ((rel % 2) ^ z)
            where = pl.ds(pl.multiple_of(at * half, half), half)
            turn_s[where, :] = piece[0:half, :].astype(F32)
            where = pl.ds(pl.multiple_of(at * eighth, eighth), eighth)
            for owner in range(4):
                col = (owner * 3 + chunk) * lanes
                up_ref[where, col : col + lanes] = piece[half + owner * eighth : half + (owner + 1) * eighth, :].astype(F32)
            if chunk == 2:
                for block in range(3):
                    first = rows + block * eighth
                    col = block * lanes
                    out_ref[where, col : col + lanes] = piece[first : first + eighth, :].astype(F32)
        down_ref[chunk * lanes : (chunk + 1) * lanes, :] = turn_s[...].T


def rows_end_kernel(*refs):
    parts, joint_ref = refs[:4], refs[4]
    me, y, z = place()
    width = parts[0].shape[1]
    third = width // 3
    piece = parts[0].shape[0] // 3
    for rel in range(4):
        at = ((rel // 2) ^ y) * 2 + ((rel % 2) ^ z)
        where = pl.ds(pl.multiple_of(at * piece, piece), piece)
        for quad in range(3):
            block = parts[rel][quad * piece : (quad + 1) * piece, :].astype(F32)
            for kind in range(3):
                col = kind * width + quad * third
                joint_ref[where, col : col + third] = block[:, kind * third : (kind + 1) * third]


def on_device(
    images,
    first_gain,
    first_shift,
    joint_weight,
    out_weight,
    second_gain,
    second_shift,
    up_weight,
    down_weight,
    keep_flags,
    cotangent,
):
    count, length, width = images.shape
    n_dp = lax.axis_size("dp")
    n_fs = lax.axis_size("fsdp")
    me = lax.axis_index("fsdp")
    y = lax.axis_index("dp") & 1
    seq = up_to(length, 16)
    window = up_to(seq, 256)
    tokens = count * seq
    long = tokens + window - seq
    ff = up_weight.shape[1]
    fourth = ff // n_fs
    third = fourth // 3
    eighth = width // 16

    def swap(axis, bit):
        n = n_dp if axis == "dp" else n_fs
        return lambda v: lax.ppermute(v, axis, [(i, i ^ bit) for i in range(n)])

    core, over_x, over_y, over_z = swap("fsdp", 1), swap("fsdp", 2), swap("dp", 1), swap("dp", 2)

    def call(body, outs, dense, pieces=(), deps=(), scratch=(), outside=False, us=1):
        args = [*dense, *pieces, *deps]
        return pl.pallas_call(
            body,
            out_shape=outs,
            in_specs=[vmem()] * len(dense) + [in_hbm()] * len(pieces) + [anywhere()] * len(deps),
            out_specs=[in_hbm() if outside else vmem()] * len(outs),
            scratch_shapes=list(scratch),
            compiler_params=pltpu.CompilerParams(vmem_limit_bytes=LIMIT),
            cost_estimate=cost(us * FLOPS, 0),
        )(*args)

    def shape(*dims, dtype=BF16):
        return jax.ShapeDtypeStruct(dims, dtype)

    def dma(n):
        return pltpu.SemaphoreType.DMA((n,))

    def tie(value, *tokens):
        return lax.optimization_barrier((value, *tokens))[0]

    half = joint_weight.shape[0] // 2
    xh_joint = over_x(lax.dynamic_slice_in_dim(joint_weight, y * half, half, 0))

    vec = jnp.concatenate([first_gain, first_shift, second_gain, second_shift])
    other = over_x(vec)
    both = jnp.stack([vec, core(vec), other, core(other)])
    both = both.reshape(n_fs, 4, -1)
    vecs = jnp.concatenate([lax.dynamic_index_in_dim(both, me ^ i, 0, False) for i in range(n_fs)], axis=1)
    vecs = jnp.pad(vecs.astype(F32), ((0, 4), (0, 0)))

    packed = (4 * (width // n_fs) + 3 * third, 3 * (width // n_fs))
    whole, mine, rest = call(
        pack_kernel,
        [shape(sum(packed), third), shape(sum(packed) // 2, third), shape(2 * packed[0], third)],
        [],
        [up_weight, down_weight, out_weight],
        scratch=[dma(44)],
        outside=True,
    )
    yh_joint = over_y(tie(xh_joint, mine, whole))
    w_joint = [joint_weight, core(joint_weight), xh_joint, yh_joint, core(xh_joint), core(yh_joint)]
    near = core(whole)
    xh = over_x(tie(mine, xh_joint, other))
    yh = over_y(xh)
    w_rest = [rest, core(rest), over_x(tie(rest, w_joint[3], vecs))]

    pads = ((0, 0), (0, seq - length), (0, 0))
    x = jnp.pad(images, pads).reshape(tokens, width)
    g = jnp.pad(cotangent, pads).reshape(tokens, width)
    live = jnp.pad(keep_flags, ((0, 0), (0, window - length))).astype(F32).reshape(count, 1, window)

    (hn1,) = call(first_norm_kernel, [shape(tokens, width)], [x, vecs])
    h1t, gt = call(turn_kernel, [shape(width, tokens), shape(width, tokens)], [hn1, g])

    def front(deps):
        prior = lambda i: jnp.maximum(i - 1, 0)
        return pl.pallas_call(
            lambda *refs: front_kernel(len(deps), *refs),
            grid=(1 + count,),
            out_shape=[pltpu.HBM((long, 3 * width), BF16), pltpu.HBM((count, 3, 4 * seq, window), BF16), shape(tokens, width)],
            in_specs=[
                pl.BlockSpec((tokens, width), lambda i: (0, 0)),
                pl.BlockSpec((count, 1, window), lambda i: (0, 0, 0)),
                *[in_hbm()] * 6,
                *[anywhere()] * len(deps),
            ],
            out_specs=[
                anywhere(),
                pl.BlockSpec((1, 3, 4 * seq, window), lambda i: (prior(i), 0, 0, 0)),
                pl.BlockSpec((seq, width), lambda i: (prior(i), 0)),
            ],
            scratch_shapes=[
                pltpu.VMEM((width, 3 * width), BF16),
                pltpu.VMEM((long, 3 * width), BF16),
                dma(6),
                pltpu.SemaphoreType.DMA,
            ],
            compiler_params=pltpu.CompilerParams(vmem_limit_bytes=LIMIT),
            cost_estimate=cost(14 * FLOPS, 0),
        )(hn1, live, *w_joint, *deps)

    def plus(*terms):
        total = terms[0].astype(F32)
        for term in terms[1:]:
            total = total + term.astype(F32)
        return total.astype(BF16)

    far_bits = [1 << bit for bit in range(2, n_dp.bit_length() - 1)]

    class Chunk:
        def __init__(self, k0, k1, s0, s1):
            self.keeps, self.parts, self.stage = (k0, k1), [], 0
            self.hops = [[over_x], [over_y], [over_z], *[[swap("dp", bit)] for bit in far_bits], [over_z, over_y], [over_y], []]
            self.flying = [core(s0), core(s1)]

        def sends(self):
            k0, k1 = self.keeps
            got, self.stage = self.flying, self.stage + 1
            left = len(self.hops) - self.stage
            if self.stage == 1:
                self.near = got[0]
                return [plus(k1, got[1])]
            if self.stage == 2:
                self.rx = got[0]
                return [plus(k0[2:4], self.near[2:4], self.rx[2:4])]
            if self.stage == 3:
                self.ry = got[0]
                return [plus(k0[1], self.near[1], self.rx[1], self.ry[1])]
            if self.stage == 4:
                total = plus(k0[0], self.near[0], self.rx[0], self.ry[0], got[0])
                return [total] * (2 if left == 2 else 1)
            if left >= 2:
                return [plus(self.sent[0], got[0])] * (2 if left == 2 else 1)
            if left == 1:
                self.parts = [self.sent[0], *got]
                rounds[-1] += got[1:]
                return got[:1]
            self.parts = self.parts + got
            rounds[-1] += got
            return []

        def fly(self):
            self.flying = [hop(array) for array, hop in zip(self.sent, self.hops[self.stage - 1])]

        @property
        def done(self):
            return len(self.parts) == 4

        def hold(self, tokens):
            if self.stage <= 3:
                k0, k1 = self.keeps
                self.keeps = (tie(k0, *tokens), tie(k1, *tokens)) if self.stage == 0 else (tie(k0, *tokens), k1)
            elif self.stage <= 3 + len(far_bits):
                self.sent = [tie(self.sent[0], *tokens), *self.sent[1:]]

    class Small:
        def __init__(self, total):
            self.total, self.flying, self.done = total, None, False
            self.hops = [core, over_z, over_y, over_x, *[swap("dp", bit) for bit in far_bits]]

        def hold(self, tokens):
            pass

        def sends(self):
            if self.flying is not None:
                self.total = self.sent[0] + self.flying[0]
            self.done = not self.hops
            return [] if self.done else [self.total]

        def fly(self):
            self.flying = [self.hops.pop(0)(self.sent[0])]

    rounds = []

    def advance(items, *tokens):
        rounds.append([])
        tokens = [*tokens, *(rounds.pop(0) if len(rounds) > 2 else [])]
        items = [item for item in items if not item.done]
        if tokens:
            for item in items:
                item.hold(tokens)
        plans = [item.sends() for item in items]
        flat = lax.optimization_barrier((*[array for arrays in plans for array in arrays], *tokens))
        sent, at = list(flat[len(flat) - len(tokens) :]), 0
        for item, arrays in zip(items, plans):
            item.sent = list(flat[at : at + len(arrays)])
            at += len(arrays)
            if arrays:
                item.fly()
                sent = [*sent, item.sent[0]]
        return sent

    joint, probs, ctx = front([])
    w_first = [whole, near, xh, yh, core(xh), core(tie(yh, ctx))]

    wide = shape(tokens, n_fs * third)
    full = shape(tokens, width, dtype=F32)
    weights = [pltpu.VMEM((width, n_fs * third), BF16), pltpu.VMEM((n_fs * third, width), BF16)]

    def grads(act, pull, deps):
        ends = call(
            lambda *refs: mlp_grad_kernel(len(deps), *refs),
            [shape(4, width // 2, third)] * 4,
            [act, pull, gt, h2t],
            deps=deps,
            us=4,
        )
        return ends

    def mlp(chunk, out_sum, dh, deps):
        return call(
            lambda *refs: mlp_kernel(chunk, len(deps), *refs),
            [wide, wide, full, full],
            [g, hn2, out_sum, dh],
            [*w_rest, fars[chunk - 1]],
            deps,
            [*weights, dma(28)],
            us=7,
        )

    act, pull, out_sum, dh, hn2, h2t, x1 = call(
        lambda *refs: mlp_kernel(0, 0, *refs),
        [wide, wide, full, full, shape(tokens, width), shape(width, tokens), full],
        [g, ctx, x, vecs],
        w_first,
        scratch=[*weights, pltpu.VMEM((width, width), BF16), dma(80)],
        us=11,
    )
    part = 2 * width
    far = tie(w_rest[2][:part], x1)
    fars = [core(far)]
    m0 = Chunk(*grads(act, pull, [far]))
    act, pull, out_sum, dh = mlp(1, out_sum, dh, [])
    fars.append(core(tie(w_rest[2][part:], dh)))
    m1 = Chunk(*grads(act, pull, advance([m0])))
    act, pull, out_sum, dh = mlp(2, out_sum, dh, advance([m0]))
    ends = grads(act, pull, [*advance([m1]), *advance([m0], dh)])
    deps = advance([m1, m0])
    result, dx1, dctx, *ends, dvec2 = call(
        lambda *refs: middle_kernel(len(deps), *refs),
        [
            shape(tokens, width),
            shape(tokens, width, dtype=F32),
            shape(tokens, width),
            *[shape(4, width // 2 + 3 * eighth, third)] * 4,
            shape(8, width, dtype=F32),
        ],
        [x1, out_sum, dh, g, vecs, ctx, *ends],
        w_first,
        deps,
        [pltpu.VMEM((width, width), BF16), pltpu.VMEM((tokens, width), BF16), pltpu.VMEM((width, tokens), BF16), dma(24)],
        us=5,
    )

    m2 = Chunk(*ends)

    def images_of(array):
        return array.reshape(count, seq, width)[:, :length]

    output = images_of(result)

    def back(first, quads, prior, deps):
        sets, specs = [], []
        for quad in range(first, first + quads):
            sets += [joint, joint, joint, probs, dctx]
            specs += [pl.BlockSpec((long, 256), lambda i, c=kind * (width // 256) + quad: (0, c)) for kind in range(3)]
            specs += [
                pl.BlockSpec((count, 1, 4 * seq, window), lambda i, quad=quad: (0, quad, 0, 0)),
                pl.BlockSpec((tokens, 256), lambda i, quad=quad: (0, quad)),
            ]
        size = eighth * (first + quads)
        return pl.pallas_call(
            lambda *refs: back_kernel(quads, first, len(deps), *refs),
            grid=(1,),
            out_shape=[shape(4, size, width)] * 4 + [shape(tokens, width)] * quads,
            in_specs=[vmem(), *specs, *[vmem()] * len(prior), *[anywhere()] * len(deps)],
            out_specs=[vmem()] * (4 + quads),
            compiler_params=pltpu.CompilerParams(vmem_limit_bytes=LIMIT),
            cost_estimate=cost(5 * quads * FLOPS, 0),
        )(h1t, *sets, *prior, *deps)

    *ends, dj0, dj1 = back(0, 2, [], advance([m2]))
    *ends, dj2 = back(2, 1, ends, advance([m2, m1, m0], dj0))
    jj = Chunk(*ends)
    deps = [*advance([jj]), *advance([m1, m0], dj0)]
    grad_x, dvec1 = call(
        lambda *refs: last_kernel(len(deps), *refs),
        [shape(length, count, width, dtype=F32), shape(8, width, dtype=F32)],
        [dj0, dj1, dj2, x, dx1, vecs],
        w_joint,
        deps,
        [pltpu.VMEM((width, 3 * width), BF16), pltpu.VMEM((tokens, width), F32), dma(6)],
    )
    small = Small(jnp.concatenate([dvec1[0:2], dvec2[0:2]], axis=0))
    grad_images = jnp.transpose(grad_x, (1, 0, 2))
    advance([m2, m1, m0], dvec1)
    advance([jj, m2, m1, small])
    advance([jj, m2, m1, m0, small])
    items = [jj, m2, m1, m0, small]
    while any(not item.done for item in items):
        advance(items)
    mine = lax.dynamic_slice_in_dim(small.total, me * (width // n_fs), width // n_fs, 1)

    grad_up, grad_down, grad_out = call(
        mlp_end_kernel,
        [shape(width // n_fs, ff, dtype=F32), shape(fourth, width, dtype=F32), shape(width // n_fs, width, dtype=F32)],
        [*m0.parts, *m1.parts, *m2.parts],
        scratch=[pltpu.VMEM((width, third), F32)],
        us=3,
    )
    (grad_joint,) = call(rows_end_kernel, [shape(width // n_fs, 3 * width, dtype=F32)], jj.parts)
    return (
        output,
        grad_images,
        mine[0],
        mine[1],
        grad_joint,
        grad_out,
        mine[2],
        mine[3],
        grad_up,
        grad_down,
    )


def solution(mesh):
    rows = P("fsdp", None)
    tokens = P(("dp", "fsdp"), None, None)
    one = P("fsdp")
    return jax.shard_map(
        on_device,
        mesh=mesh,
        in_specs=(tokens, one, one, rows, rows, one, one, rows, rows, P(("dp", "fsdp"), None), tokens),
        out_specs=(tokens, tokens, one, one, rows, rows, one, one, rows, rows),
        check_vma=False,
    )
```

```python
import jax
import jax.numpy as jnp
from jax import lax
from jax.experimental import pallas as pl
from jax.experimental.pallas import tpu as pltpu
from jax.sharding import PartitionSpec as P

HEADS = 12
EPS = 1e-06
MASKED = -1e30
F32 = jnp.float32
BF16 = jnp.bfloat16
VM = pltpu.VMEM
ANY = pl.ANY
LIMIT = 12 * 1024 * 1024
FLOPS = int(1.15e9 * 0.3)


def vmem():
    return pl.BlockSpec(memory_space=VM)


def anywhere():
    return pl.BlockSpec(memory_space=ANY)


def in_hbm():
    return pl.BlockSpec(memory_space=pltpu.HBM)


def up_to(value, step):
    return (value + step - 1) // step * step


def dot(a, b):
    return jnp.dot(a, b, preferred_element_type=F32)


def dot_bt(a, b):
    return lax.dot_general(a, b, (((1,), (1,)), ((), ())), preferred_element_type=F32)


def dot_at(a, b):
    return lax.dot_general(a, b, (((0,), (0,)), ((), ())), preferred_element_type=F32)


def place():
    me = lax.axis_index("fsdp")
    dp = lax.axis_index("dp")
    return me, dp & 1, (dp >> 1) & 1


def start(table, sems, base=0):
    copies = []
    for index, (source, first, count, dest, at, col) in enumerate(table):
        src = source if count == source.shape[0] else source.at[pl.ds(pl.multiple_of(first, 16), count)]
        where = pl.ds(pl.multiple_of(at, 16), count)
        into = dest.at[where] if col is None else dest.at[where, col : col + source.shape[1]]
        copy = pltpu.make_async_copy(src, into, sems.at[base + index])
        copy.start()
        copies.append(copy)
    return copies


def cost(flops, moved):
    return pl.CostEstimate(flops=flops, bytes_accessed=moved, transcendentals=0)


def shard_rows(pieces, dest, me, y):
    rows = pieces[0].shape[0]
    half = rows // 2
    starts = (
        me * rows,
        (me ^ 1) * rows,
        (me ^ 2) * rows + y * half,
        (me ^ 2) * rows + (1 - y) * half,
        (me ^ 3) * rows + y * half,
        (me ^ 3) * rows + (1 - y) * half,
    )
    return [(piece, 0, piece.shape[0], dest, at, None) for piece, at in zip(pieces, starts)]


def packed_rows(pieces, dests, me, y, width, chunk=0):
    rows = width // 4
    n_halves = 2 if len(pieces) == 6 else 1
    owners = ((0, (0, 1)), (1, (0, 1)), (2, (y,)), (2, (1 - y,)), (3, (y,)), (3, (1 - y,)))
    if n_halves == 1:
        owners = tuple((rel, (0,)) for rel in range(4))
    tables = ([], [], [])
    for piece, (rel, halves) in zip(pieces, owners):
        size = piece.shape[0] // len(halves)
        for index, half in enumerate(halves):
            first = index * size if len(halves) > 1 or piece.shape[0] < 4 * width else chunk * 2 * width
            for table, dest, blocks, count, at in (
                (tables[0], dests[0], 4, rows // n_halves, (me ^ rel) * rows),
                (tables[1], dests[1], 3, 256 // n_halves, (0, 2, 1, 3)[rel] * 256),
                (tables[2], dests[2], 3, rows // n_halves, (me ^ rel) * rows),
            ):
                for block in range(blocks):
                    table.append((piece, first, count, dest, at + half * count, block * 256))
                    first = first + count
    return tables


def pack_kernel(up_ref, down_ref, out_ref, whole_ref, half_ref, rest_ref, sems):
    me, y, z = place()
    rows, third = up_ref.shape[0], down_ref.shape[0] // 3
    copies = []

    def put(source, first, count, col, dest, at):
        copy = pltpu.make_async_copy(
            source.at[pl.ds(pl.multiple_of(first, 16), count), col : col + third],
            dest.at[pl.ds(at, count)],
            sems.at[len(copies)],
        )
        copy.start()
        copies.append(copy)

    for dest, halves in ((half_ref, (y,)), (whole_ref, (0, 1))):
        at = 0
        for half in halves:
            for source, first, count, cols in (
                (up_ref, 0, rows // 2, [owner * 3 * third for owner in range(4)]),
                (down_ref, 0, third // 2, [block * third for block in range(3)]),
                (out_ref, 0, rows // 2, [block * third for block in range(3)]),
            ):
                for col in cols:
                    put(source, first + half * count, count, col, dest, at)
                    at += count
    at = 0
    for chunk in (1, 2):
        for owner in range(4):
            put(up_ref, 0, rows, (owner * 3 + chunk) * third, rest_ref, at)
            at += rows
        for block in range(3):
            put(down_ref, chunk * third, third, block * third, rest_ref, at)
            at += third
    for copy in copies:
        copy.wait()


def standardize(value):
    mean = jnp.mean(value, axis=-1, keepdims=True)
    center = value - mean
    spread = jnp.mean(center * center, axis=-1, keepdims=True)
    factor = lax.rsqrt(spread + EPS)
    return center * factor, factor


def norm_back(upstream, normal, factor):
    first = jnp.mean(upstream, axis=-1, keepdims=True)
    second = jnp.mean(upstream * normal, axis=-1, keepdims=True)
    return factor * (upstream - first - normal * second)


def owner_rows(turned, dest, me, y, z):
    piece = turned.shape[0] // 16
    for block in range(16):
        owner, yb, zb = block // 4, (block // 2) % 2, block % 2
        rel = owner ^ me
        at = (rel & 1) * 8 + (rel >> 1) * 4 + (yb ^ y) * 2 + (zb ^ z)
        where = pl.ds(pl.multiple_of(at * piece, piece), piece)
        dest[where, :] = turned[block * piece : (block + 1) * piece, :]


def quarter_rows(turned, dest, y, z):
    piece = turned.shape[0] // 4
    for block in range(4):
        yb, zb = block // 2, block % 2
        at = (yb ^ y) * 2 + (zb ^ z)
        where = pl.ds(pl.multiple_of(at * piece, piece), piece)
        dest[where, :] = turned[block * piece : (block + 1) * piece, :]


def row_loop(tokens, step):
    return pl.loop(0, tokens // step)


def first_norm_kernel(x_ref, vec_ref, hn_ref):
    gain, shift = vec_ref[0:1, :], vec_ref[1:2, :]

    @row_loop(x_ref.shape[0], 208)
    def _(i):
        rows = pl.ds(pl.multiple_of(i * 208, 16), 208)
        normal, factor = standardize(x_ref[rows, :].astype(F32))
        hn_ref[rows, :] = (normal * gain + shift).astype(BF16)


def turn_kernel(hn_ref, g_ref, h1t_ref, gt_ref):
    me, y, z = place()
    owner_rows(hn_ref[...].T, h1t_ref, me, y, z)
    quarter_rows(g_ref[...].T, gt_ref, y, z)


def head_masks():
    lane = lax.broadcasted_iota(jnp.int32, (1, 256), 1) // 64
    return [lane == h for h in range(4)]


def stack(value, masks):
    return jnp.concatenate([value * mask.astype(BF16) for mask in masks], axis=0)


def pick(value, masks):
    seq = value.shape[0] // 4
    total = jnp.where(masks[0], value[0:seq], 0.0)
    for h in range(1, 4):
        total = jnp.where(masks[h], value[h * seq : (h + 1) * seq], total)
    return total


def front_kernel(deps, hn_ref, mask_ref, *refs):
    pieces, (joint_ref, p_ref, ctx_ref, w_s, joint_s, sems, out_sem) = refs[:6], refs[6 + deps :]
    me, y, z = place()
    step = pl.program_id(0)
    tokens, width = hn_ref.shape
    seq, window = ctx_ref.shape[0], mask_ref.shape[2]

    @pl.when(step == 0)
    def _():
        copies = start(shard_rows(pieces, w_s, me, y), sems)
        joint_s[tokens:, :] = jnp.zeros((joint_s.shape[0] - tokens, 3 * width), BF16)
        for copy in copies:
            copy.wait()

        @pl.loop(0, 3 * width // 256)
        def _(n):
            cols = pl.ds(pl.multiple_of(n * 256, 256), 256)
            scale = jnp.where(n < width // 256, 0.125, 1.0).astype(BF16)
            value = dot(hn_ref[...], w_s[:, cols])
            joint_s[0:tokens, cols] = value.astype(BF16) * scale

        pltpu.make_async_copy(joint_s, joint_ref, out_sem).start()

    @pl.when(step > 0)
    def _():
        image = step - 1
        base = pl.multiple_of(image * seq, 16)
        rows, keys = pl.ds(base, seq), pl.ds(base, window)
        live = mask_ref[image]
        masks = head_masks()
        for quad in range(width // 256):
            at = quad * 256
            q = joint_s[rows, at : at + 256]
            k = joint_s[keys, width + at : width + at + 256]
            v = joint_s[keys, 2 * width + at : 2 * width + at + 256]
            s = dot_bt(stack(q, masks), k)
            s = jnp.where(live > 0.5, s, MASKED)
            e = jnp.exp(s - jnp.max(s, axis=-1, keepdims=True))
            p = (e * (1.0 / jnp.sum(e, axis=-1, keepdims=True))).astype(BF16)
            p_ref[0, quad] = p
            ctx_ref[:, at : at + 256] = pick(dot(p, v), masks).astype(BF16)

    @pl.when(step == pl.num_programs(0) - 1)
    def _():
        pltpu.make_async_copy(joint_s, joint_ref, out_sem).wait()


def gelu_both(u):
    phi = 0.5 + 0.5 * lax.erf(u * 0.7071067811865476)
    bell = jnp.exp(-0.5 * (u * u)) * 0.3989422804014327
    return u * phi, phi + u * bell


def mlp_kernel(chunk, deps, g_ref, *refs):
    me, y, z = place()
    first = chunk == 0
    if first:
        (ctx_ref, x_ref, vec_ref), refs = refs[:3], refs[3:]
        pieces, refs = refs[:6], refs[6 + deps :]
        act_ref, pull_ref, out_ref, dh_ref, hn_ref, ht_ref, x1_ref, wu_s, wd_s, wo_s, sems = refs
        width = ctx_ref.shape[1]
        ups, downs, outs = packed_rows(pieces, (wu_s, wd_s, wo_s), me, y, width)
        early = start(outs, sems)
        late = start(ups + downs, sems, len(outs))
    else:
        (hn_ref, out_in, dh_in), refs = refs[:3], refs[3:]
        pieces, refs = refs[:4], refs[4 + deps :]
        act_ref, pull_ref, out_ref, dh_ref, wu_s, wd_s, sems = refs
        width = hn_ref.shape[1]
        ups, downs, _ = packed_rows(pieces, (wu_s, wd_s, None), me, y, width, chunk - 1)
        early, late = [], start(ups + downs, sems)
    rows = wd_s.shape[0] // 4
    for copy in early:
        copy.wait()
    if first:
        gain, shift = vec_ref[2:3, :], vec_ref[3:4, :]

        @row_loop(ctx_ref.shape[0], 208)
        def _(i):
            part = pl.ds(pl.multiple_of(i * 208, 16), 208)
            middle = x_ref[part, :].astype(F32) + dot(ctx_ref[part, :], wo_s[...])
            x1_ref[part, :] = middle
            normal, factor = standardize(middle)
            hn_ref[part, :] = (normal * gain + shift).astype(BF16)

        owner_rows(hn_ref[...].T, ht_ref, me, y, z)
    for copy in late:
        copy.wait()
    for c in range(2):
        cols = []
        both = slice(2 * c * rows, 2 * (c + 1) * rows)
        for x in range(2):
            owner = me ^ (c + 2 * x)
            col = pl.ds(pl.multiple_of(owner * rows, rows), rows)
            act, slope = gelu_both(dot(hn_ref[...], wu_s[:, col]))
            at = (2 * c + x) * rows
            act_ref[:, at : at + rows] = act.astype(BF16)
            pull_ref[:, at : at + rows] = (dot_bt(g_ref[...], wd_s[at : at + rows, :]) * slope).astype(BF16)
            cols.append(col)
        plus = dot(act_ref[:, both], wd_s[both, :])
        wu = jnp.concatenate([wu_s[:, col] for col in cols], axis=1)
        back = dot_bt(pull_ref[:, both], wu)
        if c == 0 and first:
            out_ref[...] = plus
            dh_ref[...] = back
        elif c == 0:
            out_ref[...] = out_in[...] + plus
            dh_ref[...] = dh_in[...] + back
        else:
            out_ref[...] += plus
            dh_ref[...] += back


def mlp_grad_kernel(deps, act_ref, pull_ref, gt_ref, ht_ref, *refs):
    k0, k1, s0, s1 = refs[deps:]
    me, y, z = place()
    keep, send = (k0, k1), (s0, s1)
    width = gt_ref.shape[0]
    rows = act_ref.shape[1] // 4
    quarter = width // 4
    eighth = width // 16
    for c in range(2):
        for x in range(2):
            owner = me ^ (c + 2 * x)
            cols = slice((2 * c + x) * rows, (2 * c + x + 1) * rows)
            gd = dot(gt_ref[...], act_ref[:, cols]).astype(BF16)
            dest = (send if c else keep)[x]
            for part in range(4):
                dest[part, 0:quarter, :] = gd[part * quarter : (part + 1) * quarter, :]
            gu = dot(ht_ref[...], pull_ref[:, cols]).astype(BF16)
            where = pl.ds(pl.multiple_of(quarter + owner * eighth, eighth), eighth)
            for block in range(16):
                dest = (send if block // 8 else keep)[(block // 4) % 2]
                dest[block % 4, where, :] = gu[block * eighth : (block + 1) * eighth, :]


def middle_kernel(deps, x1_ref, out_in, dh_in, g_ref, vec_ref, ctx_ref, *refs):
    before, refs = refs[:4], refs[4:]
    pieces, refs = refs[:6], refs[6 + deps :]
    result_ref, dx_ref, dctx_ref, k0, k1, s0, s1, dvec_ref, w_s, dy_s, ct_s, sems = refs
    me, y, z = place()
    tokens, width = ctx_ref.shape
    copies = start(packed_rows(pieces, (None, None, w_s), me, y, width)[2], sems)
    gain = vec_ref[2:3, :]
    dvec_ref[...] = jnp.zeros_like(dvec_ref)

    @row_loop(tokens, 208)
    def _(i):
        rows = pl.ds(pl.multiple_of(i * 208, 16), 208)
        middle = x1_ref[rows, :]
        normal, factor = standardize(middle)
        pull = dh_in[rows, :]
        dvec_ref[0:1, :] += jnp.sum(pull * normal, axis=0, keepdims=True)
        dvec_ref[1:2, :] += jnp.sum(pull, axis=0, keepdims=True)
        dx = g_ref[rows, :].astype(F32) + norm_back(pull * gain, normal, factor)
        dx_ref[rows, :] = dx
        dy_s[rows, :] = dx.astype(BF16)

    length, count, _ = result_ref.shape
    seq = tokens // count
    for image in range(count):
        rows = slice(image * seq, image * seq + length)
        result_ref[:, image, :] = (x1_ref[rows, :] + out_in[rows, :]).astype(BF16)
    owner_rows(ctx_ref[...].T, ct_s, me, y, z)
    for copy in copies:
        copy.wait()
    dctx_ref[...] = dot_bt(dy_s[...], w_s[...]).astype(BF16)
    value = dot(ct_s[...], dy_s[...]).astype(BF16)
    piece = width // 16
    base = before[0].shape[1]
    for old, new in zip(before, (k0, k1, s0, s1)):
        new[:, 0:base, :] = old[...]
    for block in range(16):
        dest = ((s0, s1) if block // 8 else (k0, k1))[(block // 4) % 2]
        for cols in range(width // 256):
            at = base + cols * piece
            dest[block % 4, at : at + piece, :] = value[block * piece : (block + 1) * piece, cols * 256 : cols * 256 + 256]


def store_blocks(value, keep, send, at=0):
    piece = value.shape[0] // 16
    for block in range(16):
        dest = (send if block // 8 else keep)[(block // 4) % 2]
        dest[block % 4, at : at + piece, :] = value[block * piece : (block + 1) * piece, :]


def back_kernel(quads, prior, deps, ht_ref, *refs):
    parts, refs = refs[: 5 * quads], refs[5 * quads :]
    if prior:
        before, refs = refs[:4], refs[4:]
    refs = refs[deps:]
    ends, djs = refs[:4], refs[4:]
    masks = head_masks()
    piece = ht_ref.shape[0] // 16
    if prior:
        for old, new in zip(before, ends):
            new[:, 0 : old.shape[1], :] = old[...]
    for quad in range(quads):
        joint_q, joint_k, joint_v, p_ref, dctx_ref = parts[5 * quad : 5 * quad + 5]
        dj_ref = djs[quad]
        images, _, stacked, window = p_ref.shape
        seq = stacked // 4

        @pl.loop(0, images)
        def _(b):
            base = pl.multiple_of(b * seq, 16)
            rows, keys = pl.ds(base, seq), pl.ds(base, window)
            q, k, v = joint_q[rows, :], joint_k[keys, :], joint_v[keys, :]
            p = p_ref[b, 0]
            dm, qm = stack(dctx_ref[rows, :], masks), stack(q, masks)
            pf = p.astype(F32)
            prod = pf * dot_bt(dm, v)
            ds = (prod - pf * jnp.sum(prod, axis=-1, keepdims=True)).astype(BF16)
            dj_ref[rows, 0:256] = (pick(dot(ds, k), masks) * 0.125).astype(BF16)
            dj_ref[rows, 256:512] = dot_at(ds, qm)[0:seq, :].astype(BF16)
            dj_ref[rows, 512:768] = dot_at(p, dm)[0:seq, :].astype(BF16)

        grad = dot(ht_ref[...], dj_ref[...]).astype(BF16)
        store_blocks(grad, ends[:2], ends[2:], piece * (quad + prior))


def last_kernel(deps, dj0, dj1, dj2, x_ref, dx_ref, vec_ref, *refs):
    pieces, (out_ref, dvec_ref, w_s, dh_s, sems) = refs[:6], refs[6 + deps :]
    me, y, z = place()
    copies = start(shard_rows(pieces, w_s, me, y), sems)
    gain = vec_ref[0:1, :]
    dvec_ref[...] = jnp.zeros_like(dvec_ref)
    tokens, width = x_ref.shape
    for copy in copies:
        copy.wait()
    pull = jnp.concatenate(
        [dj[:, kind * 256 : kind * 256 + 256] for kind in range(3) for dj in (dj0, dj1, dj2)], axis=1
    )
    dh_s[...] = dot_bt(pull, w_s[...])

    length, count, _ = out_ref.shape
    seq = tokens // count
    for image in range(count):
        rows = slice(image * seq, (image + 1) * seq)
        normal, factor = standardize(x_ref[rows, :].astype(F32))
        pull = dh_s[rows, :]
        dvec_ref[0:1, :] += jnp.sum(pull * normal, axis=0, keepdims=True)
        dvec_ref[1:2, :] += jnp.sum(pull, axis=0, keepdims=True)
        total = dx_ref[rows, :] + norm_back(pull * gain, normal, factor)
        out_ref[:, image, :] = total[0:length, :]


def mlp_end_kernel(*refs):
    parts, (up_ref, down_ref, out_ref, turn_s) = refs[:12], refs[12:]
    me, y, z = place()
    rows, lanes = parts[0].shape
    half = rows // 2
    eighth = half // 4
    for chunk in range(3):
        for rel in range(4):
            piece = parts[chunk * 4 + rel]
            at = ((rel // 2) ^ y) * 2 + ((rel % 2) ^ z)
            where = pl.ds(pl.multiple_of(at * half, half), half)
            turn_s[where, :] = piece[0:half, :].astype(F32)
            where = pl.ds(pl.multiple_of(at * eighth, eighth), eighth)
            for owner in range(4):
                col = (owner * 3 + chunk) * lanes
                up_ref[where, col : col + lanes] = piece[half + owner * eighth : half + (owner + 1) * eighth, :].astype(F32)
            if chunk == 2:
                for block in range(3):
                    first = rows + block * eighth
                    col = block * lanes
                    out_ref[where, col : col + lanes] = piece[first : first + eighth, :].astype(F32)
        down_ref[chunk * lanes : (chunk + 1) * lanes, :] = turn_s[...].T


def rows_end_kernel(*refs):
    parts, joint_ref = refs[:4], refs[4]
    me, y, z = place()
    width = parts[0].shape[1]
    third = width // 3
    piece = parts[0].shape[0] // 3
    for rel in range(4):
        at = ((rel // 2) ^ y) * 2 + ((rel % 2) ^ z)
        where = pl.ds(pl.multiple_of(at * piece, piece), piece)
        for quad in range(3):
            block = parts[rel][quad * piece : (quad + 1) * piece, :].astype(F32)
            for kind in range(3):
                col = kind * width + quad * third
                joint_ref[where, col : col + third] = block[:, kind * third : (kind + 1) * third]


def on_device(
    images,
    first_gain,
    first_shift,
    joint_weight,
    out_weight,
    second_gain,
    second_shift,
    up_weight,
    down_weight,
    keep_flags,
    cotangent,
):
    count, length, width = images.shape
    n_dp = lax.axis_size("dp")
    n_fs = lax.axis_size("fsdp")
    me = lax.axis_index("fsdp")
    y = lax.axis_index("dp") & 1
    seq = up_to(length, 16)
    window = up_to(seq, 256)
    tokens = count * seq
    long = tokens + window - seq
    ff = up_weight.shape[1]
    fourth = ff // n_fs
    third = fourth // 3
    eighth = width // 16

    def swap(axis, bit):
        n = n_dp if axis == "dp" else n_fs
        return lambda v: lax.ppermute(v, axis, [(i, i ^ bit) for i in range(n)])

    core, over_x, over_y, over_z = swap("fsdp", 1), swap("fsdp", 2), swap("dp", 1), swap("dp", 2)

    def call(body, outs, dense, pieces=(), deps=(), scratch=(), outside=False, us=1):
        args = [*dense, *pieces, *deps]
        return pl.pallas_call(
            body,
            out_shape=outs,
            in_specs=[vmem()] * len(dense) + [in_hbm()] * len(pieces) + [anywhere()] * len(deps),
            out_specs=[in_hbm() if outside else vmem()] * len(outs),
            scratch_shapes=list(scratch),
            compiler_params=pltpu.CompilerParams(vmem_limit_bytes=LIMIT),
            cost_estimate=cost(us * FLOPS, 0),
        )(*args)

    def shape(*dims, dtype=BF16):
        return jax.ShapeDtypeStruct(dims, dtype)

    def dma(n):
        return pltpu.SemaphoreType.DMA((n,))

    def tie(value, *tokens):
        return lax.optimization_barrier((value, *tokens))[0]

    half = joint_weight.shape[0] // 2
    xh_joint = over_x(lax.dynamic_slice_in_dim(joint_weight, y * half, half, 0))

    vec = jnp.concatenate([first_gain, first_shift, second_gain, second_shift])
    other = over_x(vec)
    both = jnp.stack([vec, core(vec), other, core(other)])
    both = both.reshape(n_fs, 4, -1)
    vecs = jnp.concatenate([lax.dynamic_index_in_dim(both, me ^ i, 0, False) for i in range(n_fs)], axis=1)
    vecs = jnp.pad(vecs.astype(F32), ((0, 4), (0, 0)))

    packed = (4 * (width // n_fs) + 3 * third, 3 * (width // n_fs))
    whole, mine, rest = call(
        pack_kernel,
        [shape(sum(packed), third), shape(sum(packed) // 2, third), shape(2 * packed[0], third)],
        [],
        [up_weight, down_weight, out_weight],
        scratch=[dma(44)],
        outside=True,
    )
    yh_joint = over_y(tie(xh_joint, mine, whole))
    w_joint = [joint_weight, core(joint_weight), xh_joint, yh_joint, core(xh_joint), core(yh_joint)]
    near = core(whole)
    xh = over_x(tie(mine, xh_joint, other))
    yh = over_y(xh)
    w_rest = [rest, core(rest), over_x(tie(rest, w_joint[3], vecs))]

    pads = ((0, 0), (0, seq - length), (0, 0))
    x = jnp.pad(images, pads).reshape(tokens, width)
    g = jnp.pad(cotangent, pads).reshape(tokens, width)
    live = jnp.pad(keep_flags, ((0, 0), (0, window - length))).astype(F32).reshape(count, 1, window)

    (hn1,) = call(first_norm_kernel, [shape(tokens, width)], [x, vecs])
    h1t, gt = call(turn_kernel, [shape(width, tokens), shape(width, tokens)], [hn1, g])

    def front(deps):
        prior = lambda i: jnp.maximum(i - 1, 0)
        return pl.pallas_call(
            lambda *refs: front_kernel(len(deps), *refs),
            grid=(1 + count,),
            out_shape=[pltpu.HBM((long, 3 * width), BF16), pltpu.HBM((count, 3, 4 * seq, window), BF16), shape(tokens, width)],
            in_specs=[
                pl.BlockSpec((tokens, width), lambda i: (0, 0)),
                pl.BlockSpec((count, 1, window), lambda i: (0, 0, 0)),
                *[in_hbm()] * 6,
                *[anywhere()] * len(deps),
            ],
            out_specs=[
                anywhere(),
                pl.BlockSpec((1, 3, 4 * seq, window), lambda i: (prior(i), 0, 0, 0)),
                pl.BlockSpec((seq, width), lambda i: (prior(i), 0)),
            ],
            scratch_shapes=[
                pltpu.VMEM((width, 3 * width), BF16),
                pltpu.VMEM((long, 3 * width), BF16),
                dma(6),
                pltpu.SemaphoreType.DMA,
            ],
            compiler_params=pltpu.CompilerParams(vmem_limit_bytes=LIMIT),
            cost_estimate=cost(14 * FLOPS, 0),
        )(hn1, live, *w_joint, *deps)

    def plus(*terms):
        total = terms[0].astype(F32)
        for term in terms[1:]:
            total = total + term.astype(F32)
        return total.astype(BF16)

    far_bits = [1 << bit for bit in range(2, n_dp.bit_length() - 1)]

    class Chunk:
        def __init__(self, k0, k1, s0, s1):
            self.keeps, self.parts, self.stage = (k0, k1), [], 0
            self.hops = [[over_x], [over_y], [over_z], *[[swap("dp", bit)] for bit in far_bits], [over_z, over_y], [over_y], []]
            self.flying = [core(s0), core(s1)]

        def sends(self):
            k0, k1 = self.keeps
            got, self.stage = self.flying, self.stage + 1
            left = len(self.hops) - self.stage
            if self.stage == 1:
                self.near = got[0]
                return [plus(k1, got[1])]
            if self.stage == 2:
                self.rx = got[0]
                return [plus(k0[2:4], self.near[2:4], self.rx[2:4])]
            if self.stage == 3:
                self.ry = got[0]
                return [plus(k0[1], self.near[1], self.rx[1], self.ry[1])]
            if self.stage == 4:
                total = plus(k0[0], self.near[0], self.rx[0], self.ry[0], got[0])
                return [total] * (2 if left == 2 else 1)
            if left >= 2:
                return [plus(self.sent[0], got[0])] * (2 if left == 2 else 1)
            if left == 1:
                self.parts = [self.sent[0], *got]
                rounds[-1] += got[1:]
                return got[:1]
            self.parts = self.parts + got
            rounds[-1] += got
            return []

        def fly(self):
            self.flying = [hop(array) for array, hop in zip(self.sent, self.hops[self.stage - 1])]

        @property
        def done(self):
            return len(self.parts) == 4

        def hold(self, tokens):
            if self.stage <= 3:
                k0, k1 = self.keeps
                self.keeps = (tie(k0, *tokens), tie(k1, *tokens)) if self.stage == 0 else (tie(k0, *tokens), k1)
            elif self.stage <= 3 + len(far_bits):
                self.sent = [tie(self.sent[0], *tokens), *self.sent[1:]]

    class Small:
        def __init__(self, total):
            self.total, self.flying, self.done = total, None, False
            self.hops = [core, over_z, over_y, over_x, *[swap("dp", bit) for bit in far_bits]]

        def hold(self, tokens):
            pass

        def sends(self):
            if self.flying is not None:
                self.total = self.sent[0] + self.flying[0]
            self.done = not self.hops
            return [] if self.done else [self.total]

        def fly(self):
            self.flying = [self.hops.pop(0)(self.sent[0])]

    rounds = []

    def advance(items, *tokens):
        rounds.append([])
        tokens = [*tokens, *(rounds.pop(0) if len(rounds) > 2 else [])]
        items = [item for item in items if not item.done]
        if tokens:
            for item in items:
                item.hold(tokens)
        plans = [item.sends() for item in items]
        flat = lax.optimization_barrier((*[array for arrays in plans for array in arrays], *tokens))
        sent, at = list(flat[len(flat) - len(tokens) :]), 0
        for item, arrays in zip(items, plans):
            item.sent = list(flat[at : at + len(arrays)])
            at += len(arrays)
            if arrays:
                item.fly()
                sent = [*sent, item.sent[0]]
        return sent

    joint, probs, ctx = front([])
    w_first = [whole, near, xh, yh, core(xh), core(tie(yh, ctx))]

    wide = shape(tokens, n_fs * third)
    full = shape(tokens, width, dtype=F32)
    weights = [pltpu.VMEM((width, n_fs * third), BF16), pltpu.VMEM((n_fs * third, width), BF16)]

    def grads(act, pull, deps):
        ends = call(
            lambda *refs: mlp_grad_kernel(len(deps), *refs),
            [shape(4, width // 2, third)] * 4,
            [act, pull, gt, h2t],
            deps=deps,
            us=4,
        )
        return ends

    def mlp(chunk, out_sum, dh, deps):
        return call(
            lambda *refs: mlp_kernel(chunk, len(deps), *refs),
            [wide, wide, full, full],
            [g, hn2, out_sum, dh],
            [*w_rest, fars[chunk - 1]],
            deps,
            [*weights, dma(28)],
            us=7,
        )

    act, pull, out_sum, dh, hn2, h2t, x1 = call(
        lambda *refs: mlp_kernel(0, 0, *refs),
        [wide, wide, full, full, shape(tokens, width), shape(width, tokens), full],
        [g, ctx, x, vecs],
        w_first,
        scratch=[*weights, pltpu.VMEM((width, width), BF16), dma(80)],
        us=11,
    )
    part = 2 * width
    far = tie(w_rest[2][:part], x1)
    fars = [core(far)]
    m0 = Chunk(*grads(act, pull, [far]))
    act, pull, out_sum, dh = mlp(1, out_sum, dh, [])
    fars.append(core(tie(w_rest[2][part:], dh)))
    m1 = Chunk(*grads(act, pull, advance([m0])))
    act, pull, out_sum, dh = mlp(2, out_sum, dh, advance([m0]))
    ends = grads(act, pull, [*advance([m1]), *advance([m0], dh)])
    deps = advance([m1, m0])
    result, dx1, dctx, *ends, dvec2 = call(
        lambda *refs: middle_kernel(len(deps), *refs),
        [
            shape(length, count, width),
            shape(tokens, width, dtype=F32),
            shape(tokens, width),
            *[shape(4, width // 2 + 3 * eighth, third)] * 4,
            shape(8, width, dtype=F32),
        ],
        [x1, out_sum, dh, g, vecs, ctx, *ends],
        w_first,
        deps,
        [pltpu.VMEM((width, width), BF16), pltpu.VMEM((tokens, width), BF16), pltpu.VMEM((width, tokens), BF16), dma(24)],
        us=5,
    )

    m2 = Chunk(*ends)

    output = jnp.transpose(result, (1, 0, 2))

    def back(first, quads, prior, deps):
        sets, specs = [], []
        for quad in range(first, first + quads):
            sets += [joint, joint, joint, probs, dctx]
            specs += [pl.BlockSpec((long, 256), lambda i, c=kind * (width // 256) + quad: (0, c)) for kind in range(3)]
            specs += [
                pl.BlockSpec((count, 1, 4 * seq, window), lambda i, quad=quad: (0, quad, 0, 0)),
                pl.BlockSpec((tokens, 256), lambda i, quad=quad: (0, quad)),
            ]
        size = eighth * (first + quads)
        return pl.pallas_call(
            lambda *refs: back_kernel(quads, first, len(deps), *refs),
            grid=(1,),
            out_shape=[shape(4, size, width)] * 4 + [shape(tokens, width)] * quads,
            in_specs=[vmem(), *specs, *[vmem()] * len(prior), *[anywhere()] * len(deps)],
            out_specs=[vmem()] * (4 + quads),
            compiler_params=pltpu.CompilerParams(vmem_limit_bytes=LIMIT),
            cost_estimate=cost(5 * quads * FLOPS, 0),
        )(h1t, *sets, *prior, *deps)

    *ends, dj0, dj1 = back(0, 2, [], advance([m2]))
    *ends, dj2 = back(2, 1, ends, advance([m2, m1, m0], dj0))
    jj = Chunk(*ends)
    deps = [*advance([jj]), *advance([m1, m0], dj0)]
    grad_x, dvec1 = call(
        lambda *refs: last_kernel(len(deps), *refs),
        [shape(length, count, width, dtype=F32), shape(8, width, dtype=F32)],
        [dj0, dj1, dj2, x, dx1, vecs],
        w_joint,
        deps,
        [pltpu.VMEM((width, 3 * width), BF16), pltpu.VMEM((tokens, width), F32), dma(6)],
    )
    small = Small(jnp.concatenate([dvec1[0:2], dvec2[0:2]], axis=0))
    grad_images = jnp.transpose(grad_x, (1, 0, 2))
    advance([m2, m1, m0], dvec1)
    advance([jj, m2, m1, small])
    advance([jj, m2, m1, m0, small])
    items = [jj, m2, m1, m0, small]
    while any(not item.done for item in items):
        advance(items)
    mine = lax.dynamic_slice_in_dim(small.total, me * (width // n_fs), width // n_fs, 1)

    grad_up, grad_down, grad_out = call(
        mlp_end_kernel,
        [shape(width // n_fs, ff, dtype=F32), shape(fourth, width, dtype=F32), shape(width // n_fs, width, dtype=F32)],
        [*m0.parts, *m1.parts, *m2.parts],
        scratch=[pltpu.VMEM((width, third), F32)],
        us=3,
    )
    (grad_joint,) = call(rows_end_kernel, [shape(width // n_fs, 3 * width, dtype=F32)], jj.parts)
    return (
        output,
        grad_images,
        mine[0],
        mine[1],
        grad_joint,
        grad_out,
        mine[2],
        mine[3],
        grad_up,
        grad_down,
    )


def solution(mesh):
    rows = P("fsdp", None)
    tokens = P(("dp", "fsdp"), None, None)
    one = P("fsdp")
    return jax.shard_map(
        on_device,
        mesh=mesh,
        in_specs=(tokens, one, one, rows, rows, one, one, rows, rows, P(("dp", "fsdp"), None), tokens),
        out_specs=(tokens, tokens, one, one, rows, rows, one, one, rows, rows),
        check_vma=False,
    )
```

```python
import jax
import jax.numpy as jnp
from jax import lax
from jax.experimental import pallas as pl
from jax.experimental.pallas import tpu as pltpu
from jax.sharding import PartitionSpec as P

HEADS = 12
EPS = 1e-06
MASKED = -1e30
F32 = jnp.float32
BF16 = jnp.bfloat16
VM = pltpu.VMEM
ANY = pl.ANY
LIMIT = 12 * 1024 * 1024
FLOPS = int(1.15e9 * 0.3)


def vmem():
    return pl.BlockSpec(memory_space=VM)


def anywhere():
    return pl.BlockSpec(memory_space=ANY)


def in_hbm():
    return pl.BlockSpec(memory_space=pltpu.HBM)


def up_to(value, step):
    return (value + step - 1) // step * step


def dot(a, b):
    return jnp.dot(a, b, preferred_element_type=F32)


def dot_bt(a, b):
    return lax.dot_general(a, b, (((1,), (1,)), ((), ())), preferred_element_type=F32)


def dot_at(a, b):
    return lax.dot_general(a, b, (((0,), (0,)), ((), ())), preferred_element_type=F32)


def place():
    me = lax.axis_index("fsdp")
    dp = lax.axis_index("dp")
    return me, dp & 1, (dp >> 1) & 1


def start(table, sems, base=0):
    copies = []
    for index, (source, first, count, dest, at, col) in enumerate(table):
        src = source if count == source.shape[0] else source.at[pl.ds(pl.multiple_of(first, 16), count)]
        where = pl.ds(pl.multiple_of(at, 16), count)
        into = dest.at[where] if col is None else dest.at[where, col : col + source.shape[1]]
        copy = pltpu.make_async_copy(src, into, sems.at[base + index])
        copy.start()
        copies.append(copy)
    return copies


def cost(flops, moved):
    return pl.CostEstimate(flops=flops, bytes_accessed=moved, transcendentals=0)


def shard_rows(pieces, dest, me, y):
    rows = pieces[0].shape[0]
    half = rows // 2
    starts = (
        me * rows,
        (me ^ 1) * rows,
        (me ^ 2) * rows + y * half,
        (me ^ 2) * rows + (1 - y) * half,
        (me ^ 3) * rows + y * half,
        (me ^ 3) * rows + (1 - y) * half,
    )
    return [(piece, 0, piece.shape[0], dest, at, None) for piece, at in zip(pieces, starts)]


def packed_rows(pieces, dests, me, y, width, chunk=0):
    rows = width // 4
    n_halves = 2 if len(pieces) == 6 else 1
    owners = ((0, (0, 1)), (1, (0, 1)), (2, (y,)), (2, (1 - y,)), (3, (y,)), (3, (1 - y,)))
    if n_halves == 1:
        owners = tuple((rel, (0,)) for rel in range(4))
    tables = ([], [], [])
    for piece, (rel, halves) in zip(pieces, owners):
        size = piece.shape[0] // len(halves)
        for index, half in enumerate(halves):
            first = index * size if len(halves) > 1 or piece.shape[0] < 4 * width else chunk * 2 * width
            for table, dest, blocks, count, at in (
                (tables[0], dests[0], 4, rows // n_halves, (me ^ rel) * rows),
                (tables[1], dests[1], 3, 256 // n_halves, (0, 2, 1, 3)[rel] * 256),
                (tables[2], dests[2], 3, rows // n_halves, (me ^ rel) * rows),
            ):
                for block in range(blocks):
                    table.append((piece, first, count, dest, at + half * count, block * 256))
                    first = first + count
    return tables


def pack_kernel(up_ref, down_ref, out_ref, whole_ref, half_ref, rest_ref, sems):
    me, y, z = place()
    rows, third = up_ref.shape[0], down_ref.shape[0] // 3
    copies = []

    def put(source, first, count, col, dest, at):
        copy = pltpu.make_async_copy(
            source.at[pl.ds(pl.multiple_of(first, 16), count), col : col + third],
            dest.at[pl.ds(at, count)],
            sems.at[len(copies)],
        )
        copy.start()
        copies.append(copy)

    for dest, halves in ((half_ref, (y,)), (whole_ref, (0, 1))):
        at = 0
        for half in halves:
            for source, first, count, cols in (
                (up_ref, 0, rows // 2, [owner * 3 * third for owner in range(4)]),
                (down_ref, 0, third // 2, [block * third for block in range(3)]),
                (out_ref, 0, rows // 2, [block * third for block in range(3)]),
            ):
                for col in cols:
                    put(source, first + half * count, count, col, dest, at)
                    at += count
    at = 0
    for chunk in (1, 2):
        for owner in range(4):
            put(up_ref, 0, rows, (owner * 3 + chunk) * third, rest_ref, at)
            at += rows
        for block in range(3):
            put(down_ref, chunk * third, third, block * third, rest_ref, at)
            at += third
    for copy in copies:
        copy.wait()


def standardize(value):
    mean = jnp.mean(value, axis=-1, keepdims=True)
    center = value - mean
    spread = jnp.mean(center * center, axis=-1, keepdims=True)
    factor = lax.rsqrt(spread + EPS)
    return center * factor, factor


def norm_back(upstream, normal, factor):
    first = jnp.mean(upstream, axis=-1, keepdims=True)
    second = jnp.mean(upstream * normal, axis=-1, keepdims=True)
    return factor * (upstream - first - normal * second)


def owner_rows(turned, dest, me, y, z):
    piece = turned.shape[0] // 16
    for block in range(16):
        owner, yb, zb = block // 4, (block // 2) % 2, block % 2
        rel = owner ^ me
        at = (rel & 1) * 8 + (rel >> 1) * 4 + (yb ^ y) * 2 + (zb ^ z)
        where = pl.ds(pl.multiple_of(at * piece, piece), piece)
        dest[where, :] = turned[block * piece : (block + 1) * piece, :]


def quarter_rows(turned, dest, y, z):
    piece = turned.shape[0] // 4
    for block in range(4):
        yb, zb = block // 2, block % 2
        at = (yb ^ y) * 2 + (zb ^ z)
        where = pl.ds(pl.multiple_of(at * piece, piece), piece)
        dest[where, :] = turned[block * piece : (block + 1) * piece, :]


def row_loop(tokens, step):
    return pl.loop(0, tokens // step)


def first_norm_kernel(x_ref, vec_ref, hn_ref):
    gain, shift = vec_ref[0:1, :], vec_ref[1:2, :]

    @row_loop(x_ref.shape[0], 208)
    def _(i):
        rows = pl.ds(pl.multiple_of(i * 208, 16), 208)
        normal, factor = standardize(x_ref[rows, :].astype(F32))
        hn_ref[rows, :] = (normal * gain + shift).astype(BF16)


def turn_kernel(hn_ref, g_ref, h1t_ref, gt_ref):
    me, y, z = place()
    owner_rows(hn_ref[...].T, h1t_ref, me, y, z)
    quarter_rows(g_ref[...].T, gt_ref, y, z)


def head_masks():
    lane = lax.broadcasted_iota(jnp.int32, (1, 256), 1) // 64
    return [lane == h for h in range(4)]


def stack(value, masks):
    return jnp.concatenate([value * mask.astype(BF16) for mask in masks], axis=0)


def pick(value, masks):
    seq = value.shape[0] // 4
    total = jnp.where(masks[0], value[0:seq], 0.0)
    for h in range(1, 4):
        total = jnp.where(masks[h], value[h * seq : (h + 1) * seq], total)
    return total


def front_kernel(deps, hn_ref, mask_ref, *refs):
    pieces, (joint_ref, p_ref, ctx_ref, w_s, joint_s, sems, out_sem) = refs[:6], refs[6 + deps :]
    me, y, z = place()
    step = pl.program_id(0)
    tokens, width = hn_ref.shape
    seq, window = ctx_ref.shape[0], mask_ref.shape[2]

    @pl.when(step == 0)
    def _():
        copies = start(shard_rows(pieces, w_s, me, y), sems)
        joint_s[tokens:, :] = jnp.zeros((joint_s.shape[0] - tokens, 3 * width), BF16)
        for copy in copies:
            copy.wait()

        @pl.loop(0, 3 * width // 256)
        def _(n):
            cols = pl.ds(pl.multiple_of(n * 256, 256), 256)
            scale = jnp.where(n < width // 256, 0.125, 1.0).astype(BF16)
            value = dot(hn_ref[...], w_s[:, cols])
            joint_s[0:tokens, cols] = value.astype(BF16) * scale

        pltpu.make_async_copy(joint_s, joint_ref, out_sem).start()

    @pl.when(step > 0)
    def _():
        image = step - 1
        base = pl.multiple_of(image * seq, 16)
        rows, keys = pl.ds(base, seq), pl.ds(base, window)
        live = mask_ref[image]
        masks = head_masks()
        for quad in range(width // 256):
            at = quad * 256
            q = joint_s[rows, at : at + 256]
            k = joint_s[keys, width + at : width + at + 256]
            v = joint_s[keys, 2 * width + at : 2 * width + at + 256]
            s = dot_bt(stack(q, masks), k)
            s = jnp.where(live > 0.5, s, MASKED)
            e = jnp.exp(s - jnp.max(s, axis=-1, keepdims=True))
            p = (e * (1.0 / jnp.sum(e, axis=-1, keepdims=True))).astype(BF16)
            p_ref[0, quad] = p
            ctx_ref[:, at : at + 256] = pick(dot(p, v), masks).astype(BF16)

    @pl.when(step == pl.num_programs(0) - 1)
    def _():
        pltpu.make_async_copy(joint_s, joint_ref, out_sem).wait()


def gelu_both(u):
    phi = 0.5 + 0.5 * lax.erf(u * 0.7071067811865476)
    bell = jnp.exp(-0.5 * (u * u)) * 0.3989422804014327
    return u * phi, phi + u * bell


def mlp_kernel(chunk, deps, g_ref, *refs):
    me, y, z = place()
    first = chunk == 0
    if first:
        (ctx_ref, x_ref, vec_ref), refs = refs[:3], refs[3:]
        pieces, refs = refs[:6], refs[6 + deps :]
        act_ref, pull_ref, out_ref, dh_ref, hn_ref, ht_ref, x1_ref, wu_s, wd_s, wo_s, sems = refs
        width = ctx_ref.shape[1]
        ups, downs, outs = packed_rows(pieces, (wu_s, wd_s, wo_s), me, y, width)
        early = start(outs, sems)
        late = start(ups + downs, sems, len(outs))
    else:
        (hn_ref, out_in, dh_in), refs = refs[:3], refs[3:]
        pieces, refs = refs[:4], refs[4 + deps :]
        act_ref, pull_ref, out_ref, dh_ref, wu_s, wd_s, sems = refs
        width = hn_ref.shape[1]
        ups, downs, _ = packed_rows(pieces, (wu_s, wd_s, None), me, y, width, chunk - 1)
        early, late = [], start(ups + downs, sems)
    rows = wd_s.shape[0] // 4
    for copy in early:
        copy.wait()
    if first:
        gain, shift = vec_ref[2:3, :], vec_ref[3:4, :]

        @row_loop(ctx_ref.shape[0], 208)
        def _(i):
            part = pl.ds(pl.multiple_of(i * 208, 16), 208)
            middle = x_ref[part, :].astype(F32) + dot(ctx_ref[part, :], wo_s[...])
            x1_ref[part, :] = middle
            normal, factor = standardize(middle)
            hn_ref[part, :] = (normal * gain + shift).astype(BF16)

        owner_rows(hn_ref[...].T, ht_ref, me, y, z)
    for copy in late:
        copy.wait()
    for c in range(2):
        cols = []
        both = slice(2 * c * rows, 2 * (c + 1) * rows)
        for x in range(2):
            owner = me ^ (c + 2 * x)
            col = pl.ds(pl.multiple_of(owner * rows, rows), rows)
            act, slope = gelu_both(dot(hn_ref[...], wu_s[:, col]))
            at = (2 * c + x) * rows
            act_ref[:, at : at + rows] = act.astype(BF16)
            pull_ref[:, at : at + rows] = (dot_bt(g_ref[...], wd_s[at : at + rows, :]) * slope).astype(BF16)
            cols.append(col)
        plus = dot(act_ref[:, both], wd_s[both, :])
        wu = jnp.concatenate([wu_s[:, col] for col in cols], axis=1)
        back = dot_bt(pull_ref[:, both], wu)
        if c == 0 and first:
            out_ref[...] = plus
            dh_ref[...] = back
        elif c == 0:
            out_ref[...] = out_in[...] + plus
            dh_ref[...] = dh_in[...] + back
        else:
            out_ref[...] += plus
            dh_ref[...] += back


def mlp_grad_kernel(deps, act_ref, pull_ref, gt_ref, ht_ref, *refs):
    k0, k1, s0, s1 = refs[deps:]
    me, y, z = place()
    keep, send = (k0, k1), (s0, s1)
    width = gt_ref.shape[0]
    rows = act_ref.shape[1] // 4
    quarter = width // 4
    eighth = width // 16
    for c in range(2):
        for x in range(2):
            owner = me ^ (c + 2 * x)
            cols = slice((2 * c + x) * rows, (2 * c + x + 1) * rows)
            gd = dot(gt_ref[...], act_ref[:, cols]).astype(BF16)
            dest = (send if c else keep)[x]
            for part in range(4):
                dest[part, 0:quarter, :] = gd[part * quarter : (part + 1) * quarter, :]
            gu = dot(ht_ref[...], pull_ref[:, cols]).astype(BF16)
            where = pl.ds(pl.multiple_of(quarter + owner * eighth, eighth), eighth)
            for block in range(16):
                dest = (send if block // 8 else keep)[(block // 4) % 2]
                dest[block % 4, where, :] = gu[block * eighth : (block + 1) * eighth, :]


def middle_kernel(deps, x1_ref, out_in, dh_in, g_ref, vec_ref, ctx_ref, *refs):
    before, refs = refs[:4], refs[4:]
    pieces, refs = refs[:6], refs[6 + deps :]
    result_ref, dx_ref, dctx_ref, k0, k1, s0, s1, dvec_ref, w_s, dy_s, ct_s, sems = refs
    me, y, z = place()
    tokens, width = ctx_ref.shape
    copies = start(packed_rows(pieces, (None, None, w_s), me, y, width)[2], sems)
    gain = vec_ref[2:3, :]
    dvec_ref[...] = jnp.zeros_like(dvec_ref)

    @row_loop(tokens, 208)
    def _(i):
        rows = pl.ds(pl.multiple_of(i * 208, 16), 208)
        middle = x1_ref[rows, :]
        normal, factor = standardize(middle)
        pull = dh_in[rows, :]
        dvec_ref[0:1, :] += jnp.sum(pull * normal, axis=0, keepdims=True)
        dvec_ref[1:2, :] += jnp.sum(pull, axis=0, keepdims=True)
        dx = g_ref[rows, :].astype(F32) + norm_back(pull * gain, normal, factor)
        dx_ref[rows, :] = dx
        dy_s[rows, :] = dx.astype(BF16)

    length, count, _ = result_ref.shape
    seq = tokens // count
    for image in range(count):
        rows = slice(image * seq, image * seq + length)
        result_ref[:, image, :] = (x1_ref[rows, :] + out_in[rows, :]).astype(BF16)
    owner_rows(ctx_ref[...].T, ct_s, me, y, z)
    for copy in copies:
        copy.wait()
    dctx_ref[...] = dot_bt(dy_s[...], w_s[...]).astype(BF16)
    value = dot(ct_s[...], dy_s[...]).astype(BF16)
    piece = width // 16
    base = before[0].shape[1]
    for old, new in zip(before, (k0, k1, s0, s1)):
        new[:, 0:base, :] = old[...]
    for block in range(16):
        dest = ((s0, s1) if block // 8 else (k0, k1))[(block // 4) % 2]
        for cols in range(width // 256):
            at = base + cols * piece
            dest[block % 4, at : at + piece, :] = value[block * piece : (block + 1) * piece, cols * 256 : cols * 256 + 256]


def store_blocks(value, keep, send, at=0):
    piece = value.shape[0] // 16
    for block in range(16):
        dest = (send if block // 8 else keep)[(block // 4) % 2]
        dest[block % 4, at : at + piece, :] = value[block * piece : (block + 1) * piece, :]


def back_kernel(quads, prior, deps, ht_ref, *refs):
    parts, refs = refs[: 5 * quads], refs[5 * quads :]
    if prior:
        before, refs = refs[:4], refs[4:]
    refs = refs[deps:]
    ends, djs = refs[:4], refs[4:]
    masks = head_masks()
    piece = ht_ref.shape[0] // 16
    if prior:
        for old, new in zip(before, ends):
            new[:, 0 : old.shape[1], :] = old[...]
    for quad in range(quads):
        joint_q, joint_k, joint_v, p_ref, dctx_ref = parts[5 * quad : 5 * quad + 5]
        dj_ref = djs[quad]
        images, _, stacked, window = p_ref.shape
        seq = stacked // 4

        @pl.loop(0, images)
        def _(b):
            base = pl.multiple_of(b * seq, 16)
            rows, keys = pl.ds(base, seq), pl.ds(base, window)
            q, k, v = joint_q[rows, :], joint_k[keys, :], joint_v[keys, :]
            p = p_ref[b, 0]
            dm, qm = stack(dctx_ref[rows, :], masks), stack(q, masks)
            pf = p.astype(F32)
            prod = pf * dot_bt(dm, v)
            ds = (prod - pf * jnp.sum(prod, axis=-1, keepdims=True)).astype(BF16)
            dj_ref[rows, 0:256] = (pick(dot(ds, k), masks) * 0.125).astype(BF16)
            dj_ref[rows, 256:512] = dot_at(ds, qm)[0:seq, :].astype(BF16)
            dj_ref[rows, 512:768] = dot_at(p, dm)[0:seq, :].astype(BF16)

        grad = dot(ht_ref[...], dj_ref[...]).astype(BF16)
        store_blocks(grad, ends[:2], ends[2:], piece * (quad + prior))


def last_kernel(deps, dj0, dj1, dj2, x_ref, dx_ref, vec_ref, *refs):
    pieces, (out_ref, dvec_ref, w_s, dh_s, sems) = refs[:6], refs[6 + deps :]
    me, y, z = place()
    copies = start(shard_rows(pieces, w_s, me, y), sems)
    gain = vec_ref[0:1, :]
    dvec_ref[...] = jnp.zeros_like(dvec_ref)
    tokens, width = x_ref.shape
    for copy in copies:
        copy.wait()
    pull = jnp.concatenate(
        [dj[:, kind * 256 : kind * 256 + 256] for kind in range(3) for dj in (dj0, dj1, dj2)], axis=1
    )
    dh_s[...] = dot_bt(pull, w_s[...])

    length, count, _ = out_ref.shape
    seq = tokens // count
    for image in range(count):
        rows = slice(image * seq, (image + 1) * seq)
        normal, factor = standardize(x_ref[rows, :].astype(F32))
        pull = dh_s[rows, :]
        dvec_ref[0:1, :] += jnp.sum(pull * normal, axis=0, keepdims=True)
        dvec_ref[1:2, :] += jnp.sum(pull, axis=0, keepdims=True)
        total = dx_ref[rows, :] + norm_back(pull * gain, normal, factor)
        out_ref[:, image, :] = total[0:length, :]


def mlp_end_kernel(*refs):
    parts, (up_ref, down_ref, out_ref, turn_s) = refs[:12], refs[12:]
    me, y, z = place()
    rows, lanes = parts[0].shape
    half = rows // 2
    eighth = half // 4
    for chunk in range(3):
        for rel in range(4):
            piece = parts[chunk * 4 + rel]
            at = ((rel // 2) ^ y) * 2 + ((rel % 2) ^ z)
            where = pl.ds(pl.multiple_of(at * half, half), half)
            turn_s[where, :] = piece[0:half, :].astype(F32)
            where = pl.ds(pl.multiple_of(at * eighth, eighth), eighth)
            for owner in range(4):
                col = (owner * 3 + chunk) * lanes
                up_ref[where, col : col + lanes] = piece[half + owner * eighth : half + (owner + 1) * eighth, :].astype(F32)
            if chunk == 2:
                for block in range(3):
                    first = rows + block * eighth
                    col = block * lanes
                    out_ref[where, col : col + lanes] = piece[first : first + eighth, :].astype(F32)
        down_ref[chunk * lanes : (chunk + 1) * lanes, :] = turn_s[...].T


def rows_end_kernel(*refs):
    parts, joint_ref = refs[:4], refs[4]
    me, y, z = place()
    width = parts[0].shape[1]
    third = width // 3
    piece = parts[0].shape[0] // 3
    for rel in range(4):
        at = ((rel // 2) ^ y) * 2 + ((rel % 2) ^ z)
        where = pl.ds(pl.multiple_of(at * piece, piece), piece)
        for quad in range(3):
            block = parts[rel][quad * piece : (quad + 1) * piece, :].astype(F32)
            for kind in range(3):
                col = kind * width + quad * third
                joint_ref[where, col : col + third] = block[:, kind * third : (kind + 1) * third]


def on_device(
    images,
    first_gain,
    first_shift,
    joint_weight,
    out_weight,
    second_gain,
    second_shift,
    up_weight,
    down_weight,
    keep_flags,
    cotangent,
):
    count, length, width = images.shape
    n_dp = lax.axis_size("dp")
    n_fs = lax.axis_size("fsdp")
    me = lax.axis_index("fsdp")
    y = lax.axis_index("dp") & 1
    seq = up_to(length, 16)
    window = up_to(seq, 256)
    tokens = count * seq
    long = tokens + window - seq
    ff = up_weight.shape[1]
    fourth = ff // n_fs
    third = fourth // 3
    eighth = width // 16

    def swap(axis, bit):
        n = n_dp if axis == "dp" else n_fs
        return lambda v: lax.ppermute(v, axis, [(i, i ^ bit) for i in range(n)])

    core, over_x, over_y, over_z = swap("fsdp", 1), swap("fsdp", 2), swap("dp", 1), swap("dp", 2)

    def call(body, outs, dense, pieces=(), deps=(), scratch=(), outside=False, us=1):
        args = [*dense, *pieces, *deps]
        return pl.pallas_call(
            body,
            out_shape=outs,
            in_specs=[vmem()] * len(dense) + [in_hbm()] * len(pieces) + [anywhere()] * len(deps),
            out_specs=[in_hbm() if outside else vmem()] * len(outs),
            scratch_shapes=list(scratch),
            compiler_params=pltpu.CompilerParams(vmem_limit_bytes=LIMIT),
            cost_estimate=cost(us * FLOPS, 0),
        )(*args)

    def shape(*dims, dtype=BF16):
        return jax.ShapeDtypeStruct(dims, dtype)

    def dma(n):
        return pltpu.SemaphoreType.DMA((n,))

    def tie(value, *tokens):
        return lax.optimization_barrier((value, *tokens))[0]

    half = joint_weight.shape[0] // 2
    xh_joint = over_x(lax.dynamic_slice_in_dim(joint_weight, y * half, half, 0))

    vec = jnp.concatenate([first_gain, first_shift, second_gain, second_shift])
    other = over_x(vec)
    both = jnp.stack([vec, core(vec), other, core(other)])
    both = both.reshape(n_fs, 4, -1)
    vecs = jnp.concatenate([lax.dynamic_index_in_dim(both, me ^ i, 0, False) for i in range(n_fs)], axis=1)
    vecs = jnp.pad(vecs.astype(F32), ((0, 4), (0, 0)))

    packed = (4 * (width // n_fs) + 3 * third, 3 * (width // n_fs))
    whole, mine, rest = call(
        pack_kernel,
        [shape(sum(packed), third), shape(sum(packed) // 2, third), shape(2 * packed[0], third)],
        [],
        [up_weight, down_weight, out_weight],
        scratch=[dma(44)],
        outside=True,
    )
    yh_joint = over_y(tie(xh_joint, mine, whole))
    w_joint = [joint_weight, core(joint_weight), xh_joint, yh_joint, core(xh_joint), core(yh_joint)]
    near = core(whole)
    xh = over_x(tie(mine, xh_joint, other))
    yh = over_y(xh)
    w_rest = [rest, core(rest), over_x(tie(rest, w_joint[3], vecs))]

    pads = ((0, 0), (0, seq - length), (0, 0))
    x = jnp.pad(images, pads).reshape(tokens, width)
    g = jnp.pad(cotangent, pads).reshape(tokens, width)
    live = jnp.pad(keep_flags, ((0, 0), (0, window - length))).astype(F32).reshape(count, 1, window)

    (hn1,) = call(first_norm_kernel, [shape(tokens, width)], [x, vecs])
    h1t, gt = call(turn_kernel, [shape(width, tokens), shape(width, tokens)], [hn1, g])

    def front(deps):
        prior = lambda i: jnp.maximum(i - 1, 0)
        return pl.pallas_call(
            lambda *refs: front_kernel(len(deps), *refs),
            grid=(1 + count,),
            out_shape=[pltpu.HBM((long, 3 * width), BF16), pltpu.HBM((count, 3, 4 * seq, window), BF16), shape(tokens, width)],
            in_specs=[
                pl.BlockSpec((tokens, width), lambda i: (0, 0)),
                pl.BlockSpec((count, 1, window), lambda i: (0, 0, 0)),
                *[in_hbm()] * 6,
                *[anywhere()] * len(deps),
            ],
            out_specs=[
                anywhere(),
                pl.BlockSpec((1, 3, 4 * seq, window), lambda i: (prior(i), 0, 0, 0)),
                pl.BlockSpec((seq, width), lambda i: (prior(i), 0)),
            ],
            scratch_shapes=[
                pltpu.VMEM((width, 3 * width), BF16),
                pltpu.VMEM((long, 3 * width), BF16),
                dma(6),
                pltpu.SemaphoreType.DMA,
            ],
            compiler_params=pltpu.CompilerParams(vmem_limit_bytes=LIMIT),
            cost_estimate=cost(14 * FLOPS, 0),
        )(hn1, live, *w_joint, *deps)

    def plus(*terms):
        total = terms[0].astype(F32)
        for term in terms[1:]:
            total = total + term.astype(F32)
        return total.astype(BF16)

    far_bits = [1 << bit for bit in range(2, n_dp.bit_length() - 1)]

    class Chunk:
        def __init__(self, k0, k1, s0, s1):
            self.keeps, self.parts, self.stage = (k0, k1), [], 0
            self.hops = [[over_x], [over_y], [over_z], *[[swap("dp", bit)] for bit in far_bits], [over_z, over_y], [over_y], []]
            self.flying = [core(s0), core(s1)]

        def sends(self):
            k0, k1 = self.keeps
            got, self.stage = self.flying, self.stage + 1
            left = len(self.hops) - self.stage
            if self.stage == 1:
                self.near = got[0]
                return [plus(k1, got[1])]
            if self.stage == 2:
                self.rx = got[0]
                return [plus(k0[2:4], self.near[2:4], self.rx[2:4])]
            if self.stage == 3:
                self.ry = got[0]
                return [plus(k0[1], self.near[1], self.rx[1], self.ry[1])]
            if self.stage == 4:
                total = plus(k0[0], self.near[0], self.rx[0], self.ry[0], got[0])
                return [total] * (2 if left == 2 else 1)
            if left >= 2:
                return [plus(self.sent[0], got[0])] * (2 if left == 2 else 1)
            if left == 1:
                self.parts = [self.sent[0], *got]
                rounds[-1] += got[1:]
                return got[:1]
            self.parts = self.parts + got
            rounds[-1] += got
            return []

        def fly(self):
            self.flying = [hop(array) for array, hop in zip(self.sent, self.hops[self.stage - 1])]

        @property
        def done(self):
            return len(self.parts) == 4

        def hold(self, tokens):
            if self.stage <= 3:
                k0, k1 = self.keeps
                self.keeps = (tie(k0, *tokens), tie(k1, *tokens)) if self.stage == 0 else (tie(k0, *tokens), k1)
            elif self.stage <= 3 + len(far_bits):
                self.sent = [tie(self.sent[0], *tokens), *self.sent[1:]]

    class Small:
        def __init__(self, total):
            self.total, self.flying, self.done = total, None, False
            self.hops = [core, over_z, over_y, over_x, *[swap("dp", bit) for bit in far_bits]]

        def hold(self, tokens):
            pass

        def sends(self):
            if self.flying is not None:
                self.total = self.sent[0] + self.flying[0]
            self.done = not self.hops
            return [] if self.done else [self.total]

        def fly(self):
            self.flying = [self.hops.pop(0)(self.sent[0])]

    rounds = []

    def advance(items, *tokens):
        rounds.append([])
        tokens = [*tokens, *(rounds.pop(0) if len(rounds) > 1 else [])]
        items = [item for item in items if not item.done]
        if tokens:
            for item in items:
                item.hold(tokens)
        plans = [item.sends() for item in items]
        flat = lax.optimization_barrier((*[array for arrays in plans for array in arrays], *tokens))
        sent, at = list(flat[len(flat) - len(tokens) :]), 0
        for item, arrays in zip(items, plans):
            item.sent = list(flat[at : at + len(arrays)])
            at += len(arrays)
            if arrays:
                item.fly()
                sent = [*sent, item.sent[0]]
        return sent

    joint, probs, ctx = front([])
    w_first = [whole, near, xh, yh, core(xh), core(tie(yh, ctx))]

    wide = shape(tokens, n_fs * third)
    full = shape(tokens, width, dtype=F32)
    weights = [pltpu.VMEM((width, n_fs * third), BF16), pltpu.VMEM((n_fs * third, width), BF16)]

    def grads(act, pull, deps):
        ends = call(
            lambda *refs: mlp_grad_kernel(len(deps), *refs),
            [shape(4, width // 2, third)] * 4,
            [act, pull, gt, h2t],
            deps=deps,
            us=4,
        )
        return ends

    def mlp(chunk, out_sum, dh, deps):
        return call(
            lambda *refs: mlp_kernel(chunk, len(deps), *refs),
            [wide, wide, full, full],
            [g, hn2, out_sum, dh],
            [*w_rest, fars[chunk - 1]],
            deps,
            [*weights, dma(28)],
            us=7,
        )

    act, pull, out_sum, dh, hn2, h2t, x1 = call(
        lambda *refs: mlp_kernel(0, 0, *refs),
        [wide, wide, full, full, shape(tokens, width), shape(width, tokens), full],
        [g, ctx, x, vecs],
        w_first,
        scratch=[*weights, pltpu.VMEM((width, width), BF16), dma(80)],
        us=11,
    )
    part = 2 * width
    far = tie(w_rest[2][:part], x1)
    fars = [core(far)]
    m0 = Chunk(*grads(act, pull, [far]))
    act, pull, out_sum, dh = mlp(1, out_sum, dh, [])
    fars.append(core(tie(w_rest[2][part:], dh)))
    m1 = Chunk(*grads(act, pull, advance([m0])))
    act, pull, out_sum, dh = mlp(2, out_sum, dh, advance([m0]))
    ends = grads(act, pull, [*advance([m1]), *advance([m0], dh)])
    deps = advance([m1, m0])
    result, dx1, dctx, *ends, dvec2 = call(
        lambda *refs: middle_kernel(len(deps), *refs),
        [
            shape(length, count, width),
            shape(tokens, width, dtype=F32),
            shape(tokens, width),
            *[shape(4, width // 2 + 3 * eighth, third)] * 4,
            shape(8, width, dtype=F32),
        ],
        [x1, out_sum, dh, g, vecs, ctx, *ends],
        w_first,
        deps,
        [pltpu.VMEM((width, width), BF16), pltpu.VMEM((tokens, width), BF16), pltpu.VMEM((width, tokens), BF16), dma(24)],
        us=5,
    )

    m2 = Chunk(*ends)

    output = jnp.transpose(result, (1, 0, 2))

    def back(first, quads, prior, deps):
        sets, specs = [], []
        for quad in range(first, first + quads):
            sets += [joint, joint, joint, probs, dctx]
            specs += [pl.BlockSpec((long, 256), lambda i, c=kind * (width // 256) + quad: (0, c)) for kind in range(3)]
            specs += [
                pl.BlockSpec((count, 1, 4 * seq, window), lambda i, quad=quad: (0, quad, 0, 0)),
                pl.BlockSpec((tokens, 256), lambda i, quad=quad: (0, quad)),
            ]
        size = eighth * (first + quads)
        return pl.pallas_call(
            lambda *refs: back_kernel(quads, first, len(deps), *refs),
            grid=(1,),
            out_shape=[shape(4, size, width)] * 4 + [shape(tokens, width)] * quads,
            in_specs=[vmem(), *specs, *[vmem()] * len(prior), *[anywhere()] * len(deps)],
            out_specs=[vmem()] * (4 + quads),
            compiler_params=pltpu.CompilerParams(vmem_limit_bytes=LIMIT),
            cost_estimate=cost(5 * quads * FLOPS, 0),
        )(h1t, *sets, *prior, *deps)

    *ends, dj0, dj1 = back(0, 2, [], advance([m2]))
    *ends, dj2 = back(2, 1, ends, advance([m2, m1, m0], dj0))
    jj = Chunk(*ends)
    deps = [*advance([jj]), *advance([m1, m0], dj0)]
    grad_x, dvec1 = call(
        lambda *refs: last_kernel(len(deps), *refs),
        [shape(length, count, width, dtype=F32), shape(8, width, dtype=F32)],
        [dj0, dj1, dj2, x, dx1, vecs],
        w_joint,
        deps,
        [pltpu.VMEM((width, 3 * width), BF16), pltpu.VMEM((tokens, width), F32), dma(6)],
    )
    small = Small(jnp.concatenate([dvec1[0:2], dvec2[0:2]], axis=0))
    grad_images = jnp.transpose(grad_x, (1, 0, 2))
    advance([m2, m1, m0], dvec1)
    advance([jj, m2, m1, small])
    advance([jj, m2, m1, m0, small])
    items = [jj, m2, m1, m0, small]
    while any(not item.done for item in items):
        advance(items)
    mine = lax.dynamic_slice_in_dim(small.total, me * (width // n_fs), width // n_fs, 1)

    grad_up, grad_down, grad_out = call(
        mlp_end_kernel,
        [shape(width // n_fs, ff, dtype=F32), shape(fourth, width, dtype=F32), shape(width // n_fs, width, dtype=F32)],
        [*m0.parts, *m1.parts, *m2.parts],
        scratch=[pltpu.VMEM((width, third), F32)],
        us=3,
    )
    (grad_joint,) = call(rows_end_kernel, [shape(width // n_fs, 3 * width, dtype=F32)], jj.parts)
    return (
        output,
        grad_images,
        mine[0],
        mine[1],
        grad_joint,
        grad_out,
        mine[2],
        mine[3],
        grad_up,
        grad_down,
    )


def solution(mesh):
    rows = P("fsdp", None)
    tokens = P(("dp", "fsdp"), None, None)
    one = P("fsdp")
    return jax.shard_map(
        on_device,
        mesh=mesh,
        in_specs=(tokens, one, one, rows, rows, one, one, rows, rows, P(("dp", "fsdp"), None), tokens),
        out_specs=(tokens, tokens, one, one, rows, rows, one, one, rows, rows),
        check_vma=False,
    )
```
